32 devices in a mesh: grp: 2 (over y), col: 8 (over z, x), row: 2 (over core).
Axes of the slice: x: 2, y: 2, z: 4, core: 2. Of those that a mesh axis runs over, the one named last changes fastest.
Arguments:
- left_bounds: bfloat16 [4, 8, 128, 8, 128], P(('grp', 'row'), 'col'), parts along dimension 0, may hold values from -0.1875 to 0.1875
- right_bounds: bfloat16 [4, 8, 128, 8, 128], P(('grp', 'row'), 'col'), parts along dimension 0, may hold values from -0.1875 to 0.1875
- site_tensors: bfloat16 [4, 8, 2, 4096], P(('grp', 'row'), 'col'), parts along dimension 0, may hold values from -2 to 2
- configuration: int32 [4, 8], P(('grp', 'row'), 'col'), parts along dimension 0, may hold values from 0 to 1
- top_env: bfloat16 [16, 128, 8, 128], P(('grp', 'col')), parts along dimension 0, may hold values from -6 to 6
- bottom_env: bfloat16 [16, 128, 8, 128], P(('grp', 'col')), parts along dimension 0, may hold values from -6 to 6
- sketch: bfloat16 [1024, 128], replicated, may hold values from -0.1875 to 0.1875
Outputs:
- gradient: float32 [4, 8, 2, 4096], P(('grp', 'row'), 'col'), parts along dimension 0
- left_updated: bfloat16 [4, 8, 128, 8, 128], P(('grp', 'row'), 'col'), parts along dimension 0
- right_updated: bfloat16 [4, 8, 128, 8, 128], P(('grp', 'row'), 'col'), parts along dimension 0
The draws below stay inside these ranges and needn't reach their ends.
There are 2 independent parts, one for each index of `grp`. The reference program is written for one: setup_inputs(seed, part) draws one part's arguments, and reference() takes and returns one part's arrays. A program takes and returns all parts, laid end to end along the dimension named above; an argument that names none is the same for every part. Nothing has to cross between parts.
All inputs are finite; a program needn't handle non-finite values.
Results may differ from the reference program's by a relative error of at most 0.015.
Values may be sent and summed in bfloat16 or wider, within the bound.
No kernel may reach another device: no remote copies, remote signals or barrier semaphores. Data moves between devices by JAX's collectives and lax.ppermute only.
A program may use at most 64 MiB of HBM per device.

```python
import math
import jax
import jax.numpy as jnp
from jax import lax

D = 8
PHYS = 2
CHI = 128
ROWS = 2
COLS = 8


def environment_field(key, noise, strength):
    row_key, col_key = jax.random.split(key, 2)
    row_part = jax.random.normal(row_key, (COLS, CHI, D, 1), jnp.float32)
    col_part = jax.random.normal(col_key, (COLS, 1, 1, CHI), jnp.float32)
    field = (noise + strength * row_part * col_part) / math.sqrt(1.0 + strength * strength)
    return jnp.clip(field, -6.0, 6.0).astype(jnp.bfloat16)


def environment_draw(key):
    noise_key, shared_key = jax.random.split(key, 2)
    noise = jax.random.normal(noise_key, (COLS, CHI, D, CHI), jnp.float32)
    strength = 1.2
    return environment_field(shared_key, noise, strength)


def draw_top_env(key, part):
    return environment_draw(jax.random.fold_in(key, 101))


def draw_bottom_env(key, part):
    return environment_draw(jax.random.fold_in(key, 202))


def set_ends(result, key, smallest, top_value):
    longest = result.shape.index(max(result.shape))
    spots = []
    for shift in (0, 1):
        where = [jax.random.randint(jax.random.fold_in(key, axis), (), 0, length) for axis, length in enumerate(result.shape)]
        where[longest] = (where[longest] + shift) % result.shape[longest]
        spots.append(tuple(where))
    return result.at[spots[0]].set(smallest).at[spots[1]].set(top_value)


def steps_of(rng, dims, shards, smallest, high):
    factor_of, own = 1.0, jax.random.fold_in(rng, 6)
    for axis_at, shards_of in shards:
        steps = jnp.exp(jax.random.uniform(jax.random.fold_in(own, axis_at), (shards_of,), jnp.float32, smallest / len(shards), high / len(shards)))
        factor_of = factor_of * jnp.repeat(steps, dims[axis_at] // shards_of).reshape([-1 if axis == axis_at else 1 for axis in range(len(dims))])
    return factor_of


def bell_draw(rng, extent, spread, limit, cuts=(), kind=jnp.bfloat16):
    drawn = spread * jax.random.normal(rng, extent, jnp.float32)
    if cuts:
        drawn = drawn * steps_of(rng, extent, cuts, -0.22, 0.18)
    return jnp.clip(drawn, -limit, limit).astype(kind)


def setup_inputs(seed: int = 0, part: int = 0) -> dict:
    key_of = jax.random.split(jax.random.key(seed), 8)
    part_keys = jax.random.split(jax.random.fold_in(key_of[7], part), 8)
    left_bounds = bell_draw(part_keys[0], (ROWS, COLS, CHI, D, CHI), (CHI * D) ** -0.5, 0.1875, ((0, 2), (1, 8)))
    right_bounds = bell_draw(part_keys[1], (ROWS, COLS, CHI, D, CHI), (CHI * D) ** -0.5, 0.1875, ((0, 2), (1, 8)))
    site_tensors = bell_draw(part_keys[2], (ROWS, COLS, PHYS, D**4), D ** -0.5, 2.0, ((0, 2), (1, 8)))
    configuration = set_ends(jax.random.randint(part_keys[3], (ROWS, COLS), 0, PHYS), jax.random.fold_in(part_keys[3], 1), 0, PHYS - 1).astype(jnp.int32)
    top_env = draw_top_env(jax.random.fold_in(jax.random.fold_in(key_of[7], part), 71), part)
    bottom_env = draw_bottom_env(jax.random.fold_in(jax.random.fold_in(key_of[7], part), 71), part)
    sketch = bell_draw(key_of[6], (CHI * D, CHI), (CHI * D) ** -0.5, 0.1875)
    return {"left_bounds": left_bounds, "right_bounds": right_bounds, "site_tensors": site_tensors, "configuration": configuration, "top_env": top_env, "bottom_env": bottom_env, "sketch": sketch}


def widen(array):
    return lax.optimization_barrier(array).astype(jnp.float32)

def orthonormal_basis(matrix):
    gram_matrix = jnp.dot(matrix.T.astype(jnp.float32), matrix.astype(jnp.float32), precision=lax.Precision.HIGHEST, preferred_element_type=jnp.float32)
    cholesky_factor = jnp.linalg.cholesky(gram_matrix)
    solved = lax.linalg.triangular_solve(cholesky_factor, matrix, left_side=False, lower=True, transpose_a=True)
    return solved.astype(jnp.bfloat16)

def project_row(frame_basis, boundary_row, oriented, sketch, closing):
    chi_size = boundary_row.shape[0]
    bond_size = boundary_row.shape[1]
    frame_tensor = widen(frame_basis).reshape(chi_size, bond_size, chi_size)
    partial_value = jnp.einsum('aup,akb->upkb', frame_tensor, widen(boundary_row)).astype(jnp.bfloat16)
    absorbed = jnp.einsum('upkb,kuod->pobd', widen(partial_value), widen(oriented)).astype(jnp.bfloat16)
    unfolded = widen(absorbed).reshape(chi_size * bond_size, chi_size * bond_size)
    if closing is None:
        closing = orthonormal_basis(jnp.dot(unfolded.T, widen(sketch)))
    unscaled = jnp.dot(unfolded, widen(closing))
    scaled = unscaled * lax.rsqrt(jnp.mean(unscaled * unscaled) + 1e-06)
    return (scaled.reshape(chi_size, bond_size, chi_size).astype(jnp.bfloat16), closing)

def pass_down(carried, western_row, core_row, eastern_row):
    partial_value = jnp.einsum('mun,mlb->unlb', widen(carried.astype(jnp.bfloat16)), widen(western_row)).astype(jnp.bfloat16)
    middle = jnp.einsum('unlb,luxd->nbxd', widen(partial_value), widen(core_row)).astype(jnp.bfloat16)
    return (partial_value, jnp.einsum('nbxd,nxc->bdc', widen(middle), widen(eastern_row)))

def pass_up(carried, western_row, core_row, eastern_row):
    lower_part = jnp.einsum('bdc,nxc->bdnx', widen(carried.astype(jnp.bfloat16)), widen(eastern_row)).astype(jnp.bfloat16)
    lower_mid = jnp.einsum('bdnx,luxd->bnlu', widen(lower_part), widen(core_row)).astype(jnp.bfloat16)
    return (lower_part, jnp.einsum('bnlu,mlb->mun', widen(lower_mid), widen(western_row)))

def reference(left_bounds, right_bounds, site_tensors, configuration, top_env, bottom_env, sketch):
    western_all = jnp.roll(left_bounds, 1, axis=1)
    eastern_all = jnp.roll(right_bounds, -1, axis=1)
    selection = jnp.arange(PHYS, dtype=jnp.int32)[None, None, :, None] == configuration[:, :, None, None]
    selected = lax.optimization_barrier(jnp.sum(jnp.where(selection, site_tensors, jnp.zeros_like(site_tensors)), axis=2))

    def column(packed):
        western, eastern, cores_flat, chooser, upper_edge, lower_edge = packed
        site_core = cores_flat.reshape(ROWS, D, D, D, D)
        mirrored = site_core.transpose(0, 3, 2, 1, 4)
        updated = []
        for boundary, oriented, upper, lower in ((western, site_core, upper_edge, lower_edge), (eastern, mirrored, upper_edge.transpose(2, 1, 0), lower_edge.transpose(2, 1, 0))):
            frame_basis = orthonormal_basis(upper.astype(jnp.float32).reshape(CHI * D, CHI))
            closing_edge = orthonormal_basis(lower.astype(jnp.float32).reshape(CHI * D, CHI))
            collected = []
            for position in range(ROWS):
                closing = closing_edge if position == ROWS - 1 else None
                new_row, frame_basis = project_row(frame_basis, boundary[position], oriented[position], sketch, closing)
                collected.append(new_row)
            updated.append(jnp.stack(collected))
        carried = upper_edge.astype(jnp.float32)
        partials = []
        for position in range(ROWS):
            partial_value, carried = pass_down(carried, western[position], site_core[position], eastern[position])
            partials.append(partial_value)
        carried = lower_edge.astype(jnp.float32)
        lowers = [None] * ROWS
        for position in reversed(range(ROWS)):
            lowers[position], carried = pass_up(carried, western[position], site_core[position], eastern[position])
        gradient_rows = jnp.stack([jnp.einsum('unlb,bdnx->luxd', widen(partials[position]), widen(lowers[position])).reshape(-1) for position in range(ROWS)])
        gradient = jnp.where(chooser, gradient_rows.reshape(ROWS, 1, D ** 4) * (D / CHI), 0.0)
        return (gradient, updated[0], updated[1])
    gradient, left_new, right_new = lax.map(column, (western_all.transpose(1, 0, 2, 3, 4), eastern_all.transpose(1, 0, 2, 3, 4), selected.transpose(1, 0, 2), selection.transpose(1, 0, 2, 3), top_env, bottom_env))
    return (gradient.transpose(1, 0, 2, 3), left_new.transpose(1, 0, 2, 3, 4), right_new.transpose(1, 0, 2, 3, 4))
```

```python
import functools

import jax
import jax.numpy as jnp
from jax import lax
from jax.experimental import pallas as pl
from jax.experimental.pallas import tpu as pltpu
from jax.sharding import PartitionSpec as P

F32 = jnp.float32
BF16 = jnp.bfloat16
VMEM_BYTES = 48 * 1024 * 1024


def nn(a, b):
    return jnp.dot(a, b, preferred_element_type=F32)


def nt(a, b):
    return lax.dot_general(a, b, (((1,), (1,)), ((), ())), preferred_element_type=F32)


def split(x):
    high = x.astype(BF16)
    return high, (x - high.astype(F32)).astype(BF16)


def iota(shape, axis):
    return lax.broadcasted_iota(jnp.int32, shape, axis)


def chol_inverse(grams):
    n = grams[0].shape[0]
    blocks = n // 8
    count = len(grams)
    lane = iota((8, n), 1)
    sub = iota((8, n), 0)
    at = [sub == j for j in range(8)]
    after = [sub > j for j in range(8)]
    tiles = [[g[8 * i : 8 * i + 8, :] for i in range(blocks)] for g in grams]

    def over_lanes(x, j):
        return jnp.broadcast_to(x[:, j : j + 1], (8, n))

    def over_rows(x, j):
        return jnp.broadcast_to(x[j : j + 1, :], (8, n))

    for b in range(blocks):
        own = (lane >= 8 * b) & (lane < 8 * b + 8)
        eye = jnp.where(lane - 8 * b == sub, 1.0, 0.0)
        diag = [[over_lanes(tiles[q][b], 8 * b + j) for j in range(8)] for q in range(count)]
        below = [
            [[over_lanes(tiles[q][i], 8 * b + j) for j in range(8)] for i in range(b + 1, blocks)]
            for q in range(count)
        ]
        forward = [jnp.where(own, eye, tiles[q][b]) for q in range(count)]
        full = list(forward)
        pivots = [jnp.ones((8, n), F32) for _ in range(count)]
        for j in range(8):
            for q in range(count):
                c = diag[q]
                pivot = over_rows(c[j], j)
                inverse = 1.0 / pivot
                pivots[q] = jnp.where(at[j], pivot, pivots[q])
                for k in range(j + 1, 8):
                    m = over_rows(c[k], j) * inverse
                    c[k] = jnp.where(at[j], m, c[k] - c[j] * m)
                row = over_rows(forward[q], j) * inverse
                forward[q] = jnp.where(after[j], forward[q] - c[j] * row, forward[q])
                full[q] = jnp.where(at[j], row, full[q] - c[j] * row)
        for q in range(count):
            rows = [over_rows(full[q], j) for j in range(8)]
            for i in range(b + 1, blocks):
                terms = [below[q][i - b - 1][j] * rows[j] for j in range(8)]
                while len(terms) > 1:
                    terms = [x + y for x, y in zip(terms[::2], terms[1::2])]
                tiles[q][i] = jnp.where(own, 0.0, tiles[q][i]) - terms[0]
            tiles[q][b] = jnp.where(lane <= sub + 8 * b, forward[q] * lax.rsqrt(pivots[q]), 0.0)
    return [jnp.concatenate(t, axis=0) for t in tiles]


def leg(scratch, j):
    chi = scratch.shape[1]
    return scratch[pl.ds(j, chi, stride=scratch.shape[0] // chi), :]


def to_kron(lhs, rhs, x_ref, transposed):
    chi = lhs.shape[1]
    bond = lhs.shape[0] // chi
    groups = chi // 8
    for t in range(0, bond, 2):
        if transposed:
            product = nt(lhs[...], rhs[t * chi : (t + 2) * chi, :])
        else:
            product = nn(lhs[...], rhs[:, t * chi : (t + 2) * chi])
        for s in range(bond):
            at = (s * bond + t) * 8
            for g in range(groups):
                rows = product[s * chi + g * 8 : s * chi + g * 8 + 8, :]
                x_ref[at : at + 16, g * chi : (g + 1) * chi] = jnp.concatenate(
                    [rows[:, :chi], rows[:, chi:]], axis=0
                ).astype(BF16)


def absorb(kron, x_ref, m_ref, bond):
    chi = m_ref.shape[0] // bond
    for g in range(0, chi // 8, 2):
        out = nn(kron, x_ref[:, g * chi : (g + 2) * chi])
        for o in range(bond):
            for d in range(bond):
                rows = out[(o * bond + d) * 8 : (o * bond + d) * 8 + 8, :]
                at = o * chi + g * 8
                m_ref[at : at + 16, d * chi : (d + 1) * chi] = jnp.concatenate(
                    [rows[:, :chi], rows[:, chi:]], axis=0
                ).astype(BF16)


def square_core(flat):
    half = flat.shape[1] // 2
    size = flat.shape[0] * 2
    i = iota((size, flat.shape[0]), 0)
    j = iota((size, flat.shape[0]), 1)
    even = jnp.where(i == 2 * j, 1.0, 0.0).astype(BF16)
    odd = jnp.where(i == 2 * j + 1, 1.0, 0.0).astype(BF16)
    return (nn(even, flat[:, :half]) + nn(odd, flat[:, half:])).astype(BF16)


def swap_order(size, bond):
    i = iota((size, size), 0)
    j = iota((size, size), 1)
    hit = (i // bond == j % bond) & (i % bond == j // bond)
    return jnp.where(hit, 1.0, 0.0).astype(BF16)


def spread(size):
    i = iota((size * 8, size), 0)
    j = iota((size * 8, size), 1)
    return jnp.where(i // 8 == j, 1.0, 0.0).astype(BF16)


def kron_of(spread_rows, size):
    wide = nt(spread_rows.astype(BF16), spread(size))
    i = iota(wide.shape, 0)
    j = iota(wide.shape, 1)
    return jnp.where(i % 8 == j % 8, wide, 0.0).astype(BF16)


def kron_ahead(core, bond):
    size = core.shape[0]
    permuted = nn(swap_order(size, bond), core).astype(BF16)
    return kron_of(nt(spread(size), permuted), size)


def kron_back(core, bond):
    size = core.shape[0]
    permuted = nn(core, swap_order(size, bond)).astype(BF16)
    return kron_of(nn(spread(size), permuted), size)


def kron_mirrored(core, bond):
    size = core.shape[0]
    i = iota((size, size), 0)
    j = iota((size, size), 1)
    total = jnp.zeros((size, size), F32)
    for u in range(bond):
        pick = jnp.where(j == (i // bond) * bond + u, 1.0, 0.0).astype(BF16)
        picked = jnp.where(i % bond == j % bond, nn(pick, core), 0.0).astype(BF16)
        place = jnp.where(j == u * bond + i // bond, 1.0, 0.0).astype(BF16)
        total = total + nn(picked, place)
    return kron_of(nn(spread(size), total.astype(BF16)), size)


def edges_kernel(
    top, bottom, sketch, sites, choice, basis, edge, first, sketch_t, core, wide, legs_top, legs_bottom
):
    side = lax.axis_index("row")
    chi = top.shape[1]
    bond = top.shape[0] // chi
    for env, legs, mine in ((top, legs_top, 0), (bottom, legs_bottom, 1)):
        wide[...] = env[...].astype(F32)

        @pl.when(side == 0)
        def _():
            for u in range(bond):
                block = leg(wide, u).T.astype(BF16)
                legs[:, u * chi : (u + 1) * chi] = block
                if mine == 0:
                    first[u * chi : (u + 1) * chi, :] = block

        @pl.when(side == 1)
        def _():
            for u in range(bond):
                block = leg(wide, u).astype(BF16)
                legs[:, u * chi : (u + 1) * chi] = block
                if mine == 1:
                    first[u * chi : (u + 1) * chi, :] = block

    wide[...] = sketch[...].astype(F32)
    for o in range(bond):
        sketch_t[:, o * chi : (o + 1) * chi] = leg(wide, o).T.astype(BF16)
    phys = sites.shape[0]
    chosen = jnp.zeros((1, sites.shape[1]), F32)
    for p in range(phys):
        chosen = chosen + jnp.where(choice[0, 0] == p, sites[p : p + 1, :].astype(F32), 0.0)
    lanes = core.shape[1]
    core[...] = jnp.concatenate(
        [chosen[:, i * lanes : (i + 1) * lanes] for i in range(core.shape[0])], axis=0
    ).astype(BF16)
    inverse_top, inverse_bottom = chol_inverse(
        [nt(legs_top[...], legs_top[...]), nt(legs_bottom[...], legs_bottom[...])]
    )
    high, low = split(inverse_top)
    ortho = (nn(high, legs_top[...]) + nn(low, legs_top[...])).astype(BF16)
    for u in range(bond):
        basis[u * chi : (u + 1) * chi, :] = ortho[:, u * chi : (u + 1) * chi]
    high, low = split(inverse_bottom)
    edge[...] = (nn(high, legs_bottom[...]) + nn(low, legs_bottom[...])).astype(BF16)


def begin_kernel(
    first, western, eastern, core, x_out, back, carried, wide_w, wide_e, ahead, behind, kron, middle
):
    side = lax.axis_index("row")
    chi = first.shape[1]
    bond = first.shape[0] // chi
    wide_w[...] = western[...].astype(F32)
    wide_e[...] = eastern[...].astype(F32)

    @pl.when(side == 0)
    def _():
        for j in range(bond):
            at = slice(j * chi, (j + 1) * chi)
            east = leg(wide_e, j)
            ahead[:, at] = leg(wide_w, j).astype(BF16)
            behind[:, at] = east.T.astype(BF16)
            back[at, :] = east.astype(BF16)
        kron[...] = kron_ahead(square_core(core[...]), bond)

    @pl.when(side == 1)
    def _():
        for j in range(bond):
            at = slice(j * chi, (j + 1) * chi)
            west = leg(wide_w, j)
            ahead[:, at] = leg(wide_e, j).T.astype(BF16)
            behind[:, at] = west.astype(BF16)
            back[at, :] = west.T.astype(BF16)
        kron[...] = kron_back(square_core(core[...]), bond)

    to_kron(first, ahead, x_out, False)
    absorb(kron[...], x_out, middle, bond)
    state = nn(behind[...], middle[...]).astype(BF16)
    for s in range(bond):
        carried[s * chi : (s + 1) * chi, :] = state[:, s * chi : (s + 1) * chi]


def rows_kernel(
    basis,
    edge,
    sketch_t,
    western,
    eastern,
    swapped,
    core_own,
    core_other,
    keep,
    send,
    wide_0,
    wide_1,
    lanes,
    kron,
    x,
    absorbed,
    next_basis,
):
    side = lax.axis_index("row")
    chi = basis.shape[1]
    bond = basis.shape[0] // chi

    @pl.when(side == 0)
    def _():
        wide_0[...] = western[...].astype(F32)
        wide_1[...] = swapped[...].astype(F32)
        kron[0] = kron_ahead(square_core(core_own[...]), bond)
        kron[1] = kron_ahead(square_core(core_other[...]), bond)

    @pl.when(side == 1)
    def _():
        wide_0[...] = swapped[...].astype(F32)
        wide_1[...] = eastern[...].astype(F32)
        kron[0] = kron_mirrored(square_core(core_other[...]), bond)
        kron[1] = kron_mirrored(square_core(core_own[...]), bond)

    def project(frame, wide, row):
        for k in range(bond):
            lanes[:, k * chi : (k + 1) * chi] = leg(wide, k).astype(BF16)
        to_kron(frame, lanes, x, False)
        absorb(kron[row], x, absorbed, bond)

    def finish(closing, wide, row):
        unscaled = nt(absorbed[...], closing)
        mean = jnp.sum(unscaled * unscaled) * (1.0 / (unscaled.shape[0] * unscaled.shape[1]))
        scaled = unscaled * lax.rsqrt(mean + 1e-06)
        for o in range(bond):
            wide[pl.ds(o, chi, stride=bond), :] = scaled[o * chi : (o + 1) * chi, :]
        new = wide[...].astype(BF16)

        @pl.when(side == row)
        def _():
            keep[...] = new

        @pl.when(side != row)
        def _():
            send[...] = new

    project(basis, wide_0, 0)
    sketched = nn(sketch_t[...], absorbed[...])
    high, low = split(sketched)
    gram = nt(high, high) + (nt(high, low) + nt(low, high))
    (inverse,) = chol_inverse([gram])
    inverse_high, inverse_low = split(inverse)
    closing = (
        nn(inverse_high, high) + (nn(inverse_high, low) + nn(inverse_low, high))
    ).astype(BF16)
    for d in range(bond):
        next_basis[d * chi : (d + 1) * chi, :] = closing[:, d * chi : (d + 1) * chi]
    finish(closing, wide_0, 0)
    project(next_basis, wide_1, 1)
    finish(edge[...], wide_1, 1)


def gradient_kernel(x_first, back, carried, choice, gradient, x_second):
    side = lax.axis_index("row")
    chi = back.shape[1]
    bond = back.shape[0] // chi
    size = bond * bond
    to_kron(back, carried, x_second, True)
    product = nt(x_first[...], x_second[...])
    i = iota(product.shape, 0)
    j = iota(product.shape, 1)
    product = jnp.where(i % 8 == j % 8, product, 0.0)
    gather = spread(size)
    high, low = split(product)
    half = nn(high, gather) + nn(low, gather)
    i = iota((size, size * 8), 0)
    j = iota((size, size * 8), 1) // 8
    ordered = jnp.where((i // bond == j % bond) & (i % bond == j // bond), 1.0, 0.0).astype(BF16)
    high, low = split(half)
    env = nn(ordered, high) + nn(ordered, low)
    env = jnp.where(side == 0, env, env.T) * (bond / chi)
    for p in range(gradient.shape[0]):
        kept = jnp.where(choice[0, 0] == p, env, 0.0)
        for r in range(size):
            gradient[p : p + 1, r * size : (r + 1) * size] = kept[r : r + 1, :]


def call(kernel, out_shapes, scratch, inputs, flops):
    vmem = pl.BlockSpec(memory_space=pltpu.VMEM)
    smem = pl.BlockSpec(memory_space=pltpu.SMEM)
    return pl.pallas_call(
        kernel,
        out_shape=[jax.ShapeDtypeStruct(s, t) for s, t in out_shapes],
        in_specs=[smem if x.dtype == jnp.int32 else vmem for x in inputs],
        out_specs=[vmem for _ in out_shapes],
        scratch_shapes=[pltpu.VMEM(s, t) for s, t in scratch],
        compiler_params=pltpu.CompilerParams(vmem_limit_bytes=VMEM_BYTES),
        cost_estimate=pl.CostEstimate(flops=flops, bytes_accessed=2**21, transcendentals=0),
    )(*inputs)


def shifted(block, axis, steps):
    count = lax.axis_size(axis)
    return lax.ppermute(block, axis, [(i, (i + steps) % count) for i in range(count)])


def exchanged(block, axis):
    return lax.ppermute(block, axis, [(0, 1), (1, 0)])


def local(left_bounds, right_bounds, site_tensors, configuration, top_env, bottom_env, sketch):
    chi = left_bounds.shape[2]
    bond = left_bounds.shape[3]
    rows = chi * bond
    size = bond * bond
    tall = (rows, chi)
    flat = (chi, rows)
    kron = (size * 8, size * 8)
    stack = (size * 8, chi // 8 * chi)
    square = (rows, rows)
    western = shifted(left_bounds, "col", 1).reshape(tall)
    eastern = shifted(right_bounds, "col", -1).reshape(tall)
    is_upper = lax.axis_index("row") == 0
    basis, edge, first, sketch_t, core = call(
        edges_kernel,
        [(tall, BF16), (flat, BF16), (tall, BF16), (flat, BF16), ((size // 2, size * 2), BF16)],
        [(tall, F32), (flat, BF16), (flat, BF16)],
        [
            top_env.reshape(tall),
            bottom_env.reshape(tall),
            sketch,
            site_tensors.reshape(site_tensors.shape[2:]),
            configuration,
        ],
        2**31,
    )
    swapped = exchanged(jnp.where(is_upper, eastern, western), "row")
    core_other = exchanged(core, "row")
    x_first, back, carried = call(
        begin_kernel,
        [(stack, BF16), (tall, BF16), (tall, BF16)],
        [(tall, F32), (tall, F32), (flat, BF16), (flat, BF16), (kron, BF16), (square, BF16)],
        [first, western, eastern, core],
        2**31,
    )
    carried = exchanged(carried, "row")
    keep, send = call(
        rows_kernel,
        [(tall, BF16), (tall, BF16)],
        [
            (tall, F32),
            (tall, F32),
            (flat, BF16),
            ((2,) + kron, BF16),
            (stack, BF16),
            (square, BF16),
            (tall, BF16),
        ],
        [basis, edge, sketch_t, western, eastern, swapped, core, core_other],
        2**33,
    )
    received = exchanged(send, "row")
    (gradient,) = call(
        gradient_kernel,
        [(site_tensors.shape[2:], F32)],
        [(stack, BF16)],
        [x_first, back, carried, configuration],
        2**31,
    )
    left_new = jnp.where(is_upper, keep, received)
    right_new = jnp.where(is_upper, received, keep)
    return (
        gradient.reshape(site_tensors.shape),
        left_new.reshape(left_bounds.shape),
        right_new.reshape(right_bounds.shape),
    )


def solution(mesh):
    return jax.shard_map(
        local,
        mesh=mesh,
        in_specs=(
            P(("grp", "row"), "col", None, None, None),
            P(("grp", "row"), "col", None, None, None),
            P(("grp", "row"), "col", None, None),
            P(("grp", "row"), "col"),
            P(("grp", "col"), None, None, None),
            P(("grp", "col"), None, None, None),
            P(),
        ),
        out_specs=(
            P(("grp", "row"), "col", None, None),
            P(("grp", "row"), "col", None, None, None),
            P(("grp", "row"), "col", None, None, None),
        ),
        check_vma=False,
    )
```

```python
import functools

import jax
import jax.numpy as jnp
from jax import lax
from jax.experimental import pallas as pl
from jax.experimental.pallas import tpu as pltpu
from jax.sharding import PartitionSpec as P

F32 = jnp.float32
BF16 = jnp.bfloat16
VMEM_BYTES = 24 * 1024 * 1024


def nn(a, b):
    return jnp.dot(a, b, preferred_element_type=F32)


def nt(a, b):
    return lax.dot_general(a, b, (((1,), (1,)), ((), ())), preferred_element_type=F32)


def split(x):
    high = x.astype(BF16)
    return high, (x - high.astype(F32)).astype(BF16)


def iota(shape, axis):
    return lax.broadcasted_iota(jnp.int32, shape, axis)


def chol_inverse(grams, near, beside=()):
    beside = list(beside)
    n = grams[0].shape[0]
    blocks = n // 8
    count = len(grams)
    lane = iota((8, n), 1)
    sub = iota((8, n), 0)
    at = [sub == j for j in range(8)]
    after = [sub > j for j in range(8)]
    tiles = [[g[8 * i : 8 * i + 8, :] for i in range(blocks)] for g in grams]

    def over_lanes(x, j):
        return jnp.broadcast_to(x[:, j : j + 1], (8, n))

    def over_rows(x, j):
        return jnp.broadcast_to(x[j : j + 1, :], (8, n))

    for b in range(blocks):
        own = (lane >= 8 * b) & (lane < 8 * b + 8)
        eye = jnp.where(lane - 8 * b == sub, 1.0, 0.0)
        by_element = range(b + 1, min(blocks, b + 1 + near))
        by_matmul = range(by_element.stop, blocks)
        diag = [[over_lanes(tiles[q][b], 8 * b + j) for j in range(8)] for q in range(count)]
        below = [
            [[over_lanes(tiles[q][i], 8 * b + j) for j in range(8)] for i in by_element]
            for q in range(count)
        ]
        forward = [jnp.where(own, eye, tiles[q][b]) for q in range(count)]
        full = list(forward)
        pivots = [jnp.ones((8, n), F32) for _ in range(count)]
        for step in beside[b * len(beside) // blocks : (b + 1) * len(beside) // blocks]:
            step()
        for j in range(8):
            for q in range(count):
                c = diag[q]
                pivot = over_rows(c[j], j)
                inverse = 1.0 / pivot
                pivots[q] = jnp.where(at[j], pivot, pivots[q])
                for k in range(j + 1, 8):
                    m = over_rows(c[k], j) * inverse
                    c[k] = jnp.where(at[j], m, c[k] - c[j] * m)
                row = over_rows(forward[q], j) * inverse
                forward[q] = jnp.where(after[j], forward[q] - c[j] * row, forward[q])
                full[q] = jnp.where(at[j], row, full[q] - c[j] * row)
        for q in range(count):
            rows = [over_rows(full[q], j) for j in range(8)]
            for i in by_element:
                terms = [below[q][i - b - 1][j] * rows[j] for j in range(8)]
                while len(terms) > 1:
                    terms = [x + y for x, y in zip(terms[::2], terms[1::2])]
                tiles[q][i] = jnp.where(own, 0.0, tiles[q][i]) - terms[0]
            if by_matmul:
                rest = jnp.concatenate([tiles[q][i] for i in by_matmul], axis=0)
                padded = [full[q], jnp.zeros((n - 8 * b - 8, n), F32)]
                if b:
                    padded = [jnp.zeros((8 * b, n), F32)] + padded
                update = jnp.dot(
                    rest,
                    jnp.concatenate(padded, axis=0),
                    precision=lax.Precision.HIGHEST,
                    preferred_element_type=F32,
                )
                for x, i in enumerate(by_matmul):
                    tiles[q][i] = jnp.where(own, 0.0, tiles[q][i]) - update[8 * x : 8 * x + 8]
            tiles[q][b] = jnp.where(lane <= sub + 8 * b, forward[q] * lax.rsqrt(pivots[q]), 0.0)
    return [jnp.concatenate(t, axis=0) for t in tiles]


def leg(scratch, j):
    chi = scratch.shape[1]
    return scratch[pl.ds(j, chi, stride=scratch.shape[0] // chi), :]


def kron_step(lhs, rhs, x_ref, t, transposed=False):
    chi = lhs.shape[1]
    bond = lhs.shape[0] // chi
    if transposed:
        product = nt(lhs[...], rhs[t * chi : (t + 2) * chi, :])
    else:
        product = nn(lhs[...], rhs[:, t * chi : (t + 2) * chi])
    for s in range(bond):
        at = (s * bond + t) * 8
        for g in range(chi // 8):
            rows = product[s * chi + g * 8 : s * chi + g * 8 + 8, :]
            x_ref[at : at + 16, g * chi : (g + 1) * chi] = jnp.concatenate(
                [rows[:, :chi], rows[:, chi:]], axis=0
            ).astype(BF16)


def absorb_step(kron, x_ref, m_ref, g, chi):
    bond = m_ref.shape[0] // chi
    out = nn(kron[...], x_ref[:, g * chi : (g + 2) * chi])
    for o in range(bond):
        for d in range(bond):
            rows = out[(o * bond + d) * 8 : (o * bond + d) * 8 + 8, :]
            at = o * chi + g * 8
            m_ref[at : at + 16, d * chi : (d + 1) * chi] = jnp.concatenate(
                [rows[:, :chi], rows[:, chi:]], axis=0
            ).astype(BF16)


def kron_steps(lhs, rhs, x_ref, transposed=False):
    bond = lhs.shape[0] // lhs.shape[1]
    return [
        functools.partial(kron_step, lhs, rhs, x_ref, t, transposed) for t in range(0, bond, 2)
    ]


def absorb_steps(kron, x_ref, m_ref, chi):
    return [
        functools.partial(absorb_step, kron, x_ref, m_ref, g, chi) for g in range(0, chi // 8, 2)
    ]


def square_core(flat):
    half = flat.shape[1] // 2
    size = flat.shape[0] * 2
    i = iota((size, flat.shape[0]), 0)
    j = iota((size, flat.shape[0]), 1)
    even = jnp.where(i == 2 * j, 1.0, 0.0).astype(BF16)
    odd = jnp.where(i == 2 * j + 1, 1.0, 0.0).astype(BF16)
    return (nn(even, flat[:, :half]) + nn(odd, flat[:, half:])).astype(BF16)


def swap_order(size, bond):
    i = iota((size, size), 0)
    j = iota((size, size), 1)
    hit = (i // bond == j % bond) & (i % bond == j // bond)
    return jnp.where(hit, 1.0, 0.0).astype(BF16)


def spread(size):
    i = iota((size * 8, size), 0)
    j = iota((size * 8, size), 1)
    return jnp.where(i // 8 == j, 1.0, 0.0).astype(BF16)


def kron_of(spread_rows, size):
    wide = nt(spread_rows.astype(BF16), spread(size))
    i = iota(wide.shape, 0)
    j = iota(wide.shape, 1)
    return jnp.where(i % 8 == j % 8, wide, 0.0).astype(BF16)


def spread_ahead(core, bond):
    size = core.shape[0]
    return nt(spread(size), nn(swap_order(size, bond), core).astype(BF16))


def spread_turned(core, bond):
    size = core.shape[0]
    return nn(spread(size), nt(swap_order(size, bond), core).astype(BF16))


def spread_back(core, bond):
    size = core.shape[0]
    return nn(spread(size), nn(core, swap_order(size, bond)).astype(BF16))


def mirrored(core, bond):
    size = core.shape[0]
    i = iota((size, size), 0)
    j = iota((size, size), 1)
    total = jnp.zeros((size, size), F32)
    for u in range(bond):
        pick = jnp.where(j == (i // bond) * bond + u, 1.0, 0.0).astype(BF16)
        picked = jnp.where(i % bond == j % bond, nn(pick, core), 0.0).astype(BF16)
        place = jnp.where(j == u * bond + i // bond, 1.0, 0.0).astype(BF16)
        total = total + nn(picked, place)
    return total.astype(BF16)


def begin_kernel(left, right, sites, choice, first, second, core, chosen, sems):
    side = lax.axis_index("row")

    def start(one, other):
        pltpu.make_async_copy(one, first, sems.at[0]).start()
        pltpu.make_async_copy(other, second, sems.at[1]).start()

    pl.when(side == 0)(functools.partial(start, left, right))
    pl.when(side == 1)(functools.partial(start, right, left))
    copy = pltpu.make_async_copy(sites, chosen, sems.at[2])
    copy.start()
    copy.wait()
    total = jnp.zeros((1, chosen.shape[1]), F32)
    for p in range(chosen.shape[0]):
        total = total + jnp.where(choice[0, 0] == p, chosen[p : p + 1, :].astype(F32), 0.0)
    flat = [total[:, i : i + core.shape[1]] for i in range(0, total.shape[1], core.shape[1])]
    core[...] = jnp.concatenate(flat, axis=0).astype(BF16)
    pltpu.make_async_copy(left, first, sems.at[0]).wait()
    pltpu.make_async_copy(right, second, sems.at[1]).wait()


def edges_kernel(
    top_hbm,
    bottom_hbm,
    sketch_hbm,
    basis,
    basis_lanes,
    edge,
    first,
    sketch_t,
    top,
    bottom,
    sketch,
    wide,
    wide_sketch,
    legs_top,
    legs_bottom,
    sems,
):
    side = lax.axis_index("row")
    chi = top.shape[1]
    bond = top.shape[0] // chi
    copies = [
        pltpu.make_async_copy(source, target, sems.at[i])
        for i, (source, target) in enumerate(
            ((top_hbm, top), (bottom_hbm, bottom), (sketch_hbm, sketch))
        )
    ]
    for copy in copies:
        copy.start()
    for env, legs, mine in ((top, legs_top, 0), (bottom, legs_bottom, 1)):
        copies[mine].wait()
        wide[...] = env[...].astype(F32)

        @pl.when(side == 0)
        def _():
            for u in range(bond):
                block = leg(wide, u).T.astype(BF16)
                legs[:, u * chi : (u + 1) * chi] = block
                if mine == 0:
                    first[u * chi : (u + 1) * chi, :] = block

        @pl.when(side == 1)
        def _():
            for u in range(bond):
                block = leg(wide, u).astype(BF16)
                legs[:, u * chi : (u + 1) * chi] = block
                if mine == 1:
                    first[u * chi : (u + 1) * chi, :] = block

    copies[2].wait()
    wide_sketch[...] = sketch[...].astype(F32)

    def turn_sketch(o):
        sketch_t[o * chi : (o + 1) * chi, :] = leg(wide_sketch, o).T.astype(BF16)

    inverse_top, inverse_bottom = chol_inverse(
        [nt(legs_top[...], legs_top[...]), nt(legs_bottom[...], legs_bottom[...])],
        1,
        [functools.partial(turn_sketch, o) for o in range(bond)],
    )
    high, low = split(inverse_top)
    ortho = (nn(high, legs_top[...]) + nn(low, legs_top[...])).astype(BF16)
    basis_lanes[...] = ortho
    for u in range(bond):
        basis[u * chi : (u + 1) * chi, :] = ortho[:, u * chi : (u + 1) * chi]
    high, low = split(inverse_bottom)
    edge[...] = (nn(high, legs_bottom[...]) + nn(low, legs_bottom[...])).astype(BF16)


def finish(absorbed, closing, wide):
    chi = closing.shape[0]
    bond = absorbed.shape[0] // chi
    unscaled = nt(absorbed[...], closing)
    mean = jnp.sum(unscaled * unscaled) * (1.0 / (unscaled.shape[0] * unscaled.shape[1]))
    scaled = unscaled * lax.rsqrt(mean + 1e-06)
    for o in range(bond):
        wide[pl.ds(o, chi, stride=bond), :] = scaled[o * chi : (o + 1) * chi, :]
    return wide[...].astype(BF16)


def prepare_kernel(
    basis_lanes, sketch_t, site, site_other, kron_0, kron_1, kron_first, sketched, x, kron_sketch
):
    side = lax.axis_index("row")
    chi = basis_lanes.shape[0]
    bond = basis_lanes.shape[1] // chi
    size = bond * bond
    is_left = side == 0
    core = square_core(site[...])
    other = square_core(site_other[...])
    mirrored_own = mirrored(core, bond)
    mirrored_other = mirrored(other, bond)
    swap = swap_order(size, bond)
    wide = spread(size)
    ahead = spread_ahead(core, bond)
    kron_0[...] = kron_of(jnp.where(is_left, ahead, nn(wide, mirrored_other)), size)
    kron_1[...] = kron_of(
        jnp.where(is_left, spread_ahead(other, bond), nn(wide, mirrored_own)), size
    )
    kron_first[...] = kron_of(jnp.where(is_left, ahead, spread_back(core, bond)), size)
    turned = nn(nn(swap, mirrored_own).astype(BF16), swap).astype(BF16)
    kron_sketch[...] = kron_of(
        jnp.where(is_left, nn(wide, turned), spread_turned(other, bond)), size
    )
    for step in kron_steps(sketch_t, basis_lanes, x) + absorb_steps(kron_sketch, x, sketched, chi):
        step()


def upper_kernel(
    basis,
    sketched,
    first,
    arrived_x,
    arrived_y,
    kron_0,
    kron_first,
    next_basis,
    new,
    x_first,
    middle,
    lanes_1,
    wide_x,
    wide_y,
    rows_0,
    lanes_0,
    ahead,
    x,
    absorbed,
):
    is_left = lax.axis_index("row") == 0
    chi = basis.shape[1]
    bond = basis.shape[0] // chi
    blocks = [slice(j * chi, (j + 1) * chi) for j in range(bond)]
    wide_x[...] = arrived_x[...].astype(F32)
    wide_y[...] = arrived_y[...].astype(F32)
    for j in range(bond):
        block = jnp.where(is_left, leg(wide_x, j), leg(wide_y, j)).astype(BF16)
        rows_0[blocks[j], :] = block
        lanes_0[:, blocks[j]] = block
    stacked = nn(sketched[...], rows_0[...])
    range_t = jnp.concatenate([stacked[blocks[d], :] for d in range(bond)], axis=1)
    high, low = split(range_t)
    gram = nt(high, high) + (nt(high, low) + nt(low, high))

    def ready_ahead(j):
        block = leg(wide_x, j)
        ahead[:, blocks[j]] = jnp.where(is_left, block, block.T).astype(BF16)

    def ready_next(j):
        lanes_1[:, blocks[j]] = jnp.where(is_left, leg(wide_y, j), leg(wide_x, j)).astype(BF16)

    beside = (
        kron_steps(basis, lanes_0, x)
        + absorb_steps(kron_0, x, absorbed, chi)
        + [functools.partial(ready_ahead, j) for j in range(bond)]
        + kron_steps(first, ahead, x_first)
        + absorb_steps(kron_first, x_first, middle, chi)
        + [functools.partial(ready_next, j) for j in range(bond)]
    )
    (inverse,) = chol_inverse([gram], 2, beside)
    inverse_high, inverse_low = split(inverse)
    closing = (
        nn(inverse_high, high) + (nn(inverse_high, low) + nn(inverse_low, high))
    ).astype(BF16)
    for d in range(bond):
        next_basis[blocks[d], :] = closing[:, blocks[d]]
    new[...] = finish(absorbed, closing, wide_x)


def state_kernel(middle, received, carried, back, wide, behind):
    side = lax.axis_index("row")
    chi = received.shape[1]
    bond = received.shape[0] // chi
    wide[...] = received[...].astype(F32)

    @pl.when(side == 0)
    def _():
        for j in range(bond):
            at = slice(j * chi, (j + 1) * chi)
            block = leg(wide, j)
            behind[:, at] = block.T.astype(BF16)
            back[at, :] = block.astype(BF16)

    @pl.when(side == 1)
    def _():
        for j in range(bond):
            at = slice(j * chi, (j + 1) * chi)
            block = leg(wide, j)
            behind[:, at] = block.astype(BF16)
            back[at, :] = block.T.astype(BF16)

    state = nn(behind[...], middle[...]).astype(BF16)
    for s in range(bond):
        carried[s * chi : (s + 1) * chi, :] = state[:, s * chi : (s + 1) * chi]


def lower_kernel(basis, edge, lanes, kron, new_0, keep, send, wide, x, absorbed):
    side = lax.axis_index("row")
    chi = basis.shape[1]
    for step in kron_steps(basis, lanes, x) + absorb_steps(kron, x, absorbed, chi):
        step()
    new = finish(absorbed, edge[...], wide)

    @pl.when(side == 0)
    def _():
        keep[...] = new_0[...]
        send[...] = new

    @pl.when(side == 1)
    def _():
        keep[...] = new
        send[...] = new_0[...]


def gradient_kernel(x_first, back, carried, choice, gradient, x_second):
    side = lax.axis_index("row")
    chi = back.shape[1]
    bond = back.shape[0] // chi
    size = bond * bond
    for step in kron_steps(back, carried, x_second, True):
        step()
    product = nt(x_first[...], x_second[...])
    i = iota(product.shape, 0)
    j = iota(product.shape, 1)
    product = jnp.where(i % 8 == j % 8, product, 0.0)
    gather = spread(size)
    high, low = split(product)
    half = nn(high, gather) + nn(low, gather)
    i = iota((size, size * 8), 0)
    j = iota((size, size * 8), 1) // 8
    ordered = jnp.where((i // bond == j % bond) & (i % bond == j // bond), 1.0, 0.0).astype(BF16)
    high, low = split(half)
    env = nn(ordered, high) + nn(ordered, low)
    env = jnp.where(side == 0, env, env.T) * (bond / chi)
    for p in range(gradient.shape[0]):
        kept = jnp.where(choice[0, 0] == p, env, 0.0)
        for r in range(size):
            gradient[p : p + 1, r * size : (r + 1) * size] = kept[r : r + 1, :]


def call(kernel, out_shapes, scratch, inputs, flops, in_place=(), copies=0):
    inputs = [
        pltpu.with_memory_space_constraint(x, pltpu.HBM) if i in in_place else x
        for i, x in enumerate(inputs)
    ]
    vmem = pl.BlockSpec(memory_space=pltpu.VMEM)
    smem = pl.BlockSpec(memory_space=pltpu.SMEM)
    return pl.pallas_call(
        kernel,
        out_shape=[jax.ShapeDtypeStruct(s, t) for s, t in out_shapes],
        in_specs=[
            smem
            if x.dtype == jnp.int32
            else pl.BlockSpec(memory_space=pltpu.HBM)
            if i in in_place
            else vmem
            for i, x in enumerate(inputs)
        ],
        out_specs=[vmem for _ in out_shapes],
        scratch_shapes=[pltpu.VMEM(s, t) for s, t in scratch]
        + ([pltpu.SemaphoreType.DMA((copies,))] if copies else []),
        compiler_params=pltpu.CompilerParams(vmem_limit_bytes=VMEM_BYTES),
        cost_estimate=pl.CostEstimate(flops=flops, bytes_accessed=2**21, transcendentals=0),
    )(*inputs)


def moved(block, pairs):
    return lax.ppermute(block, ("col", "row"), pairs)


def exchanged(block, axis):
    return lax.ppermute(block, axis, [(0, 1), (1, 0)])


def local(left_bounds, right_bounds, site_tensors, configuration, top_env, bottom_env, sketch):
    chi = left_bounds.shape[2]
    bond = left_bounds.shape[3]
    rows = chi * bond
    size = bond * bond
    tall = (rows, chi)
    flat = (chi, rows)
    kron = (size * 8, size * 8)
    stack = (size * 8, chi // 8 * chi)
    square = (rows, rows)
    count = lax.axis_size("col")
    sites = site_tensors.reshape(site_tensors.shape[2:])
    is_upper = lax.axis_index("row") == 0
    first_sent, second_sent, site = call(
        begin_kernel,
        [(tall, BF16), (tall, BF16), ((size // 2, size * 2), BF16)],
        [(sites.shape, BF16)],
        [left_bounds.reshape(tall), right_bounds.reshape(tall), sites, configuration],
        2**20,
        in_place=(0, 1, 2),
        copies=3,
    )
    ahead, behind = (
        [2 * ((c + step) % count) for c in range(count)] for step in (1, -1)
    )
    arrived_x = moved(
        first_sent,
        [(2 * c, ahead[c]) for c in range(count)]
        + [(2 * c + 1, behind[c] + 1) for c in range(count)],
    )
    arrived_y = moved(
        second_sent,
        [(2 * c, behind[c] + 1) for c in range(count)]
        + [(2 * c + 1, ahead[c]) for c in range(count)],
    )
    site_other = exchanged(site, "row")
    basis, basis_lanes, edge, first, sketch_t = call(
        edges_kernel,
        [(tall, BF16), (flat, BF16), (flat, BF16), (tall, BF16), (tall, BF16)],
        [(tall, BF16)] * 3 + [(tall, F32), (tall, F32), (flat, BF16), (flat, BF16)],
        [top_env.reshape(tall), bottom_env.reshape(tall), sketch],
        2**31,
        in_place=(0, 1, 2),
        copies=3,
    )
    site_other, basis_lanes = lax.optimization_barrier((site_other, basis_lanes))
    kron_0, kron_1, kron_first, sketched = call(
        prepare_kernel,
        [(kron, BF16), (kron, BF16), (kron, BF16), (square, BF16)],
        [(stack, BF16), (kron, BF16)],
        [basis_lanes, sketch_t, site, site_other],
        2**31,
    )
    sketched, arrived_x, arrived_y = lax.optimization_barrier((sketched, arrived_x, arrived_y))
    swapped = exchanged(arrived_y, "row")
    next_basis, new, x_first, middle, lanes = call(
        upper_kernel,
        [(tall, BF16), (tall, BF16), (stack, BF16), (square, BF16), (flat, BF16)],
        [
            (tall, F32),
            (tall, F32),
            (tall, BF16),
            (flat, BF16),
            (flat, BF16),
            (stack, BF16),
            (square, BF16),
        ],
        [basis, sketched, first, arrived_x, arrived_y, kron_0, kron_first],
        2**33,
    )
    carried, back = call(
        state_kernel,
        [(tall, BF16), (tall, BF16)],
        [(tall, F32), (flat, BF16)],
        [middle, swapped],
        2**30,
    )
    next_basis, carried = lax.optimization_barrier((next_basis, carried))
    carried = exchanged(carried, "row")
    keep, send = call(
        lower_kernel,
        [(tall, BF16), (tall, BF16)],
        [(tall, F32), (stack, BF16), (square, BF16)],
        [next_basis, edge, lanes, kron_1, new],
        2**32,
    )
    received = exchanged(send, "row")
    (gradient,) = call(
        gradient_kernel,
        [(sites.shape, F32)],
        [(stack, BF16)],
        [x_first, back, carried, configuration],
        2**31,
    )
    received, gradient = lax.optimization_barrier((received, gradient))
    left_new = jnp.where(is_upper, keep, received)
    right_new = jnp.where(is_upper, received, keep)
    return (
        gradient.reshape(site_tensors.shape),
        left_new.reshape(left_bounds.shape),
        right_new.reshape(right_bounds.shape),
    )


def solution(mesh):
    return jax.shard_map(
        local,
        mesh=mesh,
        in_specs=(
            P(("grp", "row"), "col", None, None, None),
            P(("grp", "row"), "col", None, None, None),
            P(("grp", "row"), "col", None, None),
            P(("grp", "row"), "col"),
            P(("grp", "col"), None, None, None),
            P(("grp", "col"), None, None, None),
            P(),
        ),
        out_specs=(
            P(("grp", "row"), "col", None, None),
            P(("grp", "row"), "col", None, None, None),
            P(("grp", "row"), "col", None, None, None),
        ),
        check_vma=False,
    )
```

```python
import functools

import jax
import jax.numpy as jnp
from jax import lax
from jax.experimental import pallas as pl
from jax.experimental.pallas import tpu as pltpu
from jax.sharding import PartitionSpec as P

F32 = jnp.float32
BF16 = jnp.bfloat16
VMEM_BYTES = 24 * 1024 * 1024


def nn(a, b):
    return jnp.dot(a, b, preferred_element_type=F32)


def nt(a, b):
    return lax.dot_general(a, b, (((1,), (1,)), ((), ())), preferred_element_type=F32)


def split(x):
    high = x.astype(BF16)
    return high, (x - high.astype(F32)).astype(BF16)


def iota(shape, axis):
    return lax.broadcasted_iota(jnp.int32, shape, axis)


def chol_inverse(grams, near, beside=()):
    beside = list(beside)
    n = grams[0].shape[0]
    blocks = n // 8
    count = len(grams)
    lane = iota((8, n), 1)
    sub = iota((8, n), 0)
    at = [sub == j for j in range(8)]
    after = [sub > j for j in range(8)]
    tiles = [[g[8 * i : 8 * i + 8, :] for i in range(blocks)] for g in grams]

    def over_lanes(x, j):
        return jnp.broadcast_to(x[:, j : j + 1], (8, n))

    def over_rows(x, j):
        return jnp.broadcast_to(x[j : j + 1, :], (8, n))

    for b in range(blocks):
        own = (lane >= 8 * b) & (lane < 8 * b + 8)
        eye = jnp.where(lane - 8 * b == sub, 1.0, 0.0)
        by_element = range(b + 1, min(blocks, b + 1 + near))
        by_matmul = range(by_element.stop, blocks)
        diag = [[over_lanes(tiles[q][b], 8 * b + j) for j in range(8)] for q in range(count)]
        below = [
            [[over_lanes(tiles[q][i], 8 * b + j) for j in range(8)] for i in by_element]
            for q in range(count)
        ]
        forward = [jnp.where(own, eye, tiles[q][b]) for q in range(count)]
        full = list(forward)
        pivots = [jnp.ones((8, n), F32) for _ in range(count)]
        for step in beside[b * len(beside) // blocks : (b + 1) * len(beside) // blocks]:
            step()
        for j in range(8):
            for q in range(count):
                c = diag[q]
                pivot = over_rows(c[j], j)
                inverse = 1.0 / pivot
                pivots[q] = jnp.where(at[j], pivot, pivots[q])
                for k in range(j + 1, 8):
                    m = over_rows(c[k], j) * inverse
                    c[k] = jnp.where(at[j], m, c[k] - c[j] * m)
                row = over_rows(forward[q], j) * inverse
                forward[q] = jnp.where(after[j], forward[q] - c[j] * row, forward[q])
                full[q] = jnp.where(at[j], row, full[q] - c[j] * row)
        for q in range(count):
            rows = [over_rows(full[q], j) for j in range(8)]
            for i in by_element:
                terms = [below[q][i - b - 1][j] * rows[j] for j in range(8)]
                while len(terms) > 1:
                    terms = [x + y for x, y in zip(terms[::2], terms[1::2])]
                tiles[q][i] = jnp.where(own, 0.0, tiles[q][i]) - terms[0]
            if by_matmul:
                rest = jnp.concatenate([tiles[q][i] for i in by_matmul], axis=0)
                padded = [full[q], jnp.zeros((n - 8 * b - 8, n), F32)]
                if b:
                    padded = [jnp.zeros((8 * b, n), F32)] + padded
                update = jnp.dot(
                    rest,
                    jnp.concatenate(padded, axis=0),
                    precision=lax.Precision.HIGHEST,
                    preferred_element_type=F32,
                )
                for x, i in enumerate(by_matmul):
                    tiles[q][i] = jnp.where(own, 0.0, tiles[q][i]) - update[8 * x : 8 * x + 8]
            tiles[q][b] = jnp.where(lane <= sub + 8 * b, forward[q] * lax.rsqrt(pivots[q]), 0.0)
    return [jnp.concatenate(t, axis=0) for t in tiles]


def leg(scratch, j):
    chi = scratch.shape[1]
    return scratch[pl.ds(j, chi, stride=scratch.shape[0] // chi), :]


def kron_step(lhs, rhs, x_ref, t, first, count, transposed):
    chi = lhs.shape[1]
    bond = lhs.shape[0] // chi
    some = lhs[first * chi : (first + count) * chi, :]
    if transposed:
        product = nt(some, rhs[t * chi : (t + 2) * chi, :])
    else:
        product = nn(some, rhs[:, t * chi : (t + 2) * chi])
    for s in range(count):
        at = ((first + s) * bond + t) * 8
        for g in range(chi // 8):
            rows = product[s * chi + g * 8 : s * chi + g * 8 + 8, :]
            x_ref[at : at + 16, g * chi : (g + 1) * chi] = jnp.concatenate(
                [rows[:, :chi], rows[:, chi:]], axis=0
            ).astype(BF16)


def absorb_step(kron, x_ref, m_ref, chi, g, first, count):
    bond = m_ref.shape[0] // chi
    step = bond * 8
    out = nn(kron[first * step : (first + count) * step, :], x_ref[:, g * chi : (g + 2) * chi])
    for o in range(count):
        for d in range(bond):
            rows = out[(o * bond + d) * 8 : (o * bond + d) * 8 + 8, :]
            at = (first + o) * chi + g * 8
            m_ref[at : at + 16, d * chi : (d + 1) * chi] = jnp.concatenate(
                [rows[:, :chi], rows[:, chi:]], axis=0
            ).astype(BF16)


def kron_steps(lhs, rhs, x_ref, transposed=False, count=1):
    bond = lhs.shape[0] // lhs.shape[1]
    count = min(count, bond)
    return [
        functools.partial(kron_step, lhs, rhs, x_ref, t, first, count, transposed)
        for t in range(0, bond, 2)
        for first in range(0, bond, count)
    ]


def absorb_steps(kron, x_ref, m_ref, chi, count=2):
    bond = m_ref.shape[0] // chi
    count = min(count, bond)
    return [
        functools.partial(absorb_step, kron, x_ref, m_ref, chi, g, first, count)
        for g in range(0, chi // 8, 2)
        for first in range(0, bond, count)
    ]


def square_core(flat):
    half = flat.shape[1] // 2
    size = flat.shape[0] * 2
    i = iota((size, flat.shape[0]), 0)
    j = iota((size, flat.shape[0]), 1)
    even = jnp.where(i == 2 * j, 1.0, 0.0).astype(BF16)
    odd = jnp.where(i == 2 * j + 1, 1.0, 0.0).astype(BF16)
    return (nn(even, flat[:, :half]) + nn(odd, flat[:, half:])).astype(BF16)


def swap_order(size, bond):
    i = iota((size, size), 0)
    j = iota((size, size), 1)
    hit = (i // bond == j % bond) & (i % bond == j // bond)
    return jnp.where(hit, 1.0, 0.0).astype(BF16)


def spread(size):
    i = iota((size * 8, size), 0)
    j = iota((size * 8, size), 1)
    return jnp.where(i // 8 == j, 1.0, 0.0).astype(BF16)


def kron_of(spread_rows, size):
    wide = nt(spread_rows.astype(BF16), spread(size))
    i = iota(wide.shape, 0)
    j = iota(wide.shape, 1)
    return jnp.where(i % 8 == j % 8, wide, 0.0).astype(BF16)


def spread_ahead(core, bond):
    size = core.shape[0]
    return nt(spread(size), nn(swap_order(size, bond), core).astype(BF16))


def spread_turned(core, bond):
    size = core.shape[0]
    return nn(spread(size), nt(swap_order(size, bond), core).astype(BF16))


def spread_back(core, bond):
    size = core.shape[0]
    return nn(spread(size), nn(core, swap_order(size, bond)).astype(BF16))


def mirrored(core, bond):
    size = core.shape[0]
    i = iota((size, size), 0)
    j = iota((size, size), 1)
    total = jnp.zeros((size, size), F32)
    for u in range(bond):
        pick = jnp.where(j == (i // bond) * bond + u, 1.0, 0.0).astype(BF16)
        picked = jnp.where(i % bond == j % bond, nn(pick, core), 0.0).astype(BF16)
        place = jnp.where(j == u * bond + i // bond, 1.0, 0.0).astype(BF16)
        total = total + nn(picked, place)
    return total.astype(BF16)


def begin_kernel(left, right, sites, choice, first, second, core, chosen, sems):
    side = lax.axis_index("row")

    def start(one, other):
        pltpu.make_async_copy(one, first, sems.at[0]).start()
        pltpu.make_async_copy(other, second, sems.at[1]).start()

    pl.when(side == 0)(functools.partial(start, left, right))
    pl.when(side == 1)(functools.partial(start, right, left))
    copy = pltpu.make_async_copy(sites, chosen, sems.at[2])
    copy.start()
    copy.wait()
    total = jnp.zeros((1, chosen.shape[1]), F32)
    for p in range(chosen.shape[0]):
        total = total + jnp.where(choice[0, 0] == p, chosen[p : p + 1, :].astype(F32), 0.0)
    flat = [total[:, i : i + core.shape[1]] for i in range(0, total.shape[1], core.shape[1])]
    core[...] = jnp.concatenate(flat, axis=0).astype(BF16)
    pltpu.make_async_copy(left, first, sems.at[0]).wait()
    pltpu.make_async_copy(right, second, sems.at[1]).wait()


def edges_kernel(
    top_hbm,
    bottom_hbm,
    sketch_hbm,
    site,
    site_other,
    basis,
    basis_lanes,
    edge,
    first,
    sketch_t,
    kron_0,
    kron_1,
    kron_first,
    kron_sketch,
    top,
    bottom,
    sketch,
    wide,
    wide_sketch,
    legs_top,
    legs_bottom,
    sems,
):
    side = lax.axis_index("row")
    chi = top.shape[1]
    bond = top.shape[0] // chi
    copies = [
        pltpu.make_async_copy(source, target, sems.at[i])
        for i, (source, target) in enumerate(
            ((top_hbm, top), (bottom_hbm, bottom), (sketch_hbm, sketch))
        )
    ]
    for copy in copies:
        copy.start()
    for env, legs, mine in ((top, legs_top, 0), (bottom, legs_bottom, 1)):
        copies[mine].wait()
        wide[...] = env[...].astype(F32)

        @pl.when(side == 0)
        def _():
            for u in range(bond):
                block = leg(wide, u).T.astype(BF16)
                legs[:, u * chi : (u + 1) * chi] = block
                if mine == 0:
                    first[u * chi : (u + 1) * chi, :] = block

        @pl.when(side == 1)
        def _():
            for u in range(bond):
                block = leg(wide, u).astype(BF16)
                legs[:, u * chi : (u + 1) * chi] = block
                if mine == 1:
                    first[u * chi : (u + 1) * chi, :] = block

    copies[2].wait()
    wide_sketch[...] = sketch[...].astype(F32)

    def turn_sketch(o):
        sketch_t[o * chi : (o + 1) * chi, :] = leg(wide_sketch, o).T.astype(BF16)

    is_left = side == 0
    size = bond * bond
    swap = swap_order(size, bond)
    rows_of = spread(size)
    core = square_core(site[...])
    core_other = square_core(site_other[...])
    mirrored_own = mirrored(core, bond)
    mirrored_other = mirrored(core_other, bond)
    ahead = spread_ahead(core, bond)
    turned = nn(nn(swap, mirrored_own).astype(BF16), swap).astype(BF16)
    krons = (
        (kron_sketch, nn(rows_of, turned), spread_turned(core_other, bond)),
        (kron_0, ahead, nn(rows_of, mirrored_other)),
        (kron_first, ahead, spread_back(core, bond)),
        (kron_1, spread_ahead(core_other, bond), nn(rows_of, mirrored_own)),
    )

    def build_kron(target, left, right, part):
        step = size * 8 // 4
        at = slice(part * step, (part + 1) * step)
        target[at, :] = kron_of(jnp.where(is_left, left[at, :], right[at, :]), size)

    inverse_top, inverse_bottom = chol_inverse(
        [nt(legs_top[...], legs_top[...]), nt(legs_bottom[...], legs_bottom[...])],
        1,
        [functools.partial(turn_sketch, o) for o in range(bond)]
        + [functools.partial(build_kron, *args, part) for args in krons for part in range(4)],
    )
    high, low = split(inverse_top)
    ortho = (nn(high, legs_top[...]) + nn(low, legs_top[...])).astype(BF16)
    basis_lanes[...] = ortho
    for u in range(bond):
        basis[u * chi : (u + 1) * chi, :] = ortho[:, u * chi : (u + 1) * chi]
    high, low = split(inverse_bottom)
    edge[...] = (nn(high, legs_bottom[...]) + nn(low, legs_bottom[...])).astype(BF16)


def finish(absorbed, closing, wide):
    chi = closing.shape[0]
    bond = absorbed.shape[0] // chi
    unscaled = nt(absorbed[...], closing)
    for o in range(bond):
        wide[pl.ds(o, chi, stride=bond), :] = unscaled[o * chi : (o + 1) * chi, :]
    squares = jnp.sum(unscaled * unscaled, axis=0, keepdims=True)
    mean = jnp.sum(squares, axis=1, keepdims=True) * (1.0 / (chi * bond * chi))
    return (wide[...] * lax.rsqrt(mean + 1e-06)).astype(BF16)


def prepare_kernel(basis_lanes, sketch_t, kron_sketch, sketched, x):
    chi = basis_lanes.shape[0]
    for step in kron_steps(sketch_t, basis_lanes, x) + absorb_steps(kron_sketch, x, sketched, chi):
        step()


def upper_kernel(
    basis,
    sketched,
    first,
    arrived_x,
    arrived_y,
    kron_0,
    kron_first,
    next_basis,
    new,
    x_first,
    middle,
    lanes_1,
    wide_0,
    wide_1,
    rows_0,
    lanes_0,
    ahead,
    x,
    absorbed,
):
    is_left = lax.axis_index("row") == 0
    chi = basis.shape[1]
    bond = basis.shape[0] // chi
    blocks = [slice(j * chi, (j + 1) * chi) for j in range(bond)]
    @pl.when(is_left)
    def _():
        wide_0[...] = arrived_x[...].astype(F32)

    @pl.when(jnp.logical_not(is_left))
    def _():
        wide_0[...] = arrived_y[...].astype(F32)

    for j in range(bond):
        rows_0[blocks[j], :] = leg(wide_0, j).astype(BF16)
    stacked = nn(sketched[...], rows_0[...])
    range_t = jnp.concatenate([stacked[blocks[d], :] for d in range(bond)], axis=1)
    high, low = split(range_t)
    gram = nt(high, high) + (nt(high, low) + nt(low, high))

    def ready_lanes():
        for j in range(bond):
            lanes_0[:, blocks[j]] = rows_0[blocks[j], :]

    def ready_other(part):
        step = wide_1.shape[0] // 4
        at = slice(part * step, (part + 1) * step)
        wide_1[at, :] = jnp.where(is_left, arrived_y[at, :], arrived_x[at, :]).astype(F32)

    def ready_ahead(j):
        block = leg(wide_1, j)
        lanes_1[:, blocks[j]] = block.astype(BF16)
        ahead[:, blocks[j]] = jnp.where(is_left, leg(wide_0, j), block.T).astype(BF16)

    beside = (
        [ready_lanes]
        + kron_steps(basis, lanes_0, x)
        + [functools.partial(ready_other, part) for part in range(4)]
        + absorb_steps(kron_0, x, absorbed, chi)
        + [functools.partial(ready_ahead, j) for j in range(bond)]
        + kron_steps(first, ahead, x_first)
        + absorb_steps(kron_first, x_first, middle, chi)
    )
    (inverse,) = chol_inverse([gram], 3, beside)
    inverse_high, inverse_low = split(inverse)
    closing = (
        nn(inverse_high, high) + (nn(inverse_high, low) + nn(inverse_low, high))
    ).astype(BF16)
    for d in range(bond):
        next_basis[blocks[d], :] = closing[:, blocks[d]]
    new[...] = finish(absorbed, closing, wide_0)


def state_kernel(middle, received, carried, back, wide, behind):
    side = lax.axis_index("row")
    chi = received.shape[1]
    bond = received.shape[0] // chi
    wide[...] = received[...].astype(F32)

    @pl.when(side == 0)
    def _():
        for j in range(bond):
            at = slice(j * chi, (j + 1) * chi)
            block = leg(wide, j)
            behind[:, at] = block.T.astype(BF16)
            back[at, :] = block.astype(BF16)

    @pl.when(side == 1)
    def _():
        for j in range(bond):
            at = slice(j * chi, (j + 1) * chi)
            block = leg(wide, j)
            behind[:, at] = block.astype(BF16)
            back[at, :] = block.T.astype(BF16)

    state = nn(behind[...], middle[...]).astype(BF16)
    for s in range(bond):
        carried[s * chi : (s + 1) * chi, :] = state[:, s * chi : (s + 1) * chi]


def lower_kernel(basis, edge, lanes, kron, new_0, keep, send, wide, x, absorbed):
    side = lax.axis_index("row")
    chi = basis.shape[1]
    for step in kron_steps(basis, lanes, x) + absorb_steps(kron, x, absorbed, chi):
        step()
    new = finish(absorbed, edge[...], wide)

    @pl.when(side == 0)
    def _():
        keep[...] = new_0[...]
        send[...] = new

    @pl.when(side == 1)
    def _():
        keep[...] = new
        send[...] = new_0[...]


def product_kernel(x_first, back, carried, product, x_second):
    side = lax.axis_index("row")
    for step in kron_steps(back, carried, x_second, True):
        step()

    @pl.when(side == 0)
    def _():
        product[...] = nt(x_first[...], x_second[...])

    @pl.when(side == 1)
    def _():
        product[...] = nt(x_second[...], x_first[...])


def place_kernel(product, choice, keep, received, gradient, left, right, entries, sems):
    side = lax.axis_index("row")
    is_left = side == 0
    phys_count = gradient.shape[0]
    size = product.shape[0] // 8
    bond = round(size**0.5)
    chi = keep.shape[1]

    def start(one, other):
        pltpu.make_async_copy(one, left, sems.at[0]).start()
        pltpu.make_async_copy(other, right, sems.at[1]).start()

    pl.when(side == 0)(functools.partial(start, keep, received))
    pl.when(side == 1)(functools.partial(start, received, keep))

    def one_hot(i, j, swapped):
        i = i // 8
        other = (i % bond) * bond + i // bond
        return jnp.where(j == jnp.where(swapped, other, i), 1.0, 0.0).astype(BF16)

    i = iota(product.shape, 0)
    j = iota(product.shape, 1)
    diagonal = jnp.where(i % 8 == j % 8, product[...], 0.0).astype(BF16)
    wide = (size * 8, size * 2)
    half = jnp.zeros((size // 2, size * 2), F32)
    for odd in range(2):
        columns = one_hot(iota(wide, 0), iota(wide, 1) - odd * size, side == 1)
        rows = one_hot(iota(wide[::-1], 1), iota(wide[::-1], 0) * 2 + odd, is_left)[: size // 2]
        high, low = split(nn(diagonal, columns))
        half = half + (nn(rows, high) + nn(rows, low))
    half = half * (bond / chi)
    phys = iota((phys_count, size * 2), 0)
    for r in range(size // 2):
        row = jnp.broadcast_to(half[r : r + 1, :], phys.shape)
        entries[:, r * size * 2 : (r + 1) * size * 2] = jnp.where(phys == choice[0, 0], row, 0.0)
    copy = pltpu.make_async_copy(entries, gradient, sems.at[2])
    copy.start()
    pltpu.make_async_copy(keep, left, sems.at[0]).wait()
    pltpu.make_async_copy(keep, right, sems.at[1]).wait()
    copy.wait()


def call(kernel, out_shapes, scratch, inputs, flops, in_place=(), copies=0, out_space=pltpu.VMEM):
    inputs = [
        pltpu.with_memory_space_constraint(x, pltpu.HBM) if i in in_place else x
        for i, x in enumerate(inputs)
    ]
    vmem = pl.BlockSpec(memory_space=pltpu.VMEM)
    smem = pl.BlockSpec(memory_space=pltpu.SMEM)
    return pl.pallas_call(
        kernel,
        out_shape=[jax.ShapeDtypeStruct(s, t) for s, t in out_shapes],
        in_specs=[
            smem
            if x.dtype == jnp.int32
            else pl.BlockSpec(memory_space=pltpu.HBM)
            if i in in_place
            else vmem
            for i, x in enumerate(inputs)
        ],
        out_specs=[pl.BlockSpec(memory_space=out_space) for _ in out_shapes],
        scratch_shapes=[pltpu.VMEM(s, t) for s, t in scratch]
        + ([pltpu.SemaphoreType.DMA((copies,))] if copies else []),
        compiler_params=pltpu.CompilerParams(vmem_limit_bytes=VMEM_BYTES),
        cost_estimate=pl.CostEstimate(flops=flops, bytes_accessed=2**21, transcendentals=0),
    )(*inputs)


def moved(block, pairs):
    return lax.ppermute(block, ("col", "row"), pairs)


def exchanged(block, axis):
    return lax.ppermute(block, axis, [(0, 1), (1, 0)])


def local(left_bounds, right_bounds, site_tensors, configuration, top_env, bottom_env, sketch):
    chi = left_bounds.shape[2]
    bond = left_bounds.shape[3]
    rows = chi * bond
    size = bond * bond
    tall = (rows, chi)
    flat = (chi, rows)
    kron = (size * 8, size * 8)
    stack = (size * 8, chi // 8 * chi)
    square = (rows, rows)
    count = lax.axis_size("col")
    sites = site_tensors.reshape(site_tensors.shape[2:])
    first_sent, second_sent, site = call(
        begin_kernel,
        [(tall, BF16), (tall, BF16), ((size // 2, size * 2), BF16)],
        [(sites.shape, BF16)],
        [left_bounds.reshape(tall), right_bounds.reshape(tall), sites, configuration],
        2**20,
        in_place=(0, 1, 2),
        copies=3,
    )
    ahead, behind = (
        [2 * ((c + step) % count) for c in range(count)] for step in (1, -1)
    )
    arrived_x = moved(
        first_sent,
        [(2 * c, ahead[c]) for c in range(count)]
        + [(2 * c + 1, behind[c] + 1) for c in range(count)],
    )
    arrived_y = moved(
        second_sent,
        [(2 * c, behind[c] + 1) for c in range(count)]
        + [(2 * c + 1, ahead[c]) for c in range(count)],
    )
    site_other = exchanged(site, "row")
    basis, basis_lanes, edge, first, sketch_t, kron_0, kron_1, kron_first, kron_sketch = call(
        edges_kernel,
        [(tall, BF16), (flat, BF16), (flat, BF16), (tall, BF16), (tall, BF16)] + [(kron, BF16)] * 4,
        [(tall, BF16)] * 3 + [(tall, F32), (tall, F32), (flat, BF16), (flat, BF16)],
        [top_env.reshape(tall), bottom_env.reshape(tall), sketch, site, site_other],
        2**31,
        in_place=(0, 1, 2),
        copies=3,
    )
    (sketched,) = call(
        prepare_kernel,
        [(square, BF16)],
        [(stack, BF16)],
        [basis_lanes, sketch_t, kron_sketch],
        2**31,
    )
    sketched, arrived_x, arrived_y = lax.optimization_barrier((sketched, arrived_x, arrived_y))
    swapped = exchanged(arrived_y, "row")
    next_basis, new, x_first, middle, lanes = call(
        upper_kernel,
        [(tall, BF16), (tall, BF16), (stack, BF16), (square, BF16), (flat, BF16)],
        [
            (tall, F32),
            (tall, F32),
            (tall, BF16),
            (flat, BF16),
            (flat, BF16),
            (stack, BF16),
            (square, BF16),
        ],
        [basis, sketched, first, arrived_x, arrived_y, kron_0, kron_first],
        2**33,
    )
    carried, back = call(
        state_kernel,
        [(tall, BF16), (tall, BF16)],
        [(tall, F32), (flat, BF16)],
        [middle, swapped],
        2**30,
    )
    next_basis, carried = lax.optimization_barrier((next_basis, carried))
    carried = exchanged(carried, "row")
    keep, send = call(
        lower_kernel,
        [(tall, BF16), (tall, BF16)],
        [(tall, F32), (stack, BF16), (square, BF16)],
        [next_basis, edge, lanes, kron_1, new],
        2**32,
    )
    received = exchanged(send, "row")
    (product,) = call(
        product_kernel,
        [(kron, F32)],
        [(stack, BF16)],
        [x_first, back, carried],
        2**31,
    )
    received, product = lax.optimization_barrier((received, product))
    gradient, left_new, right_new = call(
        place_kernel,
        [(sites.shape, F32), (tall, BF16), (tall, BF16)],
        [(sites.shape, F32)],
        [product, configuration, keep, received],
        2**30,
        copies=3,
        out_space=pltpu.HBM,
    )
    return (
        gradient.reshape(site_tensors.shape),
        left_new.reshape(left_bounds.shape),
        right_new.reshape(right_bounds.shape),
    )


def solution(mesh):
    return jax.shard_map(
        local,
        mesh=mesh,
        in_specs=(
            P(("grp", "row"), "col", None, None, None),
            P(("grp", "row"), "col", None, None, None),
            P(("grp", "row"), "col", None, None),
            P(("grp", "row"), "col"),
            P(("grp", "col"), None, None, None),
            P(("grp", "col"), None, None, None),
            P(),
        ),
        out_specs=(
            P(("grp", "row"), "col", None, None),
            P(("grp", "row"), "col", None, None, None),
            P(("grp", "row"), "col", None, None, None),
        ),
        check_vma=False,
    )
```

```python
import functools

import jax
import jax.numpy as jnp
from jax import lax
from jax.experimental import pallas as pl
from jax.experimental.pallas import tpu as pltpu
from jax.sharding import PartitionSpec as P

F32 = jnp.float32
BF16 = jnp.bfloat16
VMEM_BYTES = 24 * 1024 * 1024
PART = 4


def nn(a, b):
    return jnp.dot(a, b, preferred_element_type=F32)


def nt(a, b):
    return lax.dot_general(a, b, (((1,), (1,)), ((), ())), preferred_element_type=F32)


def split(x):
    high = x.astype(BF16)
    return high, (x - high.astype(F32)).astype(BF16)


def iota(shape, axis):
    return lax.broadcasted_iota(jnp.int32, shape, axis)


def chol_inverse(grams, near, beside=()):
    beside = list(beside)
    n = grams[0].shape[0]
    blocks = n // 8
    count = len(grams)
    lane = iota((8, n), 1)
    sub = iota((8, n), 0)
    at = [sub == j for j in range(8)]
    after = [sub > j for j in range(8)]
    tiles = [[g[8 * i : 8 * i + 8, :] for i in range(blocks)] for g in grams]

    def over_lanes(x, j):
        return jnp.broadcast_to(x[:, j : j + 1], (8, n))

    def over_rows(x, j):
        return jnp.broadcast_to(x[j : j + 1, :], (8, n))

    for b in range(blocks):
        own = (lane >= 8 * b) & (lane < 8 * b + 8)
        eye = jnp.where(lane - 8 * b == sub, 1.0, 0.0)
        by_element = range(b + 1, min(blocks, b + 1 + near))
        by_matmul = range(by_element.stop, blocks)
        diag = [[over_lanes(tiles[q][b], 8 * b + j) for j in range(8)] for q in range(count)]
        below = [
            [[over_lanes(tiles[q][i], 8 * b + j) for j in range(8)] for i in by_element]
            for q in range(count)
        ]
        forward = [jnp.where(own, eye, tiles[q][b]) for q in range(count)]
        full = list(forward)
        pivots = [jnp.ones((8, n), F32) for _ in range(count)]
        for step in beside[b * len(beside) // blocks : (b + 1) * len(beside) // blocks]:
            step()
        for j in range(8):
            for q in range(count):
                c = diag[q]
                pivot = over_rows(c[j], j)
                inverse = 1.0 / pivot
                pivots[q] = jnp.where(at[j], pivot, pivots[q])
                for k in range(j + 1, 8):
                    m = over_rows(c[k], j) * inverse
                    c[k] = jnp.where(at[j], m, c[k] - c[j] * m)
                row = over_rows(forward[q], j) * inverse
                forward[q] = jnp.where(after[j], forward[q] - c[j] * row, forward[q])
                full[q] = jnp.where(at[j], row, full[q] - c[j] * row)
        for q in range(count):
            rows = [over_rows(full[q], j) for j in range(8)]
            for i in by_element:
                terms = [below[q][i - b - 1][j] * rows[j] for j in range(8)]
                while len(terms) > 1:
                    terms = [x + y for x, y in zip(terms[::2], terms[1::2])]
                tiles[q][i] = jnp.where(own, 0.0, tiles[q][i]) - terms[0]
            if by_matmul:
                rest = jnp.concatenate([tiles[q][i] for i in by_matmul], axis=0)
                padded = [full[q], jnp.zeros((n - 8 * b - 8, n), F32)]
                if b:
                    padded = [jnp.zeros((8 * b, n), F32)] + padded
                update = jnp.dot(
                    rest,
                    jnp.concatenate(padded, axis=0),
                    precision=lax.Precision.HIGHEST,
                    preferred_element_type=F32,
                )
                for x, i in enumerate(by_matmul):
                    tiles[q][i] = jnp.where(own, 0.0, tiles[q][i]) - update[8 * x : 8 * x + 8]
            tiles[q][b] = jnp.where(lane <= sub + 8 * b, forward[q] * lax.rsqrt(pivots[q]), 0.0)
    return [jnp.concatenate(t, axis=0) for t in tiles]


def leg(scratch, j):
    chi = scratch.shape[1]
    return scratch[pl.ds(j, chi, stride=scratch.shape[0] // chi), :]


def weave(one, two, target, at):
    chi = one.shape[0]
    for g in range(0, chi, 2 * PART):
        rows = [block[k : k + PART, :] for k in (g, g + PART) for block in (one, two)]
        target[at + 2 * g : at + 2 * g + 4 * PART, :] = jnp.concatenate(rows, axis=0).astype(BF16)


def kron_step(lhs, rhs, x_ref, t, pair, transposed):
    chi = lhs.shape[1]
    bond = lhs.shape[0] // chi
    some = lhs[pair * 2 * chi : (pair + 1) * 2 * chi, :]
    if transposed:
        product = nt(some, rhs[t * chi : (t + 2) * chi, :])
    else:
        product = nn(some, rhs[:, t * chi : (t + 2) * chi])
    at = (pair * bond + t) * 2 * PART
    for g in range(chi // PART):
        rows = product[g * 2 * PART : (g + 1) * 2 * PART, :]
        x_ref[at : at + 4 * PART, g * chi : (g + 1) * chi] = jnp.concatenate(
            [rows[:, :chi], rows[:, chi:]], axis=0
        ).astype(BF16)


def absorb_step(kron, x_ref, m_ref, chi, g, first, count):
    bond = m_ref.shape[0] // chi
    step = bond * PART
    out = nn(kron[first * step : (first + count) * step, :], x_ref[:, g * chi : (g + 4) * chi])
    for o in range(count):
        for d in range(0, bond, 2):
            rows = out[(o * bond + d) * PART : (o * bond + d + 2) * PART, :]
            parts = [rows[:, k * chi : (k + 1) * chi] for k in range(4)]
            at = (first + o) * chi + g * PART
            for k in range(2):
                m_ref[at : at + 4 * PART, (d + k) * chi : (d + k + 1) * chi] = jnp.concatenate(
                    [part[k * PART : (k + 1) * PART, :] for part in parts], axis=0
                ).astype(BF16)


def kron_steps(lhs, rhs, x_ref, transposed=False):
    bond = lhs.shape[0] // lhs.shape[1]
    return [
        functools.partial(kron_step, lhs, rhs, x_ref, t, pair, transposed)
        for t in range(0, bond, 2)
        for pair in range(bond // 2)
    ]


def absorb_steps(kron, x_ref, m_ref, chi, count=4):
    bond = m_ref.shape[0] // chi
    return [
        functools.partial(absorb_step, kron, x_ref, m_ref, chi, g, first, count)
        for g in range(0, chi // PART, 4)
        for first in range(0, bond, count)
    ]


def square_core(row):
    values = row[...].astype(F32)
    size = round(values.shape[1] ** 0.5)
    flat = [values[:, i : i + 2 * size] for i in range(0, size * size, 2 * size)]
    flat = jnp.concatenate(flat, axis=0).astype(BF16)
    i = iota((size, size // 2), 0)
    j = iota((size, size // 2), 1)
    even = jnp.where(i == 2 * j, 1.0, 0.0).astype(BF16)
    odd = jnp.where(i == 2 * j + 1, 1.0, 0.0).astype(BF16)
    return (nn(even, flat[:, :size]) + nn(odd, flat[:, size:])).astype(BF16)


def swap_order(size, bond):
    i = iota((size, size), 0)
    j = iota((size, size), 1)
    hit = (i // bond == j % bond) & (i % bond == j // bond)
    return jnp.where(hit, 1.0, 0.0).astype(BF16)


def spread(size):
    i = iota((size * PART, size), 0)
    j = iota((size * PART, size), 1)
    return jnp.where(i // PART == j, 1.0, 0.0).astype(BF16)


def woven_pair(i, bond):
    i = i // PART
    s = (i // (2 * bond)) * 2 + i % 2
    t = (i // 4) % (bond // 2) * 2 + (i // 2) % 2
    return s, t


def kron_of(spread_rows, size):
    bond = round(size**0.5)
    s, t = woven_pair(iota((size * PART, size), 0), bond)
    spread_columns = jnp.where(s * bond + t == iota((size * PART, size), 1), 1.0, 0.0).astype(BF16)
    wide = nt(spread_rows.astype(BF16), spread_columns)
    i = iota(wide.shape, 0)
    j = iota(wide.shape, 1)
    return jnp.where(i % PART == j % PART, wide, 0.0).astype(BF16)


def spread_ahead(core, bond):
    size = core.shape[0]
    return nt(spread(size), nn(swap_order(size, bond), core).astype(BF16))


def spread_turned(core, bond):
    size = core.shape[0]
    return nn(spread(size), nt(swap_order(size, bond), core).astype(BF16))


def spread_back(core, bond):
    size = core.shape[0]
    return nn(spread(size), nn(core, swap_order(size, bond)).astype(BF16))


def mirrored(core, bond):
    size = core.shape[0]
    i = iota((size, size), 0)
    j = iota((size, size), 1)
    total = jnp.zeros((size, size), F32)
    for u in range(bond):
        pick = jnp.where(j == (i // bond) * bond + u, 1.0, 0.0).astype(BF16)
        picked = jnp.where(i % bond == j % bond, nn(pick, core), 0.0).astype(BF16)
        place = jnp.where(j == u * bond + i // bond, 1.0, 0.0).astype(BF16)
        total = total + nn(picked, place)
    return total.astype(BF16)


def begin_kernel(left, right, sites, choice, first, second, core, chosen, sems):
    side = lax.axis_index("row")

    def start(one, other):
        pltpu.make_async_copy(one, first, sems.at[0]).start()
        pltpu.make_async_copy(other, second, sems.at[1]).start()

    pl.when(side == 0)(functools.partial(start, left, right))
    pl.when(side == 1)(functools.partial(start, right, left))
    copy = pltpu.make_async_copy(sites, chosen, sems.at[2])
    copy.start()
    copy.wait()
    total = jnp.zeros((1, chosen.shape[1]), F32)
    for p in range(chosen.shape[0]):
        total = total + jnp.where(choice[0, 0] == p, chosen[p : p + 1, :].astype(F32), 0.0)
    core[...] = total.astype(BF16)
    pltpu.make_async_copy(left, first, sems.at[0]).wait()
    pltpu.make_async_copy(right, second, sems.at[1]).wait()


def edges_kernel(
    top_hbm,
    bottom_hbm,
    sketch_hbm,
    site,
    site_other,
    basis,
    basis_lanes,
    edge,
    first,
    sketch_t,
    kron_0,
    kron_1,
    kron_first,
    kron_sketch,
    top,
    bottom,
    sketch,
    wide,
    wide_sketch,
    legs_top,
    legs_bottom,
    sems,
):
    side = lax.axis_index("row")
    chi = top.shape[1]
    bond = top.shape[0] // chi
    copies = [
        pltpu.make_async_copy(source, target, sems.at[i])
        for i, (source, target) in enumerate(
            ((top_hbm, top), (bottom_hbm, bottom), (sketch_hbm, sketch))
        )
    ]
    for copy in copies:
        copy.start()
    for env, legs, mine in ((top, legs_top, 0), (bottom, legs_bottom, 1)):
        copies[mine].wait()
        wide[...] = env[...].astype(F32)

        @pl.when(side == 0)
        def _():
            for u in range(0, bond, 2):
                pair = [leg(wide, u).T, leg(wide, u + 1).T]
                for k in range(2):
                    legs[:, (u + k) * chi : (u + k + 1) * chi] = pair[k].astype(BF16)
                if mine == 0:
                    weave(*pair, first, u * chi)

        @pl.when(side == 1)
        def _():
            for u in range(0, bond, 2):
                pair = [leg(wide, u), leg(wide, u + 1)]
                for k in range(2):
                    legs[:, (u + k) * chi : (u + k + 1) * chi] = pair[k].astype(BF16)
                if mine == 1:
                    weave(*pair, first, u * chi)

    copies[2].wait()
    wide_sketch[...] = sketch[...].astype(F32)

    def turn_sketch(o):
        weave(leg(wide_sketch, o).T, leg(wide_sketch, o + 1).T, sketch_t, o * chi)

    is_left = side == 0
    size = bond * bond
    swap = swap_order(size, bond)
    rows_of = spread(size)
    core = square_core(site[...])
    core_other = square_core(site_other[...])
    mirrored_own = mirrored(core, bond)
    mirrored_other = mirrored(core_other, bond)
    ahead = spread_ahead(core, bond)
    turned = nn(nn(swap, mirrored_own).astype(BF16), swap).astype(BF16)
    krons = (
        (kron_sketch, nn(rows_of, turned), spread_turned(core_other, bond)),
        (kron_0, ahead, nn(rows_of, mirrored_other)),
        (kron_first, ahead, spread_back(core, bond)),
        (kron_1, spread_ahead(core_other, bond), nn(rows_of, mirrored_own)),
    )

    def build_kron(target, left, right, part):
        step = size * PART // 4
        at = slice(part * step, (part + 1) * step)
        target[at, :] = kron_of(jnp.where(is_left, left[at, :], right[at, :]), size)

    inverse_top, inverse_bottom = chol_inverse(
        [nt(legs_top[...], legs_top[...]), nt(legs_bottom[...], legs_bottom[...])],
        1,
        [functools.partial(turn_sketch, o) for o in range(0, bond, 2)]
        + [functools.partial(build_kron, *args, part) for args in krons for part in range(4)],
    )
    high, low = split(inverse_top)
    ortho = nn(high, legs_top[...]) + nn(low, legs_top[...])
    basis_lanes[...] = ortho.astype(BF16)
    blocks = [ortho[:, u * chi : (u + 1) * chi] for u in range(bond)]
    for u in range(0, bond, 2):
        weave(blocks[u], blocks[u + 1], basis, u * chi)
    high, low = split(inverse_bottom)
    edge[...] = (nn(high, legs_bottom[...]) + nn(low, legs_bottom[...])).astype(BF16)


def finish(absorbed, closing, wide):
    chi = closing.shape[0]
    bond = absorbed.shape[0] // chi
    unscaled = nt(absorbed[...], closing)
    for o in range(bond):
        wide[pl.ds(o, chi, stride=bond), :] = unscaled[o * chi : (o + 1) * chi, :]
    squares = jnp.sum(unscaled * unscaled, axis=0, keepdims=True)
    mean = jnp.sum(squares, axis=1, keepdims=True) * (1.0 / (chi * bond * chi))
    return (wide[...] * lax.rsqrt(mean + 1e-06)).astype(BF16)


def prepare_kernel(basis_lanes, sketch_t, kron_sketch, sketched, x):
    chi = basis_lanes.shape[0]
    for step in kron_steps(sketch_t, basis_lanes, x) + absorb_steps(kron_sketch, x, sketched, chi):
        step()


def upper_kernel(
    basis,
    sketched,
    first,
    arrived_x,
    arrived_y,
    kron_0,
    kron_first,
    next_basis,
    closing,
    absorbed,
    x_first,
    middle,
    lanes_1,
    wide_0,
    wide_1,
    rows_0,
    lanes_0,
    ahead,
    x,
):
    is_left = lax.axis_index("row") == 0
    chi = basis.shape[1]
    bond = basis.shape[0] // chi
    blocks = [slice(j * chi, (j + 1) * chi) for j in range(bond)]
    @pl.when(is_left)
    def _():
        wide_0[...] = arrived_x[...].astype(F32)

    @pl.when(jnp.logical_not(is_left))
    def _():
        wide_0[...] = arrived_y[...].astype(F32)

    for j in range(bond):
        rows_0[blocks[j], :] = leg(wide_0, j).astype(BF16)
    stacked = nn(sketched[...], rows_0[...])
    range_t = jnp.concatenate([stacked[blocks[d], :] for d in range(bond)], axis=1)
    high, low = split(range_t)
    gram = nt(high, high) + (nt(high, low) + nt(low, high))

    def ready_lanes():
        for j in range(bond):
            lanes_0[:, blocks[j]] = rows_0[blocks[j], :]

    def ready_other(part):
        step = wide_1.shape[0] // 4
        at = slice(part * step, (part + 1) * step)
        wide_1[at, :] = jnp.where(is_left, arrived_y[at, :], arrived_x[at, :]).astype(F32)

    def ready_ahead(j):
        block = leg(wide_1, j)
        lanes_1[:, blocks[j]] = block.astype(BF16)
        ahead[:, blocks[j]] = jnp.where(is_left, leg(wide_0, j), block.T).astype(BF16)

    beside = (
        [ready_lanes]
        + kron_steps(basis, lanes_0, x)
        + [functools.partial(ready_other, part) for part in range(4)]
        + absorb_steps(kron_0, x, absorbed, chi)
        + [functools.partial(ready_ahead, j) for j in range(bond)]
        + kron_steps(first, ahead, x_first)
        + absorb_steps(kron_first, x_first, middle, chi)
    )
    (inverse,) = chol_inverse([gram], 3, beside)
    inverse_high, inverse_low = split(inverse)
    ortho = nn(inverse_high, high) + (nn(inverse_high, low) + nn(inverse_low, high))
    closing[...] = ortho.astype(BF16)
    for d in range(0, bond, 2):
        weave(ortho[:, blocks[d]], ortho[:, blocks[d + 1]], next_basis, d * chi)


def state_kernel(middle, received, carried, back, wide, behind):
    side = lax.axis_index("row")
    chi = received.shape[1]
    bond = received.shape[0] // chi
    wide[...] = received[...].astype(F32)

    @pl.when(side == 0)
    def _():
        for j in range(0, bond, 2):
            pair = [leg(wide, j), leg(wide, j + 1)]
            for k in range(2):
                behind[:, (j + k) * chi : (j + k + 1) * chi] = pair[k].T.astype(BF16)
            weave(*pair, back, j * chi)

    @pl.when(side == 1)
    def _():
        for j in range(0, bond, 2):
            pair = [leg(wide, j), leg(wide, j + 1)]
            for k in range(2):
                behind[:, (j + k) * chi : (j + k + 1) * chi] = pair[k].astype(BF16)
            weave(pair[0].T, pair[1].T, back, j * chi)

    state = nn(behind[...], middle[...]).astype(BF16)
    for s in range(bond):
        carried[s * chi : (s + 1) * chi, :] = state[:, s * chi : (s + 1) * chi]


def lower_kernel(
    basis, edge, lanes, kron, closing_0, absorbed_0, keep, send, wide_0, wide, x, absorbed
):
    side = lax.axis_index("row")
    chi = basis.shape[1]
    new_0 = finish(absorbed_0, closing_0[...], wide_0)
    for step in kron_steps(basis, lanes, x) + absorb_steps(kron, x, absorbed, chi):
        step()
    new_1 = finish(absorbed, edge[...], wide)

    @pl.when(side == 0)
    def _():
        keep[...] = new_0
        send[...] = new_1

    @pl.when(side == 1)
    def _():
        keep[...] = new_1
        send[...] = new_0


def product_kernel(x_first, back, carried, product, x_second):
    side = lax.axis_index("row")
    for step in kron_steps(back, carried, x_second, True):
        step()

    @pl.when(side == 0)
    def _():
        product[...] = nt(x_first[...], x_second[...])

    @pl.when(side == 1)
    def _():
        product[...] = nt(x_second[...], x_first[...])


def place_kernel(product, choice, keep, received, gradient, left, right, entries, sems):
    side = lax.axis_index("row")
    is_left = side == 0
    phys_count = gradient.shape[0]
    size = product.shape[0] // PART
    bond = round(size**0.5)
    chi = keep.shape[1]

    def start(one, other):
        pltpu.make_async_copy(one, left, sems.at[0]).start()
        pltpu.make_async_copy(other, right, sems.at[1]).start()

    pl.when(side == 0)(functools.partial(start, keep, received))
    pl.when(side == 1)(functools.partial(start, received, keep))

    def one_hot(i, j, swapped):
        s, t = woven_pair(i, bond)
        at = jnp.where(swapped, t * bond + s, s * bond + t)
        return jnp.where(j == at, 1.0, 0.0).astype(BF16)

    i = iota(product.shape, 0)
    j = iota(product.shape, 1)
    diagonal = jnp.where(i % PART == j % PART, product[...], 0.0).astype(BF16)
    wide = (size * PART, size * 2)
    half = jnp.zeros((size // 2, size * 2), F32)
    for odd in range(2):
        columns = one_hot(iota(wide, 0), iota(wide, 1) - odd * size, side == 1)
        rows = one_hot(iota(wide[::-1], 1), iota(wide[::-1], 0) * 2 + odd, is_left)[: size // 2]
        high, low = split(nn(diagonal, columns))
        half = half + (nn(rows, high) + nn(rows, low))
    half = half * (bond / chi)
    phys = iota((phys_count, size * 2), 0)
    for r in range(size // 2):
        row = jnp.broadcast_to(half[r : r + 1, :], phys.shape)
        entries[:, r * size * 2 : (r + 1) * size * 2] = jnp.where(phys == choice[0, 0], row, 0.0)
    copy = pltpu.make_async_copy(entries, gradient, sems.at[2])
    copy.start()
    pltpu.make_async_copy(keep, left, sems.at[0]).wait()
    pltpu.make_async_copy(keep, right, sems.at[1]).wait()
    copy.wait()


def call(kernel, out_shapes, scratch, inputs, flops, in_place=(), copies=0, out_space=pltpu.VMEM):
    inputs = [
        pltpu.with_memory_space_constraint(x, pltpu.HBM) if i in in_place else x
        for i, x in enumerate(inputs)
    ]
    vmem = pl.BlockSpec(memory_space=pltpu.VMEM)
    smem = pl.BlockSpec(memory_space=pltpu.SMEM)
    return pl.pallas_call(
        kernel,
        out_shape=[jax.ShapeDtypeStruct(s, t) for s, t in out_shapes],
        in_specs=[
            smem
            if x.dtype == jnp.int32
            else pl.BlockSpec(memory_space=pltpu.HBM)
            if i in in_place
            else vmem
            for i, x in enumerate(inputs)
        ],
        out_specs=[pl.BlockSpec(memory_space=out_space) for _ in out_shapes],
        scratch_shapes=[pltpu.VMEM(s, t) for s, t in scratch]
        + ([pltpu.SemaphoreType.DMA((copies,))] if copies else []),
        compiler_params=pltpu.CompilerParams(vmem_limit_bytes=VMEM_BYTES),
        cost_estimate=pl.CostEstimate(flops=flops, bytes_accessed=2**21, transcendentals=0),
    )(*inputs)


def moved(block, pairs):
    return lax.ppermute(block, ("col", "row"), pairs)


def exchanged(block, axis):
    return lax.ppermute(block, axis, [(0, 1), (1, 0)])


def local(left_bounds, right_bounds, site_tensors, configuration, top_env, bottom_env, sketch):
    chi = left_bounds.shape[2]
    bond = left_bounds.shape[3]
    rows = chi * bond
    size = bond * bond
    tall = (rows, chi)
    flat = (chi, rows)
    kron = (size * PART, size * PART)
    stack = (size * PART, chi // PART * chi)
    square = (rows, rows)
    count = lax.axis_size("col")
    sites = site_tensors.reshape(site_tensors.shape[2:])
    first_sent, second_sent, site = call(
        begin_kernel,
        [(tall, BF16), (tall, BF16), ((1, size * size), BF16)],
        [(sites.shape, BF16)],
        [left_bounds.reshape(tall), right_bounds.reshape(tall), sites, configuration],
        2**20,
        in_place=(0, 1, 2),
        copies=3,
    )
    ahead, behind = (
        [2 * ((c + step) % count) for c in range(count)] for step in (1, -1)
    )
    arrived_x = moved(
        first_sent,
        [(2 * c, ahead[c]) for c in range(count)]
        + [(2 * c + 1, behind[c] + 1) for c in range(count)],
    )
    arrived_y = moved(
        second_sent,
        [(2 * c, behind[c] + 1) for c in range(count)]
        + [(2 * c + 1, ahead[c]) for c in range(count)],
    )
    site_other = exchanged(site, "row")
    basis, basis_lanes, edge, first, sketch_t, kron_0, kron_1, kron_first, kron_sketch = call(
        edges_kernel,
        [(tall, BF16), (flat, BF16), (flat, BF16), (tall, BF16), (tall, BF16)] + [(kron, BF16)] * 4,
        [(tall, BF16)] * 3 + [(tall, F32), (tall, F32), (flat, BF16), (flat, BF16)],
        [top_env.reshape(tall), bottom_env.reshape(tall), sketch, site, site_other],
        2**31,
        in_place=(0, 1, 2),
        copies=3,
    )
    (sketched,) = call(
        prepare_kernel,
        [(square, BF16)],
        [(stack, BF16)],
        [basis_lanes, sketch_t, kron_sketch],
        2**31,
    )
    sketched, arrived_x, arrived_y = lax.optimization_barrier((sketched, arrived_x, arrived_y))
    swapped = exchanged(arrived_y, "row")
    next_basis, closing, absorbed, x_first, middle, lanes = call(
        upper_kernel,
        [
            (tall, BF16),
            (flat, BF16),
            (square, BF16),
            (stack, BF16),
            (square, BF16),
            (flat, BF16),
        ],
        [(tall, F32), (tall, F32), (tall, BF16), (flat, BF16), (flat, BF16), (stack, BF16)],
        [basis, sketched, first, arrived_x, arrived_y, kron_0, kron_first],
        2**33,
    )
    carried, back = call(
        state_kernel,
        [(tall, BF16), (tall, BF16)],
        [(tall, F32), (flat, BF16)],
        [middle, swapped],
        2**30,
    )
    next_basis, carried = lax.optimization_barrier((next_basis, carried))
    carried = exchanged(carried, "row")
    keep, send = call(
        lower_kernel,
        [(tall, BF16), (tall, BF16)],
        [(tall, F32), (tall, F32), (stack, BF16), (square, BF16)],
        [next_basis, edge, lanes, kron_1, closing, absorbed],
        2**32,
    )
    received = exchanged(send, "row")
    (product,) = call(
        product_kernel,
        [(kron, F32)],
        [(stack, BF16)],
        [x_first, back, carried],
        2**31,
    )
    received, product = lax.optimization_barrier((received, product))
    gradient, left_new, right_new = call(
        place_kernel,
        [(sites.shape, F32), (tall, BF16), (tall, BF16)],
        [(sites.shape, F32)],
        [product, configuration, keep, received],
        2**30,
        copies=3,
        out_space=pltpu.HBM,
    )
    return (
        gradient.reshape(site_tensors.shape),
        left_new.reshape(left_bounds.shape),
        right_new.reshape(right_bounds.shape),
    )


def solution(mesh):
    return jax.shard_map(
        local,
        mesh=mesh,
        in_specs=(
            P(("grp", "row"), "col", None, None, None),
            P(("grp", "row"), "col", None, None, None),
            P(("grp", "row"), "col", None, None),
            P(("grp", "row"), "col"),
            P(("grp", "col"), None, None, None),
            P(("grp", "col"), None, None, None),
            P(),
        ),
        out_specs=(
            P(("grp", "row"), "col", None, None),
            P(("grp", "row"), "col", None, None, None),
            P(("grp", "row"), "col", None, None, None),
        ),
        check_vma=False,
    )
```

```python
import functools

import jax
import jax.numpy as jnp
from jax import lax
from jax.experimental import pallas as pl
from jax.experimental.pallas import tpu as pltpu
from jax.sharding import PartitionSpec as P

F32 = jnp.float32
BF16 = jnp.bfloat16
VMEM_BYTES = 24 * 1024 * 1024
PART = 4


def nn(a, b):
    return jnp.dot(a, b, preferred_element_type=F32)


def nt(a, b):
    return lax.dot_general(a, b, (((1,), (1,)), ((), ())), preferred_element_type=F32)


def split(x):
    high = x.astype(BF16)
    return high, (x - high.astype(F32)).astype(BF16)


def iota(shape, axis):
    return lax.broadcasted_iota(jnp.int32, shape, axis)


def chol_inverse(grams, near, beside=()):
    beside = list(beside)
    n = grams[0].shape[0]
    blocks = n // 8
    count = len(grams)
    lane = iota((8, n), 1)
    sub = iota((8, n), 0)
    at = [sub == j for j in range(8)]
    after = [sub > j for j in range(8)]
    tiles = [[g[8 * i : 8 * i + 8, :] for i in range(blocks)] for g in grams]

    def over_lanes(x, j):
        return jnp.broadcast_to(x[:, j : j + 1], (8, n))

    def over_rows(x, j):
        return jnp.broadcast_to(x[j : j + 1, :], (8, n))

    for b in range(blocks):
        own = (lane >= 8 * b) & (lane < 8 * b + 8)
        eye = jnp.where(lane - 8 * b == sub, 1.0, 0.0)
        by_element = range(b + 1, min(blocks, b + 1 + near))
        by_matmul = range(by_element.stop, blocks)
        diag = [[over_lanes(tiles[q][b], 8 * b + j) for j in range(8)] for q in range(count)]
        below = [
            [[over_lanes(tiles[q][i], 8 * b + j) for j in range(8)] for i in by_element]
            for q in range(count)
        ]
        forward = [jnp.where(own, eye, tiles[q][b]) for q in range(count)]
        full = list(forward)
        pivots = [jnp.ones((8, n), F32) for _ in range(count)]
        for step in beside[b * len(beside) // blocks : (b + 1) * len(beside) // blocks]:
            step()
        for j in range(8):
            for q in range(count):
                c = diag[q]
                pivot = over_rows(c[j], j)
                inverse = 1.0 / pivot
                pivots[q] = jnp.where(at[j], pivot, pivots[q])
                for k in range(j + 1, 8):
                    m = over_rows(c[k], j) * inverse
                    c[k] = jnp.where(at[j], m, c[k] - c[j] * m)
                row = over_rows(forward[q], j) * inverse
                forward[q] = jnp.where(after[j], forward[q] - c[j] * row, forward[q])
                full[q] = jnp.where(at[j], row, full[q] - c[j] * row)
        for q in range(count):
            rows = [over_rows(full[q], j) for j in range(8)]
            for i in by_element:
                terms = [below[q][i - b - 1][j] * rows[j] for j in range(8)]
                while len(terms) > 1:
                    terms = [x + y for x, y in zip(terms[::2], terms[1::2])]
                tiles[q][i] = jnp.where(own, 0.0, tiles[q][i]) - terms[0]
            if by_matmul:
                rest = jnp.concatenate([tiles[q][i] for i in by_matmul], axis=0)
                padded = [full[q], jnp.zeros((n - 8 * b - 8, n), F32)]
                if b:
                    padded = [jnp.zeros((8 * b, n), F32)] + padded
                update = jnp.dot(
                    rest,
                    jnp.concatenate(padded, axis=0),
                    precision=lax.Precision.HIGHEST,
                    preferred_element_type=F32,
                )
                for x, i in enumerate(by_matmul):
                    tiles[q][i] = jnp.where(own, 0.0, tiles[q][i]) - update[8 * x : 8 * x + 8]
            tiles[q][b] = jnp.where(lane <= sub + 8 * b, forward[q] * lax.rsqrt(pivots[q]), 0.0)
    return [jnp.concatenate(t, axis=0) for t in tiles]


def leg(scratch, j):
    chi = scratch.shape[1]
    return scratch[pl.ds(j, chi, stride=scratch.shape[0] // chi), :]


def weave(one, two, target, at):
    chi = one.shape[0]
    for g in range(0, chi, 2 * PART):
        rows = [block[k : k + PART, :] for k in (g, g + PART) for block in (one, two)]
        target[at + 2 * g : at + 2 * g + 4 * PART, :] = jnp.concatenate(rows, axis=0).astype(BF16)


def kron_step(lhs, rhs, x_ref, t, pair, transposed):
    chi = lhs.shape[1]
    bond = lhs.shape[0] // chi
    some = lhs[pair * 2 * chi : (pair + 1) * 2 * chi, :]
    if transposed:
        product = nt(some, rhs[t * chi : (t + 2) * chi, :])
    else:
        product = nn(some, rhs[:, t * chi : (t + 2) * chi])
    at = (pair * bond + t) * 2 * PART
    for g in range(chi // PART):
        rows = product[g * 2 * PART : (g + 1) * 2 * PART, :]
        x_ref[at : at + 4 * PART, g * chi : (g + 1) * chi] = jnp.concatenate(
            [rows[:, :chi], rows[:, chi:]], axis=0
        ).astype(BF16)


def absorb_step(kron, x_ref, m_ref, chi, g, first, count):
    bond = m_ref.shape[0] // chi
    step = bond * PART
    out = nn(kron[first * step : (first + count) * step, :], x_ref[:, g * chi : (g + 4) * chi])
    for o in range(count):
        for d in range(0, bond, 2):
            rows = out[(o * bond + d) * PART : (o * bond + d + 2) * PART, :]
            parts = [rows[:, k * chi : (k + 1) * chi] for k in range(4)]
            at = (first + o) * chi + g * PART
            for k in range(2):
                m_ref[at : at + 4 * PART, (d + k) * chi : (d + k + 1) * chi] = jnp.concatenate(
                    [part[k * PART : (k + 1) * PART, :] for part in parts], axis=0
                ).astype(BF16)


def kron_steps(lhs, rhs, x_ref, transposed=False):
    bond = lhs.shape[0] // lhs.shape[1]
    return [
        functools.partial(kron_step, lhs, rhs, x_ref, t, pair, transposed)
        for t in range(0, bond, 2)
        for pair in range(bond // 2)
    ]


def absorb_steps(kron, x_ref, m_ref, chi, count=4):
    bond = m_ref.shape[0] // chi
    return [
        functools.partial(absorb_step, kron, x_ref, m_ref, chi, g, first, count)
        for g in range(0, chi // PART, 4)
        for first in range(0, bond, count)
    ]


def square_core(row):
    row = row[...].astype(F32)
    size = round(row.shape[1] ** 0.5)
    flat = [row[:, i : i + 2 * size] for i in range(0, size * size, 2 * size)]
    flat = jnp.concatenate(flat, axis=0).astype(BF16)
    i = iota((size, size // 2), 0)
    j = iota((size, size // 2), 1)
    even = jnp.where(i == 2 * j, 1.0, 0.0).astype(BF16)
    odd = jnp.where(i == 2 * j + 1, 1.0, 0.0).astype(BF16)
    return (nn(even, flat[:, :size]) + nn(odd, flat[:, size:])).astype(BF16)


def swap_order(size, bond):
    i = iota((size, size), 0)
    j = iota((size, size), 1)
    hit = (i // bond == j % bond) & (i % bond == j // bond)
    return jnp.where(hit, 1.0, 0.0).astype(BF16)


def spread(size):
    i = iota((size * PART, size), 0)
    j = iota((size * PART, size), 1)
    return jnp.where(i // PART == j, 1.0, 0.0).astype(BF16)


def woven_pair(i, bond):
    i = i // PART
    s = (i // (2 * bond)) * 2 + i % 2
    t = (i // 4) % (bond // 2) * 2 + (i // 2) % 2
    return s, t


def kron_of(spread_rows, size):
    bond = round(size**0.5)
    s, t = woven_pair(iota((size * PART, size), 0), bond)
    spread_columns = jnp.where(s * bond + t == iota((size * PART, size), 1), 1.0, 0.0).astype(BF16)
    wide = nt(spread_rows.astype(BF16), spread_columns)
    i = iota(wide.shape, 0)
    j = iota(wide.shape, 1)
    return jnp.where(i % PART == j % PART, wide, 0.0).astype(BF16)


def spread_ahead(core, bond):
    size = core.shape[0]
    return nt(spread(size), nn(swap_order(size, bond), core).astype(BF16))


def spread_turned(core, bond):
    size = core.shape[0]
    return nn(spread(size), nt(swap_order(size, bond), core).astype(BF16))


def spread_back(core, bond):
    size = core.shape[0]
    return nn(spread(size), nn(core, swap_order(size, bond)).astype(BF16))


def mirrored(core, bond):
    size = core.shape[0]
    i = iota((size, size), 0)
    j = iota((size, size), 1)
    total = jnp.zeros((size, size), F32)
    for u in range(bond):
        pick = jnp.where(j == (i // bond) * bond + u, 1.0, 0.0).astype(BF16)
        picked = jnp.where(i % bond == j % bond, nn(pick, core), 0.0).astype(BF16)
        place = jnp.where(j == u * bond + i // bond, 1.0, 0.0).astype(BF16)
        total = total + nn(picked, place)
    return total.astype(BF16)


def edges_kernel(
    top_hbm,
    bottom_hbm,
    sketch_hbm,
    sites_hbm,
    choice,
    basis,
    basis_lanes,
    edge,
    first,
    sketch_t,
    site,
    kron_first,
    own_upper,
    own_lower,
    own_sketch,
    top,
    bottom,
    sketch,
    sites,
    wide,
    wide_sketch,
    legs_top,
    legs_bottom,
    sems,
):
    side = lax.axis_index("row")
    chi = top.shape[1]
    bond = top.shape[0] // chi
    copies = [
        pltpu.make_async_copy(source, target, sems.at[i])
        for i, (source, target) in enumerate(
            ((top_hbm, top), (bottom_hbm, bottom), (sketch_hbm, sketch), (sites_hbm, sites))
        )
    ]
    for copy in copies:
        copy.start()
    for env, legs, mine in ((top, legs_top, 0), (bottom, legs_bottom, 1)):
        copies[mine].wait()
        wide[...] = env[...].astype(F32)

        @pl.when(side == 0)
        def _():
            for u in range(0, bond, 2):
                pair = [leg(wide, u).T, leg(wide, u + 1).T]
                for k in range(2):
                    legs[:, (u + k) * chi : (u + k + 1) * chi] = pair[k].astype(BF16)
                if mine == 0:
                    weave(*pair, first, u * chi)

        @pl.when(side == 1)
        def _():
            for u in range(0, bond, 2):
                pair = [leg(wide, u), leg(wide, u + 1)]
                for k in range(2):
                    legs[:, (u + k) * chi : (u + k + 1) * chi] = pair[k].astype(BF16)
                if mine == 1:
                    weave(*pair, first, u * chi)

    copies[2].wait()
    wide_sketch[...] = sketch[...].astype(F32)

    def turn_sketch(o):
        weave(leg(wide_sketch, o).T, leg(wide_sketch, o + 1).T, sketch_t, o * chi)

    copies[3].wait()
    row = jnp.zeros((1, sites.shape[1]), F32)
    for p in range(sites.shape[0]):
        row = row + jnp.where(choice[0, 0] == p, sites[p : p + 1, :].astype(F32), 0.0)
    site[...] = row.astype(BF16)

    def build_kron():
        size = bond * bond
        core = square_core(site)
        swap = swap_order(size, bond)
        wide = spread(size)
        ahead = spread_ahead(core, bond)
        own_upper[...] = ahead.astype(BF16)
        own_lower[...] = nn(wide, nn(swap, core).astype(BF16)).astype(BF16)
        turned = nn(nn(swap, mirrored(core, bond)).astype(BF16), swap).astype(BF16)
        own_sketch[...] = nn(wide, turned).astype(BF16)
        kron_first[...] = kron_of(jnp.where(side == 0, ahead, spread_back(core, bond)), size)

    inverse_top, inverse_bottom = chol_inverse(
        [nt(legs_top[...], legs_top[...]), nt(legs_bottom[...], legs_bottom[...])],
        1,
        [functools.partial(turn_sketch, o) for o in range(0, bond, 2)] + [build_kron],
    )
    high, low = split(inverse_top)
    ortho = nn(high, legs_top[...]) + nn(low, legs_top[...])
    basis_lanes[...] = ortho.astype(BF16)
    blocks = [ortho[:, u * chi : (u + 1) * chi] for u in range(bond)]
    for u in range(0, bond, 2):
        weave(blocks[u], blocks[u + 1], basis, u * chi)
    high, low = split(inverse_bottom)
    ortho = (nn(high, legs_bottom[...]) + nn(low, legs_bottom[...])).astype(BF16)
    for d in range(bond):
        edge[d * chi : (d + 1) * chi, :] = ortho[:, d * chi : (d + 1) * chi]


def scaled(blocks, wide):
    chi = blocks[0].shape[0]
    bond = len(blocks)
    squares = jnp.zeros((1, chi), F32)
    for o, block in enumerate(blocks):
        wide[pl.ds(o, chi, stride=bond), :] = block
        squares = squares + jnp.sum(block * block, axis=0, keepdims=True)
    mean = jnp.sum(squares, axis=1, keepdims=True) * (1.0 / (chi * bond * chi))
    return (wide[...] * lax.rsqrt(mean + 1e-06)).astype(BF16)


def join_kernel(basis_lanes, sketch_t, x):
    for step in kron_steps(sketch_t, basis_lanes, x):
        step()


def prepare_kernel(
    x, site_other, own_upper, own_lower, own_sketch, kron_0, kron_1, sketched, kron_sketch
):
    is_left = lax.axis_index("row") == 0
    size = x.shape[0] // PART
    bond = round(size**0.5)
    chi = sketched.shape[0] // bond
    wide = spread(size)
    other = square_core(site_other)
    turned = spread_turned(other, bond)
    kron_sketch[...] = kron_of(jnp.where(is_left, own_sketch[...], turned.astype(BF16)), size)
    steps = absorb_steps(kron_sketch, x, sketched, chi)
    for step in steps[:6]:
        step()
    across = mirrored(other, bond)
    for step in steps[6:11]:
        step()
    upper = nn(wide, across).astype(BF16)
    kron_0[...] = kron_of(jnp.where(is_left, own_upper[...], upper), size)
    for step in steps[11:]:
        step()
    lower = nt(wide, across).astype(BF16)
    kron_1[...] = kron_of(jnp.where(is_left, lower, own_lower[...]), size)


def begin_kernel(
    first, western, eastern, kron, x_first, back, carried, wide_w, wide_e, ahead, behind, middle
):
    side = lax.axis_index("row")
    chi = first.shape[1]
    bond = first.shape[0] // chi
    wide_w[...] = western[...].astype(F32)
    wide_e[...] = eastern[...].astype(F32)

    def ready(ahead_of, behind_of, back_of):
        for j in range(0, bond, 2):
            for k in range(2):
                at = slice((j + k) * chi, (j + k + 1) * chi)
                ahead[:, at] = ahead_of(j + k).astype(BF16)
                behind[:, at] = behind_of(j + k).astype(BF16)
            weave(back_of(j), back_of(j + 1), back, j * chi)

    west = functools.partial(leg, wide_w)
    east = functools.partial(leg, wide_e)

    @pl.when(side == 0)
    def _():
        ready(west, lambda j: east(j).T, east)

    @pl.when(side == 1)
    def _():
        ready(lambda j: east(j).T, west, lambda j: west(j).T)

    for step in kron_steps(first, ahead, x_first) + absorb_steps(kron, x_first, middle, chi):
        step()
    state = nn(behind[...], middle[...]).astype(BF16)
    for s in range(bond):
        carried[s * chi : (s + 1) * chi, :] = state[:, s * chi : (s + 1) * chi]


def upper_kernel(
    basis,
    edge,
    sketched,
    western,
    eastern,
    western_other,
    eastern_other,
    kron_0,
    kron_1,
    closing,
    absorbed,
    closed,
    wide_0,
    wide_1,
    rows_0,
    lanes_0,
    woven_1,
    x,
    x_next,
):
    is_left = lax.axis_index("row") == 0
    chi = basis.shape[1]
    bond = basis.shape[0] // chi
    blocks = [slice(j * chi, (j + 1) * chi) for j in range(bond)]

    @pl.when(is_left)
    def _():
        wide_0[...] = western[...].astype(F32)

    @pl.when(jnp.logical_not(is_left))
    def _():
        wide_0[...] = eastern_other[...].astype(F32)

    for j in range(bond):
        rows_0[blocks[j], :] = leg(wide_0, j).astype(BF16)
    stacked = nn(sketched[...], rows_0[...])
    range_t = jnp.concatenate([stacked[blocks[d], :] for d in range(bond)], axis=1)
    high, low = split(range_t)
    gram = nt(high, high) + (nt(high, low) + nt(low, high))

    def ready_lanes():
        for j in range(bond):
            lanes_0[:, blocks[j]] = rows_0[blocks[j], :]

    def ready_other(part):
        step = wide_1.shape[0] // 4
        at = slice(part * step, (part + 1) * step)
        wide_1[at, :] = jnp.where(is_left, western_other[at, :], eastern[at, :]).astype(F32)

    def ready_woven(j):
        weave(leg(wide_1, j), leg(wide_1, j + 1), woven_1, j * chi)

    beside = (
        [ready_lanes]
        + kron_steps(basis, lanes_0, x)
        + [functools.partial(ready_other, part) for part in range(4)]
        + absorb_steps(kron_0, x, absorbed, chi)
        + [functools.partial(ready_woven, j) for j in range(0, bond, 2)]
        + kron_steps(woven_1, edge, x_next, True)
        + absorb_steps(kron_1, x_next, closed, chi)
    )
    (inverse,) = chol_inverse([gram], 3, beside)
    inverse_high, inverse_low = split(inverse)
    ortho = nn(inverse_high, high) + (nn(inverse_high, low) + nn(inverse_low, high))
    closing[...] = ortho.astype(BF16)


def lower_kernel(closing, absorbed, closed, keep, send, wide_0, wide_1):
    side = lax.axis_index("row")
    chi = closing.shape[0]
    bond = closing.shape[1] // chi
    blocks = [slice(j * chi, (j + 1) * chi) for j in range(bond)]
    upper = nt(absorbed[...], closing[...])
    new_0 = scaled([upper[at, :] for at in blocks], wide_0)
    lower = nn(closing[...], closed[...])
    new_1 = scaled([lower[:, at] for at in blocks], wide_1)

    @pl.when(side == 0)
    def _():
        keep[...] = new_0
        send[...] = new_1

    @pl.when(side == 1)
    def _():
        keep[...] = new_1
        send[...] = new_0


def product_kernel(x_first, back, carried, product, x_second):
    side = lax.axis_index("row")
    for step in kron_steps(back, carried, x_second, True):
        step()

    @pl.when(side == 0)
    def _():
        product[...] = nt(x_first[...], x_second[...])

    @pl.when(side == 1)
    def _():
        product[...] = nt(x_second[...], x_first[...])


def place_kernel(product, choice, keep, received, gradient, left, right, entries, sems):
    side = lax.axis_index("row")
    is_left = side == 0
    phys_count = gradient.shape[0]
    size = product.shape[0] // PART
    bond = round(size**0.5)
    chi = keep.shape[1]

    def start(one, other):
        pltpu.make_async_copy(one, left, sems.at[0]).start()
        pltpu.make_async_copy(other, right, sems.at[1]).start()

    pl.when(side == 0)(functools.partial(start, keep, received))
    pl.when(side == 1)(functools.partial(start, received, keep))

    def one_hot(i, j, swapped):
        s, t = woven_pair(i, bond)
        at = jnp.where(swapped, t * bond + s, s * bond + t)
        return jnp.where(j == at, 1.0, 0.0).astype(BF16)

    i = iota(product.shape, 0)
    j = iota(product.shape, 1)
    diagonal = jnp.where(i % PART == j % PART, product[...], 0.0).astype(BF16)
    wide = (size * PART, size * 2)
    half = jnp.zeros((size // 2, size * 2), F32)
    for odd in range(2):
        columns = one_hot(iota(wide, 0), iota(wide, 1) - odd * size, side == 1)
        rows = one_hot(iota(wide[::-1], 1), iota(wide[::-1], 0) * 2 + odd, is_left)[: size // 2]
        high, low = split(nn(diagonal, columns))
        half = half + (nn(rows, high) + nn(rows, low))
    half = half * (bond / chi)
    phys = iota((phys_count, size * 2), 0)
    for r in range(size // 2):
        row = jnp.broadcast_to(half[r : r + 1, :], phys.shape)
        entries[:, r * size * 2 : (r + 1) * size * 2] = jnp.where(phys == choice[0, 0], row, 0.0)
    copy = pltpu.make_async_copy(entries, gradient, sems.at[2])
    copy.start()
    pltpu.make_async_copy(keep, left, sems.at[0]).wait()
    pltpu.make_async_copy(keep, right, sems.at[1]).wait()
    copy.wait()


def call(kernel, out_shapes, scratch, inputs, flops, in_place=(), copies=0, out_space=pltpu.VMEM):
    inputs = [
        pltpu.with_memory_space_constraint(x, pltpu.HBM) if i in in_place else x
        for i, x in enumerate(inputs)
    ]
    vmem = pl.BlockSpec(memory_space=pltpu.VMEM)
    smem = pl.BlockSpec(memory_space=pltpu.SMEM)
    return pl.pallas_call(
        kernel,
        out_shape=[jax.ShapeDtypeStruct(s, t) for s, t in out_shapes],
        in_specs=[
            smem
            if x.shape == (1, 1)
            else pl.BlockSpec(memory_space=pltpu.HBM)
            if i in in_place
            else vmem
            for i, x in enumerate(inputs)
        ],
        out_specs=[pl.BlockSpec(memory_space=out_space) for _ in out_shapes],
        scratch_shapes=[pltpu.VMEM(s, t) for s, t in scratch]
        + ([pltpu.SemaphoreType.DMA((copies,))] if copies else []),
        compiler_params=pltpu.CompilerParams(vmem_limit_bytes=VMEM_BYTES),
        cost_estimate=pl.CostEstimate(flops=flops, bytes_accessed=2**21, transcendentals=0),
    )(*inputs)


def shifted(block, axis, steps):
    count = lax.axis_size(axis)
    return lax.ppermute(block, axis, [(i, (i + steps) % count) for i in range(count)])


def exchanged(block, axis):
    return lax.ppermute(block, axis, [(0, 1), (1, 0)])


def local(left_bounds, right_bounds, site_tensors, configuration, top_env, bottom_env, sketch):
    chi = left_bounds.shape[2]
    bond = left_bounds.shape[3]
    rows = chi * bond
    size = bond * bond
    tall = (rows, chi)
    flat = (chi, rows)
    kron = (size * PART, size * PART)
    stack = (size * PART, chi // PART * chi)
    square = (rows, rows)
    sites = site_tensors.reshape(site_tensors.shape[2:])
    western = shifted(left_bounds.reshape(tall), "col", 1)
    eastern = shifted(right_bounds.reshape(tall), "col", -1)
    basis, basis_lanes, edge, first, sketch_t, site, kron_first, *own = call(
        edges_kernel,
        [
            (tall, BF16),
            (flat, BF16),
            (tall, BF16),
            (tall, BF16),
            (tall, BF16),
            ((1, size * size), BF16),
            (kron, BF16),
        ]
        + [((size * PART, size), BF16)] * 3,
        [(tall, BF16)] * 3
        + [(sites.shape, BF16), (tall, F32), (tall, F32), (flat, BF16), (flat, BF16)],
        [top_env.reshape(tall), bottom_env.reshape(tall), sketch, sites, configuration],
        2**31,
        in_place=(0, 1, 2, 3),
        copies=4,
    )
    site_other = exchanged(site, "row")
    (joined,) = call(join_kernel, [(stack, BF16)], [], [basis_lanes, sketch_t], 2**30)
    site_other, joined = lax.optimization_barrier((site_other, joined))
    kron_0, kron_1, sketched = call(
        prepare_kernel,
        [(kron, BF16), (kron, BF16), (square, BF16)],
        [(kron, BF16)],
        [joined, site_other, *own],
        2**31,
    )
    sketched, western, eastern = lax.optimization_barrier((sketched, western, eastern))
    western_other = exchanged(western, "row")
    eastern_other = exchanged(eastern, "row")
    x_first, back, carried = call(
        begin_kernel,
        [(stack, BF16), (tall, BF16), (tall, BF16)],
        [(tall, F32), (tall, F32), (flat, BF16), (flat, BF16), (square, BF16)],
        [first, western, eastern, kron_first],
        2**32,
    )
    sketched, carried, western_other, eastern_other = lax.optimization_barrier(
        (sketched, carried, western_other, eastern_other)
    )
    carried = exchanged(carried, "row")
    closing, absorbed, closed = call(
        upper_kernel,
        [(flat, BF16), (square, BF16), (square, BF16)],
        [
            (tall, F32),
            (tall, F32),
            (tall, BF16),
            (flat, BF16),
            (tall, BF16),
            (stack, BF16),
            (stack, BF16),
        ],
        [
            basis,
            edge,
            sketched,
            western,
            eastern,
            western_other,
            eastern_other,
            kron_0,
            kron_1,
        ],
        2**33,
    )
    keep, send = call(
        lower_kernel,
        [(tall, BF16), (tall, BF16)],
        [(tall, F32), (tall, F32)],
        [closing, absorbed, closed],
        2**31,
    )
    received = exchanged(send, "row")
    (product,) = call(
        product_kernel,
        [(kron, F32)],
        [(stack, BF16)],
        [x_first, back, carried],
        2**31,
    )
    received, product = lax.optimization_barrier((received, product))
    gradient, left_new, right_new = call(
        place_kernel,
        [(sites.shape, F32), (tall, BF16), (tall, BF16)],
        [(sites.shape, F32)],
        [product, configuration, keep, received],
        2**30,
        copies=3,
        out_space=pltpu.HBM,
    )
    return (
        gradient.reshape(site_tensors.shape),
        left_new.reshape(left_bounds.shape),
        right_new.reshape(right_bounds.shape),
    )


def solution(mesh):
    return jax.shard_map(
        local,
        mesh=mesh,
        in_specs=(
            P(("grp", "row"), "col", None, None, None),
            P(("grp", "row"), "col", None, None, None),
            P(("grp", "row"), "col", None, None),
            P(("grp", "row"), "col"),
            P(("grp", "col"), None, None, None),
            P(("grp", "col"), None, None, None),
            P(),
        ),
        out_specs=(
            P(("grp", "row"), "col", None, None),
            P(("grp", "row"), "col", None, None, None),
            P(("grp", "row"), "col", None, None, None),
        ),
        check_vma=False,
    )
```

```python
import functools

import jax
import jax.numpy as jnp
from jax import lax
from jax.experimental import pallas as pl
from jax.experimental.pallas import tpu as pltpu
from jax.sharding import PartitionSpec as P

F32 = jnp.float32
BF16 = jnp.bfloat16
VMEM_BYTES = 24 * 1024 * 1024
PART = 4


def nn(a, b):
    return jnp.dot(a, b, preferred_element_type=F32)


def nt(a, b):
    return lax.dot_general(a, b, (((1,), (1,)), ((), ())), preferred_element_type=F32)


def split(x):
    high = x.astype(BF16)
    return high, (x - high.astype(F32)).astype(BF16)


def iota(shape, axis):
    return lax.broadcasted_iota(jnp.int32, shape, axis)


def chol_inverse(grams, near, beside=()):
    beside = list(beside)
    n = grams[0].shape[0]
    blocks = n // 8
    count = len(grams)
    lane = iota((8, n), 1)
    sub = iota((8, n), 0)
    at = [sub == j for j in range(8)]
    after = [sub > j for j in range(8)]
    tiles = [[g[8 * i : 8 * i + 8, :] for i in range(blocks)] for g in grams]

    def over_lanes(x, j):
        return jnp.broadcast_to(x[:, j : j + 1], (8, n))

    def over_rows(x, j):
        return jnp.broadcast_to(x[j : j + 1, :], (8, n))

    for b in range(blocks):
        own = (lane >= 8 * b) & (lane < 8 * b + 8)
        eye = jnp.where(lane - 8 * b == sub, 1.0, 0.0)
        by_element = range(b + 1, min(blocks, b + 1 + near))
        by_matmul = range(by_element.stop, blocks)
        diag = [[over_lanes(tiles[q][b], 8 * b + j) for j in range(8)] for q in range(count)]
        below = [
            [[over_lanes(tiles[q][i], 8 * b + j) for j in range(8)] for i in by_element]
            for q in range(count)
        ]
        forward = [jnp.where(own, eye, tiles[q][b]) for q in range(count)]
        full = list(forward)
        pivots = [jnp.ones((8, n), F32) for _ in range(count)]
        for step in beside[b * len(beside) // blocks : (b + 1) * len(beside) // blocks]:
            step()
        for j in range(8):
            for q in range(count):
                c = diag[q]
                pivot = over_rows(c[j], j)
                inverse = 1.0 / pivot
                pivots[q] = jnp.where(at[j], pivot, pivots[q])
                for k in range(j + 1, 8):
                    m = over_rows(c[k], j) * inverse
                    c[k] = jnp.where(at[j], m, c[k] - c[j] * m)
                row = over_rows(forward[q], j) * inverse
                forward[q] = jnp.where(after[j], forward[q] - c[j] * row, forward[q])
                full[q] = jnp.where(at[j], row, full[q] - c[j] * row)
        for q in range(count):
            rows = [over_rows(full[q], j) for j in range(8)]
            for i in by_element:
                terms = [below[q][i - b - 1][j] * rows[j] for j in range(8)]
                while len(terms) > 1:
                    terms = [x + y for x, y in zip(terms[::2], terms[1::2])]
                tiles[q][i] = jnp.where(own, 0.0, tiles[q][i]) - terms[0]
            if by_matmul:
                rest = jnp.concatenate([tiles[q][i] for i in by_matmul], axis=0)
                padded = [full[q], jnp.zeros((n - 8 * b - 8, n), F32)]
                if b:
                    padded = [jnp.zeros((8 * b, n), F32)] + padded
                update = jnp.dot(
                    rest,
                    jnp.concatenate(padded, axis=0),
                    precision=lax.Precision.HIGHEST,
                    preferred_element_type=F32,
                )
                for x, i in enumerate(by_matmul):
                    tiles[q][i] = jnp.where(own, 0.0, tiles[q][i]) - update[8 * x : 8 * x + 8]
            tiles[q][b] = jnp.where(lane <= sub + 8 * b, forward[q] * lax.rsqrt(pivots[q]), 0.0)
    return [jnp.concatenate(t, axis=0) for t in tiles]


def leg(scratch, j):
    chi = scratch.shape[1]
    return scratch[pl.ds(j, chi, stride=scratch.shape[0] // chi), :]


def weave(one, two, target, at):
    chi = one.shape[0]
    for g in range(0, chi, 2 * PART):
        rows = [block[k : k + PART, :] for k in (g, g + PART) for block in (one, two)]
        target[at + 2 * g : at + 2 * g + 4 * PART, :] = jnp.concatenate(rows, axis=0).astype(BF16)


def kron_step(lhs, rhs, x_ref, t, pair, transposed):
    chi = lhs.shape[1]
    bond = lhs.shape[0] // chi
    some = lhs[pair * 2 * chi : (pair + 1) * 2 * chi, :]
    if transposed:
        product = nt(some, rhs[t * chi : (t + 2) * chi, :])
    else:
        product = nn(some, rhs[:, t * chi : (t + 2) * chi])
    at = (pair * bond + t) * 2 * PART
    for g in range(chi // PART):
        rows = product[g * 2 * PART : (g + 1) * 2 * PART, :]
        x_ref[at : at + 4 * PART, g * chi : (g + 1) * chi] = jnp.concatenate(
            [rows[:, :chi], rows[:, chi:]], axis=0
        ).astype(BF16)


def absorb_step(kron, x_ref, m_ref, chi, g, first, count):
    bond = m_ref.shape[0] // chi
    step = bond * PART
    out = nn(kron[first * step : (first + count) * step, :], x_ref[:, g * chi : (g + 4) * chi])
    for o in range(count):
        for d in range(0, bond, 2):
            rows = out[(o * bond + d) * PART : (o * bond + d + 2) * PART, :]
            parts = [rows[:, k * chi : (k + 1) * chi] for k in range(4)]
            at = (first + o) * chi + g * PART
            for k in range(2):
                m_ref[at : at + 4 * PART, (d + k) * chi : (d + k + 1) * chi] = jnp.concatenate(
                    [part[k * PART : (k + 1) * PART, :] for part in parts], axis=0
                ).astype(BF16)


def kron_steps(lhs, rhs, x_ref, transposed=False):
    bond = lhs.shape[0] // lhs.shape[1]
    return [
        functools.partial(kron_step, lhs, rhs, x_ref, t, pair, transposed)
        for t in range(0, bond, 2)
        for pair in range(bond // 2)
    ]


def absorb_steps(kron, x_ref, m_ref, chi, count=4):
    bond = m_ref.shape[0] // chi
    return [
        functools.partial(absorb_step, kron, x_ref, m_ref, chi, g, first, count)
        for g in range(0, chi // PART, 4)
        for first in range(0, bond, count)
    ]


def square_core(row):
    row = row[...].astype(F32)
    size = round(row.shape[1] ** 0.5)
    flat = [row[:, i : i + 2 * size] for i in range(0, size * size, 2 * size)]
    flat = jnp.concatenate(flat, axis=0).astype(BF16)
    i = iota((size, size // 2), 0)
    j = iota((size, size // 2), 1)
    even = jnp.where(i == 2 * j, 1.0, 0.0).astype(BF16)
    odd = jnp.where(i == 2 * j + 1, 1.0, 0.0).astype(BF16)
    return (nn(even, flat[:, :size]) + nn(odd, flat[:, size:])).astype(BF16)


def swap_order(size, bond):
    i = iota((size, size), 0)
    j = iota((size, size), 1)
    hit = (i // bond == j % bond) & (i % bond == j // bond)
    return jnp.where(hit, 1.0, 0.0).astype(BF16)


def spread(size):
    i = iota((size * PART, size), 0)
    j = iota((size * PART, size), 1)
    return jnp.where(i // PART == j, 1.0, 0.0).astype(BF16)


def woven_pair(i, bond):
    i = i // PART
    s = (i // (2 * bond)) * 2 + i % 2
    t = (i // 4) % (bond // 2) * 2 + (i // 2) % 2
    return s, t


def kron_of(spread_rows, size):
    bond = round(size**0.5)
    s, t = woven_pair(iota((size * PART, size), 0), bond)
    spread_columns = jnp.where(s * bond + t == iota((size * PART, size), 1), 1.0, 0.0).astype(BF16)
    wide = nt(spread_rows.astype(BF16), spread_columns)
    i = iota(wide.shape, 0)
    j = iota(wide.shape, 1)
    return jnp.where(i % PART == j % PART, wide, 0.0).astype(BF16)


def spread_ahead(core, bond):
    size = core.shape[0]
    return nt(spread(size), nn(swap_order(size, bond), core).astype(BF16))


def spread_turned(core, bond):
    size = core.shape[0]
    return nn(spread(size), nt(swap_order(size, bond), core).astype(BF16))


def spread_back(core, bond):
    size = core.shape[0]
    return nn(spread(size), nn(core, swap_order(size, bond)).astype(BF16))


def mirrored(core, bond):
    size = core.shape[0]
    i = iota((size, size), 0)
    j = iota((size, size), 1)
    total = jnp.zeros((size, size), F32)
    for u in range(bond):
        pick = jnp.where(j == (i // bond) * bond + u, 1.0, 0.0).astype(BF16)
        picked = jnp.where(i % bond == j % bond, nn(pick, core), 0.0).astype(BF16)
        place = jnp.where(j == u * bond + i // bond, 1.0, 0.0).astype(BF16)
        total = total + nn(picked, place)
    return total.astype(BF16)


def edges_kernel(
    top_hbm,
    bottom_hbm,
    sketch_hbm,
    sites_hbm,
    choice,
    basis,
    basis_lanes,
    edge,
    first,
    sketch_t,
    site,
    kron_first,
    own_upper,
    own_lower,
    own_sketch,
    top,
    bottom,
    sketch,
    sites,
    wide,
    wide_sketch,
    legs_top,
    legs_bottom,
    sems,
):
    side = lax.axis_index("row")
    chi = top.shape[1]
    bond = top.shape[0] // chi
    copies = [
        pltpu.make_async_copy(source, target, sems.at[i])
        for i, (source, target) in enumerate(
            ((top_hbm, top), (bottom_hbm, bottom), (sketch_hbm, sketch), (sites_hbm, sites))
        )
    ]
    for copy in copies:
        copy.start()
    for env, legs, mine in ((top, legs_top, 0), (bottom, legs_bottom, 1)):
        copies[mine].wait()
        wide[...] = env[...].astype(F32)

        @pl.when(side == 0)
        def _():
            for u in range(0, bond, 2):
                pair = [leg(wide, u).T, leg(wide, u + 1).T]
                for k in range(2):
                    legs[:, (u + k) * chi : (u + k + 1) * chi] = pair[k].astype(BF16)
                if mine == 0:
                    weave(*pair, first, u * chi)

        @pl.when(side == 1)
        def _():
            for u in range(0, bond, 2):
                pair = [leg(wide, u), leg(wide, u + 1)]
                for k in range(2):
                    legs[:, (u + k) * chi : (u + k + 1) * chi] = pair[k].astype(BF16)
                if mine == 1:
                    weave(*pair, first, u * chi)

    copies[2].wait()
    wide_sketch[...] = sketch[...].astype(F32)

    def turn_sketch(o):
        weave(leg(wide_sketch, o).T, leg(wide_sketch, o + 1).T, sketch_t, o * chi)

    copies[3].wait()
    row = jnp.zeros((1, sites.shape[1]), F32)
    for p in range(sites.shape[0]):
        row = row + jnp.where(choice[0, 0] == p, sites[p : p + 1, :].astype(F32), 0.0)
    site[...] = row.astype(BF16)

    def build_kron():
        size = bond * bond
        core = square_core(site)
        swap = swap_order(size, bond)
        wide = spread(size)
        ahead = spread_ahead(core, bond)
        own_upper[...] = ahead.astype(BF16)
        own_lower[...] = nn(wide, nn(swap, core).astype(BF16)).astype(BF16)
        turned = nn(nn(swap, mirrored(core, bond)).astype(BF16), swap).astype(BF16)
        own_sketch[...] = nn(wide, turned).astype(BF16)
        kron_first[...] = kron_of(jnp.where(side == 0, ahead, spread_back(core, bond)), size)

    inverse_top, inverse_bottom = chol_inverse(
        [nt(legs_top[...], legs_top[...]), nt(legs_bottom[...], legs_bottom[...])],
        1,
        [functools.partial(turn_sketch, o) for o in range(0, bond, 2)] + [build_kron],
    )
    high, low = split(inverse_top)
    ortho = nn(high, legs_top[...]) + nn(low, legs_top[...])
    basis_lanes[...] = ortho.astype(BF16)
    blocks = [ortho[:, u * chi : (u + 1) * chi] for u in range(bond)]
    for u in range(0, bond, 2):
        weave(blocks[u], blocks[u + 1], basis, u * chi)
    high, low = split(inverse_bottom)
    ortho = (nn(high, legs_bottom[...]) + nn(low, legs_bottom[...])).astype(BF16)
    for d in range(bond):
        edge[d * chi : (d + 1) * chi, :] = ortho[:, d * chi : (d + 1) * chi]


def scaled(blocks, wide):
    chi = blocks[0].shape[0]
    bond = len(blocks)
    squares = jnp.zeros((1, chi), F32)
    for o, block in enumerate(blocks):
        wide[pl.ds(o, chi, stride=bond), :] = block
        squares = squares + jnp.sum(block * block, axis=0, keepdims=True)
    mean = jnp.sum(squares, axis=1, keepdims=True) * (1.0 / (chi * bond * chi))
    return (wide[...] * lax.rsqrt(mean + 1e-06)).astype(BF16)


def join_kernel(basis_lanes, sketch_t, x):
    for step in kron_steps(sketch_t, basis_lanes, x):
        step()


def prepare_kernel(
    x, site_other, own_upper, own_lower, own_sketch, kron_0, kron_1, sketched, kron_sketch
):
    is_left = lax.axis_index("row") == 0
    size = x.shape[0] // PART
    bond = round(size**0.5)
    chi = sketched.shape[0] // bond
    wide = spread(size)
    other = square_core(site_other)
    turned = spread_turned(other, bond)
    kron_sketch[...] = kron_of(jnp.where(is_left, own_sketch[...], turned.astype(BF16)), size)
    steps = absorb_steps(kron_sketch, x, sketched, chi)
    for step in steps[:6]:
        step()
    across = mirrored(other, bond)
    for step in steps[6:11]:
        step()
    upper = nn(wide, across).astype(BF16)
    kron_0[...] = kron_of(jnp.where(is_left, own_upper[...], upper), size)
    for step in steps[11:]:
        step()
    lower = nt(wide, across).astype(BF16)
    kron_1[...] = kron_of(jnp.where(is_left, lower, own_lower[...]), size)


def begin_kernel(
    first, western, eastern, kron, x_first, back, carried, wide_w, wide_e, ahead, behind, middle
):
    side = lax.axis_index("row")
    chi = first.shape[1]
    bond = first.shape[0] // chi
    wide_w[...] = western[...].astype(F32)
    wide_e[...] = eastern[...].astype(F32)

    def ready(ahead_of, behind_of, back_of):
        for j in range(0, bond, 2):
            for k in range(2):
                at = slice((j + k) * chi, (j + k + 1) * chi)
                ahead[:, at] = ahead_of(j + k).astype(BF16)
                behind[:, at] = behind_of(j + k).astype(BF16)
            weave(back_of(j), back_of(j + 1), back, j * chi)

    west = functools.partial(leg, wide_w)
    east = functools.partial(leg, wide_e)

    @pl.when(side == 0)
    def _():
        ready(west, lambda j: east(j).T, east)

    @pl.when(side == 1)
    def _():
        ready(lambda j: east(j).T, west, lambda j: west(j).T)

    for step in kron_steps(first, ahead, x_first) + absorb_steps(kron, x_first, middle, chi):
        step()
    state = nn(behind[...], middle[...]).astype(BF16)
    for s in range(bond):
        carried[s * chi : (s + 1) * chi, :] = state[:, s * chi : (s + 1) * chi]


def upper_kernel(
    basis,
    edge,
    sketched,
    western,
    eastern,
    western_other,
    eastern_other,
    kron_0,
    kron_1,
    closing,
    absorbed,
    closed,
    wide_0,
    wide_1,
    rows_0,
    lanes_0,
    woven_1,
    x,
    x_next,
):
    is_left = lax.axis_index("row") == 0
    chi = basis.shape[1]
    bond = basis.shape[0] // chi
    blocks = [slice(j * chi, (j + 1) * chi) for j in range(bond)]

    @pl.when(is_left)
    def _():
        wide_0[...] = western[...].astype(F32)

    @pl.when(jnp.logical_not(is_left))
    def _():
        wide_0[...] = eastern_other[...].astype(F32)

    for j in range(bond):
        rows_0[blocks[j], :] = leg(wide_0, j).astype(BF16)
    stacked = nn(sketched[...], rows_0[...])
    range_t = jnp.concatenate([stacked[blocks[d], :] for d in range(bond)], axis=1)
    high, low = split(range_t)
    gram = nt(high, high) + (nt(high, low) + nt(low, high))

    def ready_lanes():
        for j in range(bond):
            lanes_0[:, blocks[j]] = rows_0[blocks[j], :]

    def ready_other(part):
        step = wide_1.shape[0] // 4
        at = slice(part * step, (part + 1) * step)
        wide_1[at, :] = jnp.where(is_left, western_other[at, :], eastern[at, :]).astype(F32)

    def ready_woven(j):
        weave(leg(wide_1, j), leg(wide_1, j + 1), woven_1, j * chi)

    beside = (
        [ready_lanes]
        + kron_steps(basis, lanes_0, x)
        + [functools.partial(ready_other, part) for part in range(4)]
        + absorb_steps(kron_0, x, absorbed, chi)
        + [functools.partial(ready_woven, j) for j in range(0, bond, 2)]
        + kron_steps(woven_1, edge, x_next, True)
        + absorb_steps(kron_1, x_next, closed, chi)
    )
    (inverse,) = chol_inverse([gram], 2, beside)
    inverse_high, inverse_low = split(inverse)
    ortho = nn(inverse_high, high) + (nn(inverse_high, low) + nn(inverse_low, high))
    closing[...] = ortho.astype(BF16)


def lower_kernel(closing, absorbed, closed, keep, send, wide_0, wide_1):
    side = lax.axis_index("row")
    chi = closing.shape[0]
    bond = closing.shape[1] // chi
    blocks = [slice(j * chi, (j + 1) * chi) for j in range(bond)]
    upper = nt(absorbed[...], closing[...])
    new_0 = scaled([upper[at, :] for at in blocks], wide_0)
    lower = nn(closing[...], closed[...])
    new_1 = scaled([lower[:, at] for at in blocks], wide_1)

    @pl.when(side == 0)
    def _():
        keep[...] = new_0
        send[...] = new_1

    @pl.when(side == 1)
    def _():
        keep[...] = new_1
        send[...] = new_0


def product_kernel(x_first, back, carried, product, x_second):
    side = lax.axis_index("row")
    for step in kron_steps(back, carried, x_second, True):
        step()

    @pl.when(side == 0)
    def _():
        product[...] = nt(x_first[...], x_second[...])

    @pl.when(side == 1)
    def _():
        product[...] = nt(x_second[...], x_first[...])


def place_kernel(product, choice, keep, received, gradient, left, right, entries, sems):
    side = lax.axis_index("row")
    is_left = side == 0
    phys_count = gradient.shape[0]
    size = product.shape[0] // PART
    bond = round(size**0.5)
    chi = keep.shape[1]

    def start(one, other):
        pltpu.make_async_copy(one, left, sems.at[0]).start()
        pltpu.make_async_copy(other, right, sems.at[1]).start()

    pl.when(side == 0)(functools.partial(start, keep, received))
    pl.when(side == 1)(functools.partial(start, received, keep))

    def one_hot(i, j, swapped):
        s, t = woven_pair(i, bond)
        at = jnp.where(swapped, t * bond + s, s * bond + t)
        return jnp.where(j == at, 1.0, 0.0).astype(BF16)

    i = iota(product.shape, 0)
    j = iota(product.shape, 1)
    diagonal = jnp.where(i % PART == j % PART, product[...], 0.0).astype(BF16)
    wide = (size * PART, size * 2)
    half = jnp.zeros((size // 2, size * 2), F32)
    for odd in range(2):
        columns = one_hot(iota(wide, 0), iota(wide, 1) - odd * size, side == 1)
        rows = one_hot(iota(wide[::-1], 1), iota(wide[::-1], 0) * 2 + odd, is_left)[: size // 2]
        high, low = split(nn(diagonal, columns))
        half = half + (nn(rows, high) + nn(rows, low))
    half = half * (bond / chi)
    phys = iota((phys_count, size * 2), 0)
    for r in range(size // 2):
        row = jnp.broadcast_to(half[r : r + 1, :], phys.shape)
        entries[:, r * size * 2 : (r + 1) * size * 2] = jnp.where(phys == choice[0, 0], row, 0.0)
    copy = pltpu.make_async_copy(entries, gradient, sems.at[2])
    copy.start()
    pltpu.make_async_copy(keep, left, sems.at[0]).wait()
    pltpu.make_async_copy(keep, right, sems.at[1]).wait()
    copy.wait()


def call(kernel, out_shapes, scratch, inputs, flops, in_place=(), copies=0, out_space=pltpu.VMEM):
    inputs = [
        pltpu.with_memory_space_constraint(x, pltpu.HBM) if i in in_place else x
        for i, x in enumerate(inputs)
    ]
    vmem = pl.BlockSpec(memory_space=pltpu.VMEM)
    smem = pl.BlockSpec(memory_space=pltpu.SMEM)
    return pl.pallas_call(
        kernel,
        out_shape=[jax.ShapeDtypeStruct(s, t) for s, t in out_shapes],
        in_specs=[
            smem
            if x.shape == (1, 1)
            else pl.BlockSpec(memory_space=pltpu.HBM)
            if i in in_place
            else vmem
            for i, x in enumerate(inputs)
        ],
        out_specs=[pl.BlockSpec(memory_space=out_space) for _ in out_shapes],
        scratch_shapes=[pltpu.VMEM(s, t) for s, t in scratch]
        + ([pltpu.SemaphoreType.DMA((copies,))] if copies else []),
        compiler_params=pltpu.CompilerParams(vmem_limit_bytes=VMEM_BYTES),
        cost_estimate=pl.CostEstimate(flops=flops, bytes_accessed=2**21, transcendentals=0),
    )(*inputs)


def shifted(block, axis, steps):
    count = lax.axis_size(axis)
    return lax.ppermute(block, axis, [(i, (i + steps) % count) for i in range(count)])


def exchanged(block, axis):
    return lax.ppermute(block, axis, [(0, 1), (1, 0)])


def local(left_bounds, right_bounds, site_tensors, configuration, top_env, bottom_env, sketch):
    chi = left_bounds.shape[2]
    bond = left_bounds.shape[3]
    rows = chi * bond
    size = bond * bond
    tall = (rows, chi)
    flat = (chi, rows)
    kron = (size * PART, size * PART)
    stack = (size * PART, chi // PART * chi)
    square = (rows, rows)
    sites = site_tensors.reshape(site_tensors.shape[2:])
    western = shifted(left_bounds.reshape(tall), "col", 1)
    eastern = shifted(right_bounds.reshape(tall), "col", -1)
    basis, basis_lanes, edge, first, sketch_t, site, kron_first, *own = call(
        edges_kernel,
        [
            (tall, BF16),
            (flat, BF16),
            (tall, BF16),
            (tall, BF16),
            (tall, BF16),
            ((1, size * size), BF16),
            (kron, BF16),
        ]
        + [((size * PART, size), BF16)] * 3,
        [(tall, BF16)] * 3
        + [(sites.shape, BF16), (tall, F32), (tall, F32), (flat, BF16), (flat, BF16)],
        [top_env.reshape(tall), bottom_env.reshape(tall), sketch, sites, configuration],
        2**31,
        in_place=(0, 1, 2, 3),
        copies=4,
    )
    site_other = exchanged(site, "row")
    (joined,) = call(join_kernel, [(stack, BF16)], [], [basis_lanes, sketch_t], 2**30)
    site_other, joined = lax.optimization_barrier((site_other, joined))
    kron_0, kron_1, sketched = call(
        prepare_kernel,
        [(kron, BF16), (kron, BF16), (square, BF16)],
        [(kron, BF16)],
        [joined, site_other, *own],
        2**31,
    )
    sketched, western, eastern = lax.optimization_barrier((sketched, western, eastern))
    western_other = exchanged(western, "row")
    eastern_other = exchanged(eastern, "row")
    x_first, back, carried = call(
        begin_kernel,
        [(stack, BF16), (tall, BF16), (tall, BF16)],
        [(tall, F32), (tall, F32), (flat, BF16), (flat, BF16), (square, BF16)],
        [first, western, eastern, kron_first],
        2**32,
    )
    sketched, carried, western_other, eastern_other = lax.optimization_barrier(
        (sketched, carried, western_other, eastern_other)
    )
    carried = exchanged(carried, "row")
    closing, absorbed, closed = call(
        upper_kernel,
        [(flat, BF16), (square, BF16), (square, BF16)],
        [
            (tall, F32),
            (tall, F32),
            (tall, BF16),
            (flat, BF16),
            (tall, BF16),
            (stack, BF16),
            (stack, BF16),
        ],
        [
            basis,
            edge,
            sketched,
            western,
            eastern,
            western_other,
            eastern_other,
            kron_0,
            kron_1,
        ],
        2**33,
    )
    keep, send = call(
        lower_kernel,
        [(tall, BF16), (tall, BF16)],
        [(tall, F32), (tall, F32)],
        [closing, absorbed, closed],
        2**31,
    )
    received = exchanged(send, "row")
    (product,) = call(
        product_kernel,
        [(kron, F32)],
        [(stack, BF16)],
        [x_first, back, carried],
        2**31,
    )
    received, product = lax.optimization_barrier((received, product))
    gradient, left_new, right_new = call(
        place_kernel,
        [(sites.shape, F32), (tall, BF16), (tall, BF16)],
        [(sites.shape, F32)],
        [product, configuration, keep, received],
        2**30,
        copies=3,
        out_space=pltpu.HBM,
    )
    return (
        gradient.reshape(site_tensors.shape),
        left_new.reshape(left_bounds.shape),
        right_new.reshape(right_bounds.shape),
    )


def solution(mesh):
    return jax.shard_map(
        local,
        mesh=mesh,
        in_specs=(
            P(("grp", "row"), "col", None, None, None),
            P(("grp", "row"), "col", None, None, None),
            P(("grp", "row"), "col", None, None),
            P(("grp", "row"), "col"),
            P(("grp", "col"), None, None, None),
            P(("grp", "col"), None, None, None),
            P(),
        ),
        out_specs=(
            P(("grp", "row"), "col", None, None),
            P(("grp", "row"), "col", None, None, None),
            P(("grp", "row"), "col", None, None, None),
        ),
        check_vma=False,
    )
```

```python
import functools

import jax
import jax.numpy as jnp
from jax import lax
from jax.experimental import pallas as pl
from jax.experimental.pallas import tpu as pltpu
from jax.sharding import PartitionSpec as P

F32 = jnp.float32
BF16 = jnp.bfloat16
VMEM_BYTES = 24 * 1024 * 1024
PART = 4


def nn(a, b):
    return jnp.dot(a, b, preferred_element_type=F32)


def nt(a, b):
    return lax.dot_general(a, b, (((1,), (1,)), ((), ())), preferred_element_type=F32)


def split(x):
    high = x.astype(BF16)
    return high, (x - high.astype(F32)).astype(BF16)


def iota(shape, axis):
    return lax.broadcasted_iota(jnp.int32, shape, axis)


def chol_inverse(grams, near, beside=()):
    beside = list(beside)
    n = grams[0].shape[0]
    blocks = n // 8
    count = len(grams)
    lane = iota((8, n), 1)
    sub = iota((8, n), 0)
    at = [sub == j for j in range(8)]
    after = [sub > j for j in range(8)]
    tiles = [[g[8 * i : 8 * i + 8, :] for i in range(blocks)] for g in grams]

    def over_lanes(x, j):
        return jnp.broadcast_to(x[:, j : j + 1], (8, n))

    def over_rows(x, j):
        return jnp.broadcast_to(x[j : j + 1, :], (8, n))

    for b in range(blocks):
        own = (lane >= 8 * b) & (lane < 8 * b + 8)
        eye = jnp.where(lane - 8 * b == sub, 1.0, 0.0)
        by_element = range(b + 1, min(blocks, b + 1 + near))
        by_matmul = range(by_element.stop, blocks)
        diag = [[over_lanes(tiles[q][b], 8 * b + j) for j in range(8)] for q in range(count)]
        below = [
            [[over_lanes(tiles[q][i], 8 * b + j) for j in range(8)] for i in by_element]
            for q in range(count)
        ]
        forward = [jnp.where(own, eye, tiles[q][b]) for q in range(count)]
        full = list(forward)
        pivots = [jnp.ones((8, n), F32) for _ in range(count)]
        for step in beside[b * len(beside) // blocks : (b + 1) * len(beside) // blocks]:
            step()
        for j in range(8):
            for q in range(count):
                c = diag[q]
                pivot = over_rows(c[j], j)
                inverse = 1.0 / pivot
                pivots[q] = jnp.where(at[j], pivot, pivots[q])
                for k in range(j + 1, 8):
                    m = over_rows(c[k], j) * inverse
                    c[k] = jnp.where(at[j], m, c[k] - c[j] * m)
                row = over_rows(forward[q], j) * inverse
                forward[q] = jnp.where(after[j], forward[q] - c[j] * row, forward[q])
                full[q] = jnp.where(at[j], row, full[q] - c[j] * row)
        for q in range(count):
            rows = [over_rows(full[q], j) for j in range(8)]
            for i in by_element:
                terms = [below[q][i - b - 1][j] * rows[j] for j in range(8)]
                while len(terms) > 1:
                    terms = [x + y for x, y in zip(terms[::2], terms[1::2])]
                tiles[q][i] = jnp.where(own, 0.0, tiles[q][i]) - terms[0]
            if by_matmul:
                rest = jnp.concatenate([tiles[q][i] for i in by_matmul], axis=0)
                padded = [full[q], jnp.zeros((n - 8 * b - 8, n), F32)]
                if b:
                    padded = [jnp.zeros((8 * b, n), F32)] + padded
                update = jnp.dot(
                    rest,
                    jnp.concatenate(padded, axis=0),
                    precision=lax.Precision.HIGHEST,
                    preferred_element_type=F32,
                )
                for x, i in enumerate(by_matmul):
                    tiles[q][i] = jnp.where(own, 0.0, tiles[q][i]) - update[8 * x : 8 * x + 8]
            tiles[q][b] = jnp.where(lane <= sub + 8 * b, forward[q] * lax.rsqrt(pivots[q]), 0.0)
    return [jnp.concatenate(t, axis=0) for t in tiles]


def leg(scratch, j):
    chi = scratch.shape[1]
    return scratch[pl.ds(j, chi, stride=scratch.shape[0] // chi), :]


def weave(one, two, target, at):
    chi = one.shape[0]
    for g in range(0, chi, 2 * PART):
        rows = [block[k : k + PART, :] for k in (g, g + PART) for block in (one, two)]
        target[at + 2 * g : at + 2 * g + 4 * PART, :] = jnp.concatenate(rows, axis=0).astype(BF16)


def kron_step(lhs, rhs, x_ref, t, pair, transposed):
    chi = lhs.shape[1]
    bond = lhs.shape[0] // chi
    some = lhs[pair * 2 * chi : (pair + 1) * 2 * chi, :]
    if transposed:
        product = nt(some, rhs[t * chi : (t + 2) * chi, :])
    else:
        product = nn(some, rhs[:, t * chi : (t + 2) * chi])
    at = (pair * bond + t) * 2 * PART
    for g in range(chi // PART):
        rows = product[g * 2 * PART : (g + 1) * 2 * PART, :]
        x_ref[at : at + 4 * PART, g * chi : (g + 1) * chi] = jnp.concatenate(
            [rows[:, :chi], rows[:, chi:]], axis=0
        ).astype(BF16)


def absorb_step(kron, x_ref, m_ref, chi, g, first, count):
    bond = m_ref.shape[0] // chi
    step = bond * PART
    out = nn(kron[first * step : (first + count) * step, :], x_ref[:, g * chi : (g + 4) * chi])
    for o in range(count):
        for d in range(0, bond, 2):
            rows = out[(o * bond + d) * PART : (o * bond + d + 2) * PART, :]
            parts = [rows[:, k * chi : (k + 1) * chi] for k in range(4)]
            at = (first + o) * chi + g * PART
            for k in range(2):
                m_ref[at : at + 4 * PART, (d + k) * chi : (d + k + 1) * chi] = jnp.concatenate(
                    [part[k * PART : (k + 1) * PART, :] for part in parts], axis=0
                ).astype(BF16)


def kron_steps(lhs, rhs, x_ref, transposed=False):
    bond = lhs.shape[0] // lhs.shape[1]
    return [
        functools.partial(kron_step, lhs, rhs, x_ref, t, pair, transposed)
        for t in range(0, bond, 2)
        for pair in range(bond // 2)
    ]


def absorb_steps(kron, x_ref, m_ref, chi, count=4):
    bond = m_ref.shape[0] // chi
    return [
        functools.partial(absorb_step, kron, x_ref, m_ref, chi, g, first, count)
        for g in range(0, chi // PART, 4)
        for first in range(0, bond, count)
    ]


def square_core(row):
    row = row[...].astype(F32)
    size = round(row.shape[1] ** 0.5)
    flat = [row[:, i : i + 2 * size] for i in range(0, size * size, 2 * size)]
    flat = jnp.concatenate(flat, axis=0).astype(BF16)
    i = iota((size, size // 2), 0)
    j = iota((size, size // 2), 1)
    even = jnp.where(i == 2 * j, 1.0, 0.0).astype(BF16)
    odd = jnp.where(i == 2 * j + 1, 1.0, 0.0).astype(BF16)
    return (nn(even, flat[:, :size]) + nn(odd, flat[:, size:])).astype(BF16)


def swap_order(size, bond):
    i = iota((size, size), 0)
    j = iota((size, size), 1)
    hit = (i // bond == j % bond) & (i % bond == j // bond)
    return jnp.where(hit, 1.0, 0.0).astype(BF16)


def spread(size):
    i = iota((size * PART, size), 0)
    j = iota((size * PART, size), 1)
    return jnp.where(i // PART == j, 1.0, 0.0).astype(BF16)


def woven_pair(i, bond):
    i = i // PART
    s = (i // (2 * bond)) * 2 + i % 2
    t = (i // 4) % (bond // 2) * 2 + (i // 2) % 2
    return s, t


def kron_of(spread_rows, size):
    bond = round(size**0.5)
    s, t = woven_pair(iota((size * PART, size), 0), bond)
    spread_columns = jnp.where(s * bond + t == iota((size * PART, size), 1), 1.0, 0.0).astype(BF16)
    wide = nt(spread_rows.astype(BF16), spread_columns)
    i = iota(wide.shape, 0)
    j = iota(wide.shape, 1)
    return jnp.where(i % PART == j % PART, wide, 0.0).astype(BF16)


def spread_ahead(core, bond):
    size = core.shape[0]
    return nt(spread(size), nn(swap_order(size, bond), core).astype(BF16))


def spread_turned(core, bond):
    size = core.shape[0]
    return nn(spread(size), nt(swap_order(size, bond), core).astype(BF16))


def spread_back(core, bond):
    size = core.shape[0]
    return nn(spread(size), nn(core, swap_order(size, bond)).astype(BF16))


def mirrored(core, bond):
    size = core.shape[0]
    i = iota((size, size), 0)
    j = iota((size, size), 1)
    total = jnp.zeros((size, size), F32)
    for u in range(bond):
        pick = jnp.where(j == (i // bond) * bond + u, 1.0, 0.0).astype(BF16)
        picked = jnp.where(i % bond == j % bond, nn(pick, core), 0.0).astype(BF16)
        place = jnp.where(j == u * bond + i // bond, 1.0, 0.0).astype(BF16)
        total = total + nn(picked, place)
    return total.astype(BF16)


def edges_kernel(
    top_hbm,
    bottom_hbm,
    sketch_hbm,
    sites_hbm,
    choice,
    basis,
    basis_lanes,
    edge,
    first,
    sketch_t,
    site,
    kron_first,
    own_upper,
    own_lower,
    own_sketch,
    top,
    bottom,
    sketch,
    sites,
    wide,
    wide_sketch,
    legs_top,
    legs_bottom,
    sems,
):
    side = lax.axis_index("row")
    chi = top.shape[1]
    bond = top.shape[0] // chi
    copies = [
        pltpu.make_async_copy(source, target, sems.at[i])
        for i, (source, target) in enumerate(
            ((top_hbm, top), (bottom_hbm, bottom), (sketch_hbm, sketch), (sites_hbm, sites))
        )
    ]
    for copy in copies:
        copy.start()
    for env, legs, mine in ((top, legs_top, 0), (bottom, legs_bottom, 1)):
        copies[mine].wait()
        wide[...] = env[...].astype(F32)

        @pl.when(side == 0)
        def _():
            for u in range(0, bond, 2):
                pair = [leg(wide, u).T, leg(wide, u + 1).T]
                for k in range(2):
                    legs[:, (u + k) * chi : (u + k + 1) * chi] = pair[k].astype(BF16)
                if mine == 0:
                    weave(*pair, first, u * chi)

        @pl.when(side == 1)
        def _():
            for u in range(0, bond, 2):
                pair = [leg(wide, u), leg(wide, u + 1)]
                for k in range(2):
                    legs[:, (u + k) * chi : (u + k + 1) * chi] = pair[k].astype(BF16)
                if mine == 1:
                    weave(*pair, first, u * chi)

    copies[2].wait()
    wide_sketch[...] = sketch[...].astype(F32)

    def turn_sketch(o):
        weave(leg(wide_sketch, o).T, leg(wide_sketch, o + 1).T, sketch_t, o * chi)

    copies[3].wait()
    row = jnp.zeros((1, sites.shape[1]), F32)
    for p in range(sites.shape[0]):
        row = row + jnp.where(choice[0, 0] == p, sites[p : p + 1, :].astype(F32), 0.0)
    site[...] = row.astype(BF16)

    def build_kron():
        size = bond * bond
        core = square_core(site)
        swap = swap_order(size, bond)
        wide = spread(size)
        ahead = spread_ahead(core, bond)
        own_upper[...] = ahead.astype(BF16)
        own_lower[...] = nn(wide, nn(swap, core).astype(BF16)).astype(BF16)
        turned = nn(nn(swap, mirrored(core, bond)).astype(BF16), swap).astype(BF16)
        own_sketch[...] = nn(wide, turned).astype(BF16)
        kron_first[...] = kron_of(jnp.where(side == 0, ahead, spread_back(core, bond)), size)

    inverse_top, inverse_bottom = chol_inverse(
        [nt(legs_top[...], legs_top[...]), nt(legs_bottom[...], legs_bottom[...])],
        1,
        [functools.partial(turn_sketch, o) for o in range(0, bond, 2)] + [build_kron],
    )
    high, low = split(inverse_top)
    ortho = nn(high, legs_top[...]) + nn(low, legs_top[...])
    basis_lanes[...] = ortho.astype(BF16)
    blocks = [ortho[:, u * chi : (u + 1) * chi] for u in range(bond)]
    for u in range(0, bond, 2):
        weave(blocks[u], blocks[u + 1], basis, u * chi)
    high, low = split(inverse_bottom)
    ortho = (nn(high, legs_bottom[...]) + nn(low, legs_bottom[...])).astype(BF16)
    for d in range(bond):
        edge[d * chi : (d + 1) * chi, :] = ortho[:, d * chi : (d + 1) * chi]


def scaled(blocks, wide):
    chi = blocks[0].shape[0]
    bond = len(blocks)
    squares = jnp.zeros((1, chi), F32)
    for o, block in enumerate(blocks):
        wide[pl.ds(o, chi, stride=bond), :] = block
        squares = squares + jnp.sum(block * block, axis=0, keepdims=True)
    mean = jnp.sum(squares, axis=1, keepdims=True) * (1.0 / (chi * bond * chi))
    return (wide[...] * lax.rsqrt(mean + 1e-06)).astype(BF16)


def join_kernel(basis_lanes, sketch_t, x):
    for step in kron_steps(sketch_t, basis_lanes, x):
        step()


def prepare_kernel(
    x, site_other, own_upper, own_lower, own_sketch, kron_0, kron_1, sketched, kron_sketch
):
    is_left = lax.axis_index("row") == 0
    size = x.shape[0] // PART
    bond = round(size**0.5)
    chi = sketched.shape[0] // bond
    wide = spread(size)
    other = square_core(site_other)
    turned = spread_turned(other, bond)
    kron_sketch[...] = kron_of(jnp.where(is_left, own_sketch[...], turned.astype(BF16)), size)
    steps = absorb_steps(kron_sketch, x, sketched, chi)
    for step in steps[:6]:
        step()
    across = mirrored(other, bond)
    for step in steps[6:11]:
        step()
    upper = nn(wide, across).astype(BF16)
    kron_0[...] = kron_of(jnp.where(is_left, own_upper[...], upper), size)
    for step in steps[11:]:
        step()
    lower = nt(wide, across).astype(BF16)
    kron_1[...] = kron_of(jnp.where(is_left, lower, own_lower[...]), size)


def begin_kernel(
    first, western, eastern, kron, x_first, back, carried, wide_w, wide_e, ahead, behind, middle
):
    side = lax.axis_index("row")
    chi = first.shape[1]
    bond = first.shape[0] // chi
    wide_w[...] = western[...].astype(F32)
    wide_e[...] = eastern[...].astype(F32)

    def ready(ahead_of, behind_of, back_of):
        for j in range(0, bond, 2):
            for k in range(2):
                at = slice((j + k) * chi, (j + k + 1) * chi)
                ahead[:, at] = ahead_of(j + k).astype(BF16)
                behind[:, at] = behind_of(j + k).astype(BF16)
            weave(back_of(j), back_of(j + 1), back, j * chi)

    west = functools.partial(leg, wide_w)
    east = functools.partial(leg, wide_e)

    @pl.when(side == 0)
    def _():
        ready(west, lambda j: east(j).T, east)

    @pl.when(side == 1)
    def _():
        ready(lambda j: east(j).T, west, lambda j: west(j).T)

    for step in kron_steps(first, ahead, x_first) + absorb_steps(kron, x_first, middle, chi):
        step()
    state = nn(behind[...], middle[...]).astype(BF16)
    for s in range(bond):
        carried[s * chi : (s + 1) * chi, :] = state[:, s * chi : (s + 1) * chi]


def rows_kernel(
    basis,
    edge,
    sketched,
    western,
    eastern,
    western_other,
    eastern_other,
    kron_0,
    kron_1,
    keep,
    send,
    absorbed,
    closed,
    wide_0,
    wide_1,
    rows_0,
    lanes_0,
    woven_1,
    x,
    x_next,
):
    is_left = lax.axis_index("row") == 0
    chi = basis.shape[1]
    bond = basis.shape[0] // chi
    blocks = [slice(j * chi, (j + 1) * chi) for j in range(bond)]

    @pl.when(is_left)
    def _():
        wide_0[...] = western[...].astype(F32)

    @pl.when(jnp.logical_not(is_left))
    def _():
        wide_0[...] = eastern_other[...].astype(F32)

    for j in range(bond):
        rows_0[blocks[j], :] = leg(wide_0, j).astype(BF16)
    stacked = nn(sketched[...], rows_0[...])
    range_t = jnp.concatenate([stacked[blocks[d], :] for d in range(bond)], axis=1)
    high, low = split(range_t)
    gram = nt(high, high) + (nt(high, low) + nt(low, high))

    def ready_lanes():
        for j in range(bond):
            lanes_0[:, blocks[j]] = rows_0[blocks[j], :]

    def ready_other(part):
        step = wide_1.shape[0] // 4
        at = slice(part * step, (part + 1) * step)
        wide_1[at, :] = jnp.where(is_left, western_other[at, :], eastern[at, :]).astype(F32)

    def ready_woven(j):
        weave(leg(wide_1, j), leg(wide_1, j + 1), woven_1, j * chi)

    beside = (
        [ready_lanes]
        + kron_steps(basis, lanes_0, x)
        + [functools.partial(ready_other, part) for part in range(4)]
        + absorb_steps(kron_0, x, absorbed, chi)
        + [functools.partial(ready_woven, j) for j in range(0, bond, 2)]
        + kron_steps(woven_1, edge, x_next, True)
        + absorb_steps(kron_1, x_next, closed, chi)
    )
    (inverse,) = chol_inverse([gram], 2, beside)
    inverse_high, inverse_low = split(inverse)
    ortho = nn(inverse_high, high) + (nn(inverse_high, low) + nn(inverse_low, high))
    closing = ortho.astype(BF16)
    upper = nt(absorbed[...], closing)
    lower = nn(closing, closed[...])
    new_0 = scaled([upper[at, :] for at in blocks], wide_0)
    new_1 = scaled([lower[:, at] for at in blocks], wide_1)

    @pl.when(is_left)
    def _():
        keep[...] = new_0
        send[...] = new_1

    @pl.when(jnp.logical_not(is_left))
    def _():
        keep[...] = new_1
        send[...] = new_0


def product_kernel(x_first, back, carried, product, x_second):
    side = lax.axis_index("row")
    for step in kron_steps(back, carried, x_second, True):
        step()

    @pl.when(side == 0)
    def _():
        product[...] = nt(x_first[...], x_second[...])

    @pl.when(side == 1)
    def _():
        product[...] = nt(x_second[...], x_first[...])


def place_kernel(product, choice, keep, received, gradient, left, right, entries, sems):
    side = lax.axis_index("row")
    is_left = side == 0
    phys_count = gradient.shape[0]
    size = product.shape[0] // PART
    bond = round(size**0.5)
    chi = keep.shape[1]

    def start(one, other):
        pltpu.make_async_copy(one, left, sems.at[0]).start()
        pltpu.make_async_copy(other, right, sems.at[1]).start()

    pl.when(side == 0)(functools.partial(start, keep, received))
    pl.when(side == 1)(functools.partial(start, received, keep))

    def one_hot(i, j, swapped):
        s, t = woven_pair(i, bond)
        at = jnp.where(swapped, t * bond + s, s * bond + t)
        return jnp.where(j == at, 1.0, 0.0).astype(BF16)

    i = iota(product.shape, 0)
    j = iota(product.shape, 1)
    diagonal = jnp.where(i % PART == j % PART, product[...], 0.0).astype(BF16)
    wide = (size * PART, size * 2)
    half = jnp.zeros((size // 2, size * 2), F32)
    for odd in range(2):
        columns = one_hot(iota(wide, 0), iota(wide, 1) - odd * size, side == 1)
        rows = one_hot(iota(wide[::-1], 1), iota(wide[::-1], 0) * 2 + odd, is_left)[: size // 2]
        high, low = split(nn(diagonal, columns))
        half = half + (nn(rows, high) + nn(rows, low))
    half = half * (bond / chi)
    phys = iota((phys_count, size * 2), 0)
    for r in range(size // 2):
        row = jnp.broadcast_to(half[r : r + 1, :], phys.shape)
        entries[:, r * size * 2 : (r + 1) * size * 2] = jnp.where(phys == choice[0, 0], row, 0.0)
    copy = pltpu.make_async_copy(entries, gradient, sems.at[2])
    copy.start()
    pltpu.make_async_copy(keep, left, sems.at[0]).wait()
    pltpu.make_async_copy(keep, right, sems.at[1]).wait()
    copy.wait()


def call(kernel, out_shapes, scratch, inputs, flops, in_place=(), copies=0, out_space=pltpu.VMEM):
    inputs = [
        pltpu.with_memory_space_constraint(x, pltpu.HBM) if i in in_place else x
        for i, x in enumerate(inputs)
    ]
    vmem = pl.BlockSpec(memory_space=pltpu.VMEM)
    smem = pl.BlockSpec(memory_space=pltpu.SMEM)
    return pl.pallas_call(
        kernel,
        out_shape=[jax.ShapeDtypeStruct(s, t) for s, t in out_shapes],
        in_specs=[
            smem
            if x.shape == (1, 1)
            else pl.BlockSpec(memory_space=pltpu.HBM)
            if i in in_place
            else vmem
            for i, x in enumerate(inputs)
        ],
        out_specs=[pl.BlockSpec(memory_space=out_space) for _ in out_shapes],
        scratch_shapes=[pltpu.VMEM(s, t) for s, t in scratch]
        + ([pltpu.SemaphoreType.DMA((copies,))] if copies else []),
        compiler_params=pltpu.CompilerParams(vmem_limit_bytes=VMEM_BYTES),
        cost_estimate=pl.CostEstimate(flops=flops, bytes_accessed=2**21, transcendentals=0),
    )(*inputs)


def shifted(block, axis, steps):
    count = lax.axis_size(axis)
    return lax.ppermute(block, axis, [(i, (i + steps) % count) for i in range(count)])


def exchanged(block, axis):
    return lax.ppermute(block, axis, [(0, 1), (1, 0)])


def local(left_bounds, right_bounds, site_tensors, configuration, top_env, bottom_env, sketch):
    chi = left_bounds.shape[2]
    bond = left_bounds.shape[3]
    rows = chi * bond
    size = bond * bond
    tall = (rows, chi)
    flat = (chi, rows)
    kron = (size * PART, size * PART)
    stack = (size * PART, chi // PART * chi)
    square = (rows, rows)
    sites = site_tensors.reshape(site_tensors.shape[2:])
    western = shifted(left_bounds.reshape(tall), "col", 1)
    eastern = shifted(right_bounds.reshape(tall), "col", -1)
    basis, basis_lanes, edge, first, sketch_t, site, kron_first, *own = call(
        edges_kernel,
        [
            (tall, BF16),
            (flat, BF16),
            (tall, BF16),
            (tall, BF16),
            (tall, BF16),
            ((1, size * size), BF16),
            (kron, BF16),
        ]
        + [((size * PART, size), BF16)] * 3,
        [(tall, BF16)] * 3
        + [(sites.shape, BF16), (tall, F32), (tall, F32), (flat, BF16), (flat, BF16)],
        [top_env.reshape(tall), bottom_env.reshape(tall), sketch, sites, configuration],
        2**24,
        in_place=(0, 1, 2, 3),
        copies=4,
    )
    site_other = exchanged(site, "row")
    (joined,) = call(join_kernel, [(stack, BF16)], [], [basis_lanes, sketch_t], 2**24)
    site_other, joined = lax.optimization_barrier((site_other, joined))
    kron_0, kron_1, sketched = call(
        prepare_kernel,
        [(kron, BF16), (kron, BF16), (square, BF16)],
        [(kron, BF16)],
        [joined, site_other, *own],
        2**24,
    )
    sketched, western, eastern = lax.optimization_barrier((sketched, western, eastern))
    western_other = exchanged(western, "row")
    eastern_other = exchanged(eastern, "row")
    x_first, back, carried = call(
        begin_kernel,
        [(stack, BF16), (tall, BF16), (tall, BF16)],
        [(tall, F32), (tall, F32), (flat, BF16), (flat, BF16), (square, BF16)],
        [first, western, eastern, kron_first],
        2**32,
    )
    sketched, carried, western_other, eastern_other = lax.optimization_barrier(
        (sketched, carried, western_other, eastern_other)
    )
    carried = exchanged(carried, "row")
    keep, send = call(
        rows_kernel,
        [(tall, BF16), (tall, BF16)],
        [
            (square, BF16),
            (square, BF16),
            (tall, F32),
            (tall, F32),
            (tall, BF16),
            (flat, BF16),
            (tall, BF16),
            (stack, BF16),
            (stack, BF16),
        ],
        [
            basis,
            edge,
            sketched,
            western,
            eastern,
            western_other,
            eastern_other,
            kron_0,
            kron_1,
        ],
        2**33,
    )
    received = exchanged(send, "row")
    (product,) = call(
        product_kernel,
        [(kron, F32)],
        [(stack, BF16)],
        [x_first, back, carried],
        2**31,
    )
    received, product = lax.optimization_barrier((received, product))
    gradient, left_new, right_new = call(
        place_kernel,
        [(sites.shape, F32), (tall, BF16), (tall, BF16)],
        [(sites.shape, F32)],
        [product, configuration, keep, received],
        2**30,
        copies=3,
        out_space=pltpu.HBM,
    )
    return (
        gradient.reshape(site_tensors.shape),
        left_new.reshape(left_bounds.shape),
        right_new.reshape(right_bounds.shape),
    )


def solution(mesh):
    return jax.shard_map(
        local,
        mesh=mesh,
        in_specs=(
            P(("grp", "row"), "col", None, None, None),
            P(("grp", "row"), "col", None, None, None),
            P(("grp", "row"), "col", None, None),
            P(("grp", "row"), "col"),
            P(("grp", "col"), None, None, None),
            P(("grp", "col"), None, None, None),
            P(),
        ),
        out_specs=(
            P(("grp", "row"), "col", None, None),
            P(("grp", "row"), "col", None, None, None),
            P(("grp", "row"), "col", None, None, None),
        ),
        check_vma=False,
    )
```

```python
import functools

import jax
import jax.numpy as jnp
from jax import lax
from jax.experimental import pallas as pl
from jax.experimental.pallas import tpu as pltpu
from jax.sharding import PartitionSpec as P

F32 = jnp.float32
BF16 = jnp.bfloat16
VMEM_BYTES = 24 * 1024 * 1024
PART = 4


def nn(a, b):
    return jnp.dot(a, b, preferred_element_type=F32)


def nt(a, b):
    return lax.dot_general(a, b, (((1,), (1,)), ((), ())), preferred_element_type=F32)


def split(x):
    high = x.astype(BF16)
    return high, (x - high.astype(F32)).astype(BF16)


def iota(shape, axis):
    return lax.broadcasted_iota(jnp.int32, shape, axis)


def chol_inverse(grams, near, beside=()):
    beside = list(beside)
    n = grams[0].shape[0]
    blocks = n // 8
    count = len(grams)
    lane = iota((8, n), 1)
    sub = iota((8, n), 0)
    at = [sub == j for j in range(8)]
    after = [sub > j for j in range(8)]
    tiles = [[g[8 * i : 8 * i + 8, :] for i in range(blocks)] for g in grams]

    def over_lanes(x, j):
        return jnp.broadcast_to(x[:, j : j + 1], (8, n))

    def over_rows(x, j):
        return jnp.broadcast_to(x[j : j + 1, :], (8, n))

    for b in range(blocks):
        own = (lane >= 8 * b) & (lane < 8 * b + 8)
        eye = jnp.where(lane - 8 * b == sub, 1.0, 0.0)
        by_element = range(b + 1, min(blocks, b + 1 + near))
        by_matmul = range(by_element.stop, blocks)
        diag = [[over_lanes(tiles[q][b], 8 * b + j) for j in range(8)] for q in range(count)]
        below = [
            [[over_lanes(tiles[q][i], 8 * b + j) for j in range(8)] for i in by_element]
            for q in range(count)
        ]
        forward = [jnp.where(own, eye, tiles[q][b]) for q in range(count)]
        full = list(forward)
        pivots = [jnp.ones((8, n), F32) for _ in range(count)]
        for step in beside[b * len(beside) // blocks : (b + 1) * len(beside) // blocks]:
            step()
        for j in range(8):
            for q in range(count):
                c = diag[q]
                pivot = over_rows(c[j], j)
                inverse = 1.0 / pivot
                pivots[q] = jnp.where(at[j], pivot, pivots[q])
                for k in range(j + 1, 8):
                    m = over_rows(c[k], j) * inverse
                    c[k] = jnp.where(at[j], m, c[k] - c[j] * m)
                row = over_rows(forward[q], j) * inverse
                forward[q] = jnp.where(after[j], forward[q] - c[j] * row, forward[q])
                full[q] = jnp.where(at[j], row, full[q] - c[j] * row)
        for q in range(count):
            rows = [over_rows(full[q], j) for j in range(8)]
            for i in by_element:
                terms = [below[q][i - b - 1][j] * rows[j] for j in range(8)]
                while len(terms) > 1:
                    terms = [x + y for x, y in zip(terms[::2], terms[1::2])]
                tiles[q][i] = jnp.where(own, 0.0, tiles[q][i]) - terms[0]
            if by_matmul:
                rest = jnp.concatenate([tiles[q][i] for i in by_matmul], axis=0)
                padded = [full[q], jnp.zeros((n - 8 * b - 8, n), F32)]
                if b:
                    padded = [jnp.zeros((8 * b, n), F32)] + padded
                update = jnp.dot(
                    rest,
                    jnp.concatenate(padded, axis=0),
                    precision=lax.Precision.HIGHEST,
                    preferred_element_type=F32,
                )
                for x, i in enumerate(by_matmul):
                    tiles[q][i] = jnp.where(own, 0.0, tiles[q][i]) - update[8 * x : 8 * x + 8]
            tiles[q][b] = jnp.where(lane <= sub + 8 * b, forward[q] * lax.rsqrt(pivots[q]), 0.0)
    return [jnp.concatenate(t, axis=0) for t in tiles]


def leg(scratch, j):
    chi = scratch.shape[1]
    return scratch[pl.ds(j, chi, stride=scratch.shape[0] // chi), :]


def weave(one, two, target, at):
    chi = one.shape[0]
    for g in range(0, chi, 2 * PART):
        rows = [block[k : k + PART, :] for k in (g, g + PART) for block in (one, two)]
        target[at + 2 * g : at + 2 * g + 4 * PART, :] = jnp.concatenate(rows, axis=0).astype(BF16)


def kron_step(lhs, rhs, x_ref, t, pair, transposed):
    chi = lhs.shape[1]
    bond = lhs.shape[0] // chi
    some = lhs[pair * 2 * chi : (pair + 1) * 2 * chi, :]
    if transposed:
        product = nt(some, rhs[t * chi : (t + 2) * chi, :])
    else:
        product = nn(some, rhs[:, t * chi : (t + 2) * chi])
    at = (pair * bond + t) * 2 * PART
    for g in range(chi // PART):
        rows = product[g * 2 * PART : (g + 1) * 2 * PART, :]
        x_ref[at : at + 4 * PART, g * chi : (g + 1) * chi] = jnp.concatenate(
            [rows[:, :chi], rows[:, chi:]], axis=0
        ).astype(BF16)


def absorb_step(kron, x_ref, m_ref, chi, g, first, count):
    bond = m_ref.shape[0] // chi
    step = bond * PART
    out = nn(kron[first * step : (first + count) * step, :], x_ref[:, g * chi : (g + 4) * chi])
    for o in range(count):
        for d in range(0, bond, 2):
            rows = out[(o * bond + d) * PART : (o * bond + d + 2) * PART, :]
            parts = [rows[:, k * chi : (k + 1) * chi] for k in range(4)]
            at = (first + o) * chi + g * PART
            for k in range(2):
                m_ref[at : at + 4 * PART, (d + k) * chi : (d + k + 1) * chi] = jnp.concatenate(
                    [part[k * PART : (k + 1) * PART, :] for part in parts], axis=0
                ).astype(BF16)


def kron_steps(lhs, rhs, x_ref, transposed=False):
    bond = lhs.shape[0] // lhs.shape[1]
    return [
        functools.partial(kron_step, lhs, rhs, x_ref, t, pair, transposed)
        for t in range(0, bond, 2)
        for pair in range(bond // 2)
    ]


def absorb_steps(kron, x_ref, m_ref, chi, count=4):
    bond = m_ref.shape[0] // chi
    return [
        functools.partial(absorb_step, kron, x_ref, m_ref, chi, g, first, count)
        for g in range(0, chi // PART, 4)
        for first in range(0, bond, count)
    ]


def square_core(row):
    row = row[...].astype(F32)
    size = round(row.shape[1] ** 0.5)
    flat = [row[:, i : i + 2 * size] for i in range(0, size * size, 2 * size)]
    flat = jnp.concatenate(flat, axis=0).astype(BF16)
    i = iota((size, size // 2), 0)
    j = iota((size, size // 2), 1)
    even = jnp.where(i == 2 * j, 1.0, 0.0).astype(BF16)
    odd = jnp.where(i == 2 * j + 1, 1.0, 0.0).astype(BF16)
    return (nn(even, flat[:, :size]) + nn(odd, flat[:, size:])).astype(BF16)


def swap_order(size, bond):
    i = iota((size, size), 0)
    j = iota((size, size), 1)
    hit = (i // bond == j % bond) & (i % bond == j // bond)
    return jnp.where(hit, 1.0, 0.0).astype(BF16)


def spread(size):
    i = iota((size * PART, size), 0)
    j = iota((size * PART, size), 1)
    return jnp.where(i // PART == j, 1.0, 0.0).astype(BF16)


def woven_pair(i, bond):
    i = i // PART
    s = (i // (2 * bond)) * 2 + i % 2
    t = (i // 4) % (bond // 2) * 2 + (i // 2) % 2
    return s, t


def kron_of(spread_rows, size):
    bond = round(size**0.5)
    s, t = woven_pair(iota((size * PART, size), 0), bond)
    spread_columns = jnp.where(s * bond + t == iota((size * PART, size), 1), 1.0, 0.0).astype(BF16)
    wide = nt(spread_rows.astype(BF16), spread_columns)
    i = iota(wide.shape, 0)
    j = iota(wide.shape, 1)
    return jnp.where(i % PART == j % PART, wide, 0.0).astype(BF16)


def spread_ahead(core, bond):
    size = core.shape[0]
    return nt(spread(size), nn(swap_order(size, bond), core).astype(BF16))


def spread_turned(core, bond):
    size = core.shape[0]
    return nn(spread(size), nt(swap_order(size, bond), core).astype(BF16))


def spread_back(core, bond):
    size = core.shape[0]
    return nn(spread(size), nn(core, swap_order(size, bond)).astype(BF16))


def mirrored(core, bond):
    size = core.shape[0]
    i = iota((size, size), 0)
    j = iota((size, size), 1)
    total = jnp.zeros((size, size), F32)
    for u in range(bond):
        pick = jnp.where(j == (i // bond) * bond + u, 1.0, 0.0).astype(BF16)
        picked = jnp.where(i % bond == j % bond, nn(pick, core), 0.0).astype(BF16)
        place = jnp.where(j == u * bond + i // bond, 1.0, 0.0).astype(BF16)
        total = total + nn(picked, place)
    return total.astype(BF16)


def edges_kernel(
    top_hbm,
    bottom_hbm,
    sketch_hbm,
    sites_hbm,
    choice,
    basis,
    basis_lanes,
    edge,
    first,
    sketch_t,
    site,
    kron_first,
    own_upper,
    own_lower,
    own_sketch,
    top,
    bottom,
    sketch,
    sites,
    wide,
    wide_sketch,
    legs_top,
    legs_bottom,
    sems,
):
    side = lax.axis_index("row")
    chi = top.shape[1]
    bond = top.shape[0] // chi
    copies = [
        pltpu.make_async_copy(source, target, sems.at[i])
        for i, (source, target) in enumerate(
            ((top_hbm, top), (bottom_hbm, bottom), (sketch_hbm, sketch), (sites_hbm, sites))
        )
    ]
    for copy in copies:
        copy.start()
    for env, legs, mine in ((top, legs_top, 0), (bottom, legs_bottom, 1)):
        copies[mine].wait()
        wide[...] = env[...].astype(F32)

        @pl.when(side == 0)
        def _():
            for u in range(0, bond, 2):
                pair = [leg(wide, u).T, leg(wide, u + 1).T]
                for k in range(2):
                    legs[:, (u + k) * chi : (u + k + 1) * chi] = pair[k].astype(BF16)
                if mine == 0:
                    weave(*pair, first, u * chi)

        @pl.when(side == 1)
        def _():
            for u in range(0, bond, 2):
                pair = [leg(wide, u), leg(wide, u + 1)]
                for k in range(2):
                    legs[:, (u + k) * chi : (u + k + 1) * chi] = pair[k].astype(BF16)
                if mine == 1:
                    weave(*pair, first, u * chi)

    copies[2].wait()
    wide_sketch[...] = sketch[...].astype(F32)

    def turn_sketch(o):
        weave(leg(wide_sketch, o).T, leg(wide_sketch, o + 1).T, sketch_t, o * chi)

    copies[3].wait()
    row = jnp.zeros((1, sites.shape[1]), F32)
    for p in range(sites.shape[0]):
        row = row + jnp.where(choice[0, 0] == p, sites[p : p + 1, :].astype(F32), 0.0)
    site[...] = row.astype(BF16)

    def build_kron():
        size = bond * bond
        core = square_core(site)
        swap = swap_order(size, bond)
        wide = spread(size)
        ahead = spread_ahead(core, bond)
        own_upper[...] = ahead.astype(BF16)
        own_lower[...] = nn(wide, nn(swap, core).astype(BF16)).astype(BF16)
        turned = nn(nn(swap, mirrored(core, bond)).astype(BF16), swap).astype(BF16)
        own_sketch[...] = nn(wide, turned).astype(BF16)
        kron_first[...] = kron_of(jnp.where(side == 0, ahead, spread_back(core, bond)), size)

    inverse_top, inverse_bottom = chol_inverse(
        [nt(legs_top[...], legs_top[...]), nt(legs_bottom[...], legs_bottom[...])],
        1,
        [functools.partial(turn_sketch, o) for o in range(0, bond, 2)] + [build_kron],
    )
    high, low = split(inverse_top)
    ortho = nn(high, legs_top[...]) + nn(low, legs_top[...])
    basis_lanes[...] = ortho.astype(BF16)
    blocks = [ortho[:, u * chi : (u + 1) * chi] for u in range(bond)]
    for u in range(0, bond, 2):
        weave(blocks[u], blocks[u + 1], basis, u * chi)
    high, low = split(inverse_bottom)
    ortho = (nn(high, legs_bottom[...]) + nn(low, legs_bottom[...])).astype(BF16)
    for d in range(bond):
        edge[d * chi : (d + 1) * chi, :] = ortho[:, d * chi : (d + 1) * chi]


def scaled(blocks, wide):
    chi = blocks[0].shape[0]
    bond = len(blocks)
    squares = jnp.zeros((1, chi), F32)
    for o, block in enumerate(blocks):
        wide[pl.ds(o, chi, stride=bond), :] = block
        squares = squares + jnp.sum(block * block, axis=0, keepdims=True)
    mean = jnp.sum(squares, axis=1, keepdims=True) * (1.0 / (chi * bond * chi))
    return (wide[...] * lax.rsqrt(mean + 1e-06)).astype(BF16)


def join_kernel(basis_lanes, sketch_t, x):
    for step in kron_steps(sketch_t, basis_lanes, x):
        step()


def prepare_kernel(
    x, site_other, own_upper, own_lower, own_sketch, kron_0, kron_1, sketched, kron_sketch
):
    is_left = lax.axis_index("row") == 0
    size = x.shape[0] // PART
    bond = round(size**0.5)
    chi = sketched.shape[0] // bond
    wide = spread(size)
    other = square_core(site_other)
    turned = spread_turned(other, bond)
    kron_sketch[...] = kron_of(jnp.where(is_left, own_sketch[...], turned.astype(BF16)), size)
    steps = absorb_steps(kron_sketch, x, sketched, chi)
    for step in steps[:6]:
        step()
    across = mirrored(other, bond)
    for step in steps[6:11]:
        step()
    upper = nn(wide, across).astype(BF16)
    kron_0[...] = kron_of(jnp.where(is_left, own_upper[...], upper), size)
    for step in steps[11:]:
        step()
    lower = nt(wide, across).astype(BF16)
    kron_1[...] = kron_of(jnp.where(is_left, lower, own_lower[...]), size)


def begin_kernel(
    first, western, eastern, kron, x_first, back, carried, wide_w, wide_e, ahead, behind, middle
):
    side = lax.axis_index("row")
    chi = first.shape[1]
    bond = first.shape[0] // chi
    wide_w[...] = western[...].astype(F32)
    wide_e[...] = eastern[...].astype(F32)

    def ready(ahead_of, behind_of, back_of):
        for j in range(0, bond, 2):
            for k in range(2):
                at = slice((j + k) * chi, (j + k + 1) * chi)
                ahead[:, at] = ahead_of(j + k).astype(BF16)
                behind[:, at] = behind_of(j + k).astype(BF16)
            weave(back_of(j), back_of(j + 1), back, j * chi)

    west = functools.partial(leg, wide_w)
    east = functools.partial(leg, wide_e)

    @pl.when(side == 0)
    def _():
        ready(west, lambda j: east(j).T, east)

    @pl.when(side == 1)
    def _():
        ready(lambda j: east(j).T, west, lambda j: west(j).T)

    for step in kron_steps(first, ahead, x_first) + absorb_steps(kron, x_first, middle, chi):
        step()
    state = nn(behind[...], middle[...]).astype(BF16)
    for s in range(bond):
        carried[s * chi : (s + 1) * chi, :] = state[:, s * chi : (s + 1) * chi]


def rows_kernel(
    basis,
    edge,
    sketched,
    western,
    eastern,
    western_other,
    eastern_other,
    kron_0,
    kron_1,
    keep,
    send,
    absorbed,
    closed,
    wide_0,
    wide_1,
    rows_0,
    lanes_0,
    woven_1,
    x,
    x_next,
):
    is_left = lax.axis_index("row") == 0
    chi = basis.shape[1]
    bond = basis.shape[0] // chi
    blocks = [slice(j * chi, (j + 1) * chi) for j in range(bond)]

    @pl.when(is_left)
    def _():
        wide_0[...] = western[...].astype(F32)

    @pl.when(jnp.logical_not(is_left))
    def _():
        wide_0[...] = eastern_other[...].astype(F32)

    for j in range(bond):
        rows_0[blocks[j], :] = leg(wide_0, j).astype(BF16)
    stacked = nn(sketched[...], rows_0[...])
    range_t = jnp.concatenate([stacked[blocks[d], :] for d in range(bond)], axis=1)
    high, low = split(range_t)

    def ready_lanes():
        for j in range(bond):
            lanes_0[:, blocks[j]] = rows_0[blocks[j], :]

    def ready_other(part):
        step = wide_1.shape[0] // 4
        at = slice(part * step, (part + 1) * step)
        wide_1[at, :] = jnp.where(is_left, western_other[at, :], eastern[at, :]).astype(F32)

    def ready_woven(j):
        weave(leg(wide_1, j), leg(wide_1, j + 1), woven_1, j * chi)

    beside = (
        [ready_lanes]
        + kron_steps(basis, lanes_0, x)
        + [functools.partial(ready_other, part) for part in range(4)]
        + absorb_steps(kron_0, x, absorbed, chi)
        + [functools.partial(ready_woven, j) for j in range(0, bond, 2)]
        + kron_steps(woven_1, edge, x_next, True)
        + absorb_steps(kron_1, x_next, closed, chi)
    )
    for step in beside[:3]:
        step()
    gram = nt(high, high) + (nt(high, low) + nt(low, high))
    for step in beside[3:6]:
        step()
    (inverse,) = chol_inverse([gram], 2, beside[6:])
    inverse_high, inverse_low = split(inverse)
    ortho = nn(inverse_high, high) + (nn(inverse_high, low) + nn(inverse_low, high))
    closing = ortho.astype(BF16)
    upper = nt(absorbed[...], closing)
    lower = nn(closing, closed[...])
    new_0 = scaled([upper[at, :] for at in blocks], wide_0)
    new_1 = scaled([lower[:, at] for at in blocks], wide_1)

    @pl.when(is_left)
    def _():
        keep[...] = new_0
        send[...] = new_1

    @pl.when(jnp.logical_not(is_left))
    def _():
        keep[...] = new_1
        send[...] = new_0


def product_kernel(x_first, back, carried, product, x_second):
    side = lax.axis_index("row")
    for step in kron_steps(back, carried, x_second, True):
        step()

    @pl.when(side == 0)
    def _():
        product[...] = nt(x_first[...], x_second[...])

    @pl.when(side == 1)
    def _():
        product[...] = nt(x_second[...], x_first[...])


def place_kernel(product, choice, keep, received, gradient, left, right, entries, sems):
    side = lax.axis_index("row")
    is_left = side == 0
    phys_count = gradient.shape[0]
    size = product.shape[0] // PART
    bond = round(size**0.5)
    chi = keep.shape[1]

    def start(one, other):
        pltpu.make_async_copy(one, left, sems.at[0]).start()
        pltpu.make_async_copy(other, right, sems.at[1]).start()

    pl.when(side == 0)(functools.partial(start, keep, received))
    pl.when(side == 1)(functools.partial(start, received, keep))

    def one_hot(i, j, swapped):
        s, t = woven_pair(i, bond)
        at = jnp.where(swapped, t * bond + s, s * bond + t)
        return jnp.where(j == at, 1.0, 0.0).astype(BF16)

    i = iota(product.shape, 0)
    j = iota(product.shape, 1)
    diagonal = jnp.where(i % PART == j % PART, product[...], 0.0).astype(BF16)
    wide = (size * PART, size * 2)
    half = jnp.zeros((size // 2, size * 2), F32)
    for odd in range(2):
        columns = one_hot(iota(wide, 0), iota(wide, 1) - odd * size, side == 1)
        rows = one_hot(iota(wide[::-1], 1), iota(wide[::-1], 0) * 2 + odd, is_left)[: size // 2]
        high, low = split(nn(diagonal, columns))
        half = half + (nn(rows, high) + nn(rows, low))
    half = half * (bond / chi)
    phys = iota((phys_count, size * 2), 0)
    for r in range(size // 2):
        row = jnp.broadcast_to(half[r : r + 1, :], phys.shape)
        entries[:, r * size * 2 : (r + 1) * size * 2] = jnp.where(phys == choice[0, 0], row, 0.0)
    copy = pltpu.make_async_copy(entries, gradient, sems.at[2])
    copy.start()
    pltpu.make_async_copy(keep, left, sems.at[0]).wait()
    pltpu.make_async_copy(keep, right, sems.at[1]).wait()
    copy.wait()


def call(kernel, out_shapes, scratch, inputs, flops, in_place=(), copies=0, out_space=pltpu.VMEM):
    inputs = [
        pltpu.with_memory_space_constraint(x, pltpu.HBM) if i in in_place else x
        for i, x in enumerate(inputs)
    ]
    vmem = pl.BlockSpec(memory_space=pltpu.VMEM)
    smem = pl.BlockSpec(memory_space=pltpu.SMEM)
    return pl.pallas_call(
        kernel,
        out_shape=[jax.ShapeDtypeStruct(s, t) for s, t in out_shapes],
        in_specs=[
            smem
            if x.shape == (1, 1)
            else pl.BlockSpec(memory_space=pltpu.HBM)
            if i in in_place
            else vmem
            for i, x in enumerate(inputs)
        ],
        out_specs=[pl.BlockSpec(memory_space=out_space) for _ in out_shapes],
        scratch_shapes=[pltpu.VMEM(s, t) for s, t in scratch]
        + ([pltpu.SemaphoreType.DMA((copies,))] if copies else []),
        compiler_params=pltpu.CompilerParams(vmem_limit_bytes=VMEM_BYTES),
        cost_estimate=pl.CostEstimate(flops=flops, bytes_accessed=2**21, transcendentals=0),
    )(*inputs)


def shifted(block, axis, steps):
    count = lax.axis_size(axis)
    return lax.ppermute(block, axis, [(i, (i + steps) % count) for i in range(count)])


def exchanged(block, axis):
    return lax.ppermute(block, axis, [(0, 1), (1, 0)])


def local(left_bounds, right_bounds, site_tensors, configuration, top_env, bottom_env, sketch):
    chi = left_bounds.shape[2]
    bond = left_bounds.shape[3]
    rows = chi * bond
    size = bond * bond
    tall = (rows, chi)
    flat = (chi, rows)
    kron = (size * PART, size * PART)
    stack = (size * PART, chi // PART * chi)
    square = (rows, rows)
    sites = site_tensors.reshape(site_tensors.shape[2:])
    western = shifted(left_bounds.reshape(tall), "col", 1)
    eastern = shifted(right_bounds.reshape(tall), "col", -1)
    basis, basis_lanes, edge, first, sketch_t, site, kron_first, *own = call(
        edges_kernel,
        [
            (tall, BF16),
            (flat, BF16),
            (tall, BF16),
            (tall, BF16),
            (tall, BF16),
            ((1, size * size), BF16),
            (kron, BF16),
        ]
        + [((size * PART, size), BF16)] * 3,
        [(tall, BF16)] * 3
        + [(sites.shape, BF16), (tall, F32), (tall, F32), (flat, BF16), (flat, BF16)],
        [top_env.reshape(tall), bottom_env.reshape(tall), sketch, sites, configuration],
        2**24,
        in_place=(0, 1, 2, 3),
        copies=4,
    )
    site_other = exchanged(site, "row")
    (joined,) = call(join_kernel, [(stack, BF16)], [], [basis_lanes, sketch_t], 2**24)
    site_other, joined = lax.optimization_barrier((site_other, joined))
    kron_0, kron_1, sketched = call(
        prepare_kernel,
        [(kron, BF16), (kron, BF16), (square, BF16)],
        [(kron, BF16)],
        [joined, site_other, *own],
        2**24,
    )
    sketched, western, eastern = lax.optimization_barrier((sketched, western, eastern))
    western_other = exchanged(western, "row")
    eastern_other = exchanged(eastern, "row")
    x_first, back, carried = call(
        begin_kernel,
        [(stack, BF16), (tall, BF16), (tall, BF16)],
        [(tall, F32), (tall, F32), (flat, BF16), (flat, BF16), (square, BF16)],
        [first, western, eastern, kron_first],
        2**32,
    )
    sketched, carried, western_other, eastern_other = lax.optimization_barrier(
        (sketched, carried, western_other, eastern_other)
    )
    carried = exchanged(carried, "row")
    keep, send = call(
        rows_kernel,
        [(tall, BF16), (tall, BF16)],
        [
            (square, BF16),
            (square, BF16),
            (tall, F32),
            (tall, F32),
            (tall, BF16),
            (flat, BF16),
            (tall, BF16),
            (stack, BF16),
            (stack, BF16),
        ],
        [
            basis,
            edge,
            sketched,
            western,
            eastern,
            western_other,
            eastern_other,
            kron_0,
            kron_1,
        ],
        2**33,
    )
    received = exchanged(send, "row")
    (product,) = call(
        product_kernel,
        [(kron, F32)],
        [(stack, BF16)],
        [x_first, back, carried],
        2**31,
    )
    received, product = lax.optimization_barrier((received, product))
    gradient, left_new, right_new = call(
        place_kernel,
        [(sites.shape, F32), (tall, BF16), (tall, BF16)],
        [(sites.shape, F32)],
        [product, configuration, keep, received],
        2**30,
        copies=3,
        out_space=pltpu.HBM,
    )
    return (
        gradient.reshape(site_tensors.shape),
        left_new.reshape(left_bounds.shape),
        right_new.reshape(right_bounds.shape),
    )


def solution(mesh):
    return jax.shard_map(
        local,
        mesh=mesh,
        in_specs=(
            P(("grp", "row"), "col", None, None, None),
            P(("grp", "row"), "col", None, None, None),
            P(("grp", "row"), "col", None, None),
            P(("grp", "row"), "col"),
            P(("grp", "col"), None, None, None),
            P(("grp", "col"), None, None, None),
            P(),
        ),
        out_specs=(
            P(("grp", "row"), "col", None, None),
            P(("grp", "row"), "col", None, None, None),
            P(("grp", "row"), "col", None, None, None),
        ),
        check_vma=False,
    )
```
